32 devices in a mesh: dp: 8 (over z, x), tensor: 4 (over y, core).
Axes of the slice: x: 2, y: 2, z: 4, core: 2. Of those that a mesh axis runs over, the one named last changes fastest.
Arguments:
- tokens: bfloat16 [8, 1024, 768], P('dp', 'tensor'), may hold values from -6 to 6
- row_lengths: int32 [8], P('dp'), may hold values from 769 to 1024, as said below
- instruction_mask: int32 [8, 1024], P('dp', 'tensor'), may hold values from 0 to 1, as said below
- task_groups: int32 [8], replicated, may hold values from 0 to 3
- rel_buckets: int32 [2047], replicated, may hold values from 0 to 31
- gain_attn: float32 [768], replicated, may hold values from 0.5 to 1.5
- w_query: bfloat16 [768, 768], P(None, 'tensor'), may hold values from -0.109375 to 0.109375
- w_key: bfloat16 [768, 768], P(None, 'tensor'), may hold values from -0.109375 to 0.109375
- w_value: bfloat16 [768, 768], P(None, 'tensor'), may hold values from -0.21875 to 0.21875
- rel_table: float32 [32, 12], P(None, 'tensor'), may hold values from -4 to 4
- w_out: bfloat16 [768, 768], P('tensor'), may hold values from -0.875 to 0.875
- gain_ffn: float32 [768], replicated, may hold values from 0.5 to 1.5
- w_in: bfloat16 [768, 3072], P(None, 'tensor'), may hold values from -0.21875 to 0.21875
- w_back: bfloat16 [3072, 768], P('tensor'), may hold values from -0.15625 to 0.15625
- out_grad: bfloat16 [8, 1024, 768], P('dp', 'tensor'), may hold values from -6 to 6
Outputs:
- mixed: bfloat16 [8, 1024, 768], P('dp', 'tensor')
- grad_tokens: float32 [8, 1024, 768], P('dp', 'tensor')
- grad_gain_attn: float32 [768], replicated
- grad_query: float32 [768, 768], P(None, 'tensor')
- grad_key: float32 [768, 768], P(None, 'tensor')
- grad_value: float32 [768, 768], P(None, 'tensor')
- grad_table: float32 [32, 12], P(None, 'tensor')
- grad_out: float32 [768, 768], P('tensor')
- grad_gain_ffn: float32 [768], replicated
- grad_in: float32 [768, 3072], P(None, 'tensor')
- grad_back: float32 [3072, 768], P('tensor')
The draws below stay inside these ranges and needn't reach their ends.
Inputs may be any that keep to these rules, and one draw needn't show every extreme that they name: `row_lengths`: in each aligned block of 1 row one row is longer than 768; some row has length 1024. `instruction_mask`: the ones of each row form a prefix of 1 to 128 positions.
All inputs are finite; a program needn't handle non-finite values.
Results may differ from the reference program's by a relative error of at most 0.017.
Values may be sent and summed in bfloat16 or wider, within the bound.
No kernel may reach another device: no remote copies, remote signals or barrier semaphores. Data moves between devices by JAX's collectives and lax.ppermute only.
A program may use at most 192 MiB of HBM per device.

```python
import jax
import jax.numpy as jnp
from jax import lax

D = 768
HEADS = 12
HEAD_DIM = 64
FF = 3072
BUCKETS = 32
SEQ = 1024
ROWS_DEV = 1
ROWS = 8
GROUPS = 4


def draw_row_lengths(key, part):
    key = jax.random.fold_in(key, 11)
    first_key, second_key, third_key, fourth_key = jax.random.split(key, 4)
    lengths = jax.random.randint(first_key, (ROWS,), SEQ // 4, SEQ + 1, dtype=jnp.int32)
    chosen = jax.random.randint(second_key, (ROWS // ROWS_DEV,), 0, ROWS_DEV, dtype=jnp.int32)
    long_rows = jnp.arange(ROWS // ROWS_DEV, dtype=jnp.int32) * ROWS_DEV + chosen
    long_lengths = jax.random.randint(third_key, (ROWS // ROWS_DEV,), 3 * SEQ // 4 + 1, SEQ + 1, dtype=jnp.int32)
    lengths = lengths.at[long_rows].set(long_lengths)
    full_block = jax.random.randint(fourth_key, (), 0, ROWS // ROWS_DEV, dtype=jnp.int32)
    return lengths.at[long_rows[full_block]].set(SEQ)


def draw_instruction_mask(key, part):
    key = jax.random.fold_in(key, 23)
    prefix = jax.random.randint(key, (ROWS, 1), 1, SEQ // 8 + 1, dtype=jnp.int32)
    return (jnp.arange(SEQ, dtype=jnp.int32)[None, :] < prefix).astype(jnp.int32)


def set_ends(result, stream_key, low, largest):
    place = [jax.random.randint(jax.random.fold_in(stream_key, axis), (), 0, length) for axis, length in enumerate(result.shape)]
    longest = result.shape.index(max(result.shape))
    next_to = place[:longest] + [(place[longest] + 1) % result.shape[longest]] + place[longest + 1:]
    return result.at[tuple(place)].set(low).at[tuple(next_to)].set(largest)


def shard_levels(own_key, shape, cuts, least, largest):
    factor_of = 1.0
    for dim, blocks in cuts:
        draws = jax.random.uniform(jax.random.fold_in(jax.random.fold_in(own_key, 6), dim), (blocks,), jnp.float32, least / len(cuts), largest / len(cuts))
        factor_of = factor_of * jnp.repeat(jnp.exp(draws), shape[dim] // blocks).reshape((-1,) + (1,) * (len(shape) - 1 - dim))
    return factor_of


def centred(own_key, extent, width, limit, cuts=(), kind=jnp.bfloat16):
    factor_of = shard_levels(own_key, extent, cuts, -0.22, 0.18) if cuts else 1.0
    result = jax.random.normal(own_key, extent, jnp.float32) * width * factor_of
    return jnp.minimum(jnp.maximum(result, -limit), limit).astype(kind)


def setup_inputs(seed: int = 0) -> dict:
    arg_keys = jax.random.split(jax.random.key(seed), 16)
    return {
        "tokens": centred(arg_keys[0], (ROWS, SEQ, D), 1.0, 6.0, ((0, 8), (1, 4))),
        "row_lengths": draw_row_lengths(jax.random.fold_in(arg_keys[15], 71), 0),
        "instruction_mask": draw_instruction_mask(jax.random.fold_in(arg_keys[15], 71), 0),
        "task_groups": set_ends(jax.random.randint(arg_keys[3], (ROWS,), 0, GROUPS), jax.random.fold_in(arg_keys[3], 1), 0, GROUPS - 1).astype(jnp.int32),
        "rel_buckets": set_ends(jax.random.randint(arg_keys[4], (2 * SEQ - 1,), 0, BUCKETS), jax.random.fold_in(arg_keys[4], 1), 0, BUCKETS - 1).astype(jnp.int32),
        "gain_attn": jnp.clip(1.0 + 0.1 * jax.random.normal(arg_keys[5], (D,), jnp.float32), 0.5, 1.5),
        "w_query": centred(arg_keys[6], (D, D), (4 * D) ** -0.5, 0.109375, ((1, 4),)),
        "w_key": centred(arg_keys[7], (D, D), (4 * D) ** -0.5, 0.109375, ((1, 4),)),
        "w_value": centred(arg_keys[8], (D, D), D ** -0.5, 0.21875, ((1, 4),)),
        "rel_table": centred(arg_keys[9], (BUCKETS, HEADS), 1.0, 4.0, ((1, 4),), jnp.float32),
        "w_out": centred(arg_keys[10], (D, D), (D // 16) ** -0.5, 0.875, ((0, 4),)),
        "gain_ffn": jnp.clip(1.0 + 0.1 * jax.random.normal(arg_keys[11], (D,), jnp.float32), 0.5, 1.5),
        "w_in": centred(arg_keys[12], (D, FF), D ** -0.5, 0.21875, ((1, 4),)),
        "w_back": centred(arg_keys[13], (FF, D), (FF // 2) ** -0.5, 0.15625, ((0, 4),)),
        "out_grad": centred(arg_keys[14], (ROWS, SEQ, D), 1.0, 6.0, ((0, 8), (1, 4))),
    }


NORM_EPS = 1e-06
MASK_FILL = -1000000000.0

@jax.custom_vjp
def low(v):
    return lax.optimization_barrier(v.astype(jnp.bfloat16)).astype(jnp.float32)

@jax.custom_vjp
def low_back(v):
    return v

def low_keep(v):
    return (low(v), None)

def low_pass(kept, grad):
    return (grad,)

def back_keep(v):
    return (v, None)

def back_low(kept, grad):
    return (low(grad),)
low.defvjp(low_keep, low_pass)
low_back.defvjp(back_keep, back_low)

def rms_norm(values, gain_vec):
    return values * lax.rsqrt(lax.optimization_barrier(jnp.mean(values * values, axis=-1, keepdims=True)) + NORM_EPS) * gain_vec

def high_dot(left, right):
    return jnp.dot(left, right, precision=lax.Precision.HIGHEST)

def head_split(values):
    return values.reshape(SEQ, HEADS, HEAD_DIM).transpose(1, 0, 2)

def layer_row(x_row, length, rel_buckets, params):
    gain_attn, w_query, w_key, w_value, rel_table, w_out, gain_ffn, w_in, w_back = params
    normed = low(rms_norm(x_row, gain_attn))
    query = head_split(low(low_back(high_dot(normed, w_query))))
    key_rows = head_split(low(low_back(high_dot(normed, w_key))))
    value_rows = head_split(low(low_back(high_dot(normed, w_value))))
    positions = jnp.arange(SEQ, dtype=jnp.int32)
    offsets = positions[None, :] - positions[:, None] + SEQ - 1
    bias = jnp.transpose(rel_table[rel_buckets[offsets]], (2, 0, 1))
    scores = jnp.einsum('hqd,hkd->hqk', query, key_rows, precision=lax.Precision.HIGHEST) + bias
    scores = low_back(scores)
    scores = jnp.where((positions < length)[None, None, :], scores, MASK_FILL)
    probs = jax.nn.softmax(scores, axis=-1)
    context = jnp.einsum('hqk,hkd->hqd', low(probs), value_rows, precision=lax.Precision.HIGHEST)
    context = low(low_back(context.transpose(1, 0, 2).reshape(SEQ, HEADS * HEAD_DIM)))
    hidden = x_row + low_back(high_dot(context, w_out))
    normed_ffn = low(rms_norm(hidden, gain_ffn))
    upward = low_back(high_dot(normed_ffn, w_in))
    active = low(jax.nn.gelu(upward))
    return hidden + low_back(high_dot(active, w_back))

def reference(tokens, row_lengths, instruction_mask, task_groups, rel_buckets, gain_attn, w_query, w_key, w_value, rel_table, w_out, gain_ffn, w_in, w_back, out_grad):
    params = tuple((param.astype(jnp.float32) for param in (gain_attn, w_query, w_key, w_value, rel_table, w_out, gain_ffn, w_in, w_back)))

    def forward(inputs, weights):

        def one_row(pair):
            return layer_row(pair[0], pair[1], rel_buckets, weights)
        return lax.map(jax.checkpoint(one_row), (inputs, row_lengths))
    mixed, pullback = jax.vjp(forward, tokens.astype(jnp.float32), params)
    same_group = (task_groups[:, None] == task_groups[None, :]).astype(jnp.float32)
    row_scale = lax.rsqrt(lax.optimization_barrier(jnp.sum(same_group, axis=1)))
    positions = jnp.arange(SEQ, dtype=jnp.int32)
    token_keep = ((positions[None, :] < row_lengths[:, None]) & (instruction_mask == 0)).astype(jnp.float32)
    cotangent = out_grad.astype(jnp.float32) * row_scale[:, None, None] * token_keep[:, :, None]
    grad_tokens, grads = pullback(cotangent)
    return (mixed.astype(jnp.bfloat16), grad_tokens, grads[0], grads[1], grads[2], grads[3], grads[4], grads[5], grads[6], grads[7], grads[8])
```

```python
import functools

import jax
import jax.numpy as jnp
from jax import lax
from jax.experimental import pallas as pl
from jax.experimental.pallas import tpu as pltpu
from jax.sharding import PartitionSpec as P

NORM_EPS = 1e-06
MASK_FILL = -1000000000.0
F32 = jnp.float32
BF16 = jnp.bfloat16
LANES = 128
GELU_SCALE = 0.7978845608028654
GELU_CUBE = 0.044715


def dot_nn(left, right):
    return jnp.dot(left, right, preferred_element_type=F32)


def dot_nt(left, right):
    return lax.dot_general(left, right, (((1,), (1,)), ((), ())), preferred_element_type=F32)


def dot_tn(left, right):
    return lax.dot_general(left, right, (((0,), (0,)), ((), ())), preferred_element_type=F32)


def vmem_whole(shape):
    return pl.BlockSpec(shape, lambda i: (0,) * len(shape))


def kernel_params(mib):
    return pltpu.CompilerParams(vmem_limit_bytes=mib << 20)


def block_order(count):
    order = [0]
    bit = count // 2
    while bit:
        order = order + [slot | bit for slot in order]
        bit //= 2
    return order


def tensor_bits(count):
    bits = []
    bit = count // 2
    while bit:
        bits.append(bit)
        bit //= 2
    return bits


def swap_tensor(value, bit):
    size = lax.axis_size("tensor")
    return lax.ppermute(value, "tensor", [(i, i ^ bit) for i in range(size)])


def gather_tensor(value, count):
    slots = [value]
    for bit in tensor_bits(count):
        slots = slots + [swap_tensor(piece, bit) for piece in slots]
    return slots


def scatter_tensor(value, count):
    for bit in reversed(tensor_bits(count)):
        half = value.shape[0] // 2
        came = swap_tensor(value[half:], bit)
        value = (value[:half].astype(F32) + came.astype(F32)).astype(BF16)
    return value


def dp_steps(count):
    bits = []
    bit = 1
    while bit < count:
        bits.append(bit)
        bit *= 2
    return list(zip(bits, bits[1:] + bits[:1], strict=True))


def swap_dp(value, pair):
    rows, cols = lax.axis_size("dp"), lax.axis_size("tensor")
    route = []
    for row in range(rows):
        for col in range(cols):
            route.append((row * cols + col, (row ^ pair[col % 2]) * cols + col))
    return lax.ppermute(value, ("dp", "tensor"), route)


def high_side(pair):
    row, col = lax.axis_index("dp"), lax.axis_index("tensor")
    bit = jnp.where(col % 2 == 1, pair[1], pair[0])
    return (row & bit) != 0


def sum_dp(value):
    steps = dp_steps(lax.axis_size("dp"))
    for pair in steps:
        half = value.shape[0] // 2
        side = high_side(pair).astype(jnp.int32)
        sent = lax.dynamic_slice_in_dim(value, (1 - side) * half, half)
        kept = lax.dynamic_slice_in_dim(value, side * half, half)
        came = swap_dp(sent, pair)
        value = (kept.astype(F32) + came.astype(F32)).astype(BF16)
    for pair in reversed(steps):
        came = swap_dp(value, pair)
        side = high_side(pair)
        value = jnp.concatenate((jnp.where(side, came, value), jnp.where(side, value, came)))
    return value


def sum_small(own_cols, shared, count):
    rows = own_cols.shape[0]
    value = jnp.concatenate((own_cols, shared))
    for pair in dp_steps(lax.axis_size("dp")):
        value = value + swap_dp(value, (pair[0], pair[0]))
    shared = value[rows:]
    for bit in reversed(tensor_bits(count)):
        shared = shared + swap_tensor(shared, bit)
    return value[:rows], shared


def norm_rows(values):
    return lax.rsqrt(jnp.mean(values * values, axis=-1, keepdims=True) + NORM_EPS)


def attend_kernel(
    heads, count, length_ref, starts_ref, table_ref, buckets_ref, gain_ref, wq_ref, wk_ref, wv_ref, *refs
):
    tok_refs = refs[:count]
    ctx_ref, exps_ref, linv_ref, normed_ref, q_ref, k_ref, v_ref, bias_ref, all_normed = refs[count:]
    step = pl.program_id(0)
    blk = ctx_ref.shape[0]
    seq = blk * count
    head_cols = wq_ref.shape[1]
    width = head_cols // heads
    wide = 2 * seq

    @pl.when(step == 0)
    def _():
        which = buckets_ref[...]
        for h in range(heads):
            rel = jnp.zeros((8, wide), F32)
            for b in range(table_ref.shape[0]):
                rel = jnp.where(which == b, table_ref[b, h], rel)
            full = jnp.broadcast_to(rel[0:1], (LANES, wide))
            bias_ref[h] = pltpu.roll(full, wide - (LANES - 1), 1, stride=1, stride_axis=0)
        lane = lax.broadcasted_iota(jnp.int32, (blk, LANES - width), 1)
        row = lax.broadcasted_iota(jnp.int32, (blk, LANES - width), 0)
        first = lane == 0
        ones_q = jnp.where(first, 1.0, 0.0).astype(BF16)
        ones_v = jnp.where(lane < 2, 1.0, 0.0).astype(BF16)
        for b in range(count):
            values = tok_refs[b][...].astype(F32)
            normed = (values * norm_rows(values) * gain_ref[...]).astype(BF16)
            rows = slice(b * blk, (b + 1) * blk)
            all_normed[rows] = normed
            masked = first & (row + starts_ref[b] >= length_ref[0])
            fill = jnp.where(masked, MASK_FILL, 0.0).astype(BF16)
            query = dot_nn(normed, wq_ref[...]).astype(BF16)
            keys = dot_nn(normed, wk_ref[...]).astype(BF16)
            values = dot_nn(normed, wv_ref[...]).astype(BF16)
            for h in range(heads):
                cols = slice(h * width, (h + 1) * width)
                q_ref[h, rows] = jnp.concatenate((query[:, cols], ones_q), axis=1)
                k_ref[h, rows] = jnp.concatenate((keys[:, cols], fill), axis=1)
                v_ref[h, rows] = jnp.concatenate((values[:, cols], ones_v), axis=1)

    row0 = pl.multiple_of(step * blk, blk)
    first_row = starts_ref[step]
    normed_ref[...] = all_normed[pl.ds(row0, blk)]
    outs = []
    linv = jnp.zeros((blk, LANES), F32)
    stat_lane = lax.broadcasted_iota(jnp.int32, (blk, LANES), 1)
    for h in range(heads):
        scores = dot_nt(q_ref[h, pl.ds(row0, blk)], k_ref[h])
        bias = []
        for a in range(blk // LANES):
            line = []
            for b in range(count):
                start = seq - LANES - a * LANES - first_row + starts_ref[b]
                line.append(bias_ref[h, :, pl.ds(pl.multiple_of(start, LANES), blk)])
            bias.append(jnp.concatenate(line, axis=1))
        scores = scores + jnp.concatenate(bias, axis=0)
        top = jnp.max(scores, axis=1, keepdims=True)
        exps = jnp.exp(scores - top).astype(BF16)
        exps_ref[h] = exps
        mixed = dot_nn(exps, v_ref[h])
        inverse = 1.0 / mixed[:, width : width + 1]
        outs.append(mixed[:, :width] * inverse)
        linv = jnp.where(stat_lane == h, inverse, linv)
    ctx_ref[...] = jnp.concatenate(outs, axis=1).astype(BF16)
    linv_ref[...] = linv


def attend(length, starts, table, buckets, gain, w_query, w_key, w_value, tok):
    count = len(tok)
    blk, model = tok[0].shape
    seq = blk * count
    heads = table.shape[1]
    head_cols = w_query.shape[1]
    smem = pl.BlockSpec(memory_space=pltpu.SMEM)
    heads_whole = vmem_whole((heads, seq, LANES))
    flops = 2 * seq * (3 * model * head_cols + 2 * seq * head_cols)
    return pl.pallas_call(
        functools.partial(attend_kernel, heads, count),
        grid=(count,),
        in_specs=[smem, smem, smem, vmem_whole((8, 2 * seq)), vmem_whole((1, model))]
        + [vmem_whole((model, head_cols))] * 3
        + [vmem_whole((blk, model))] * count,
        out_specs=[
            pl.BlockSpec((blk, head_cols), lambda i: (i, 0)),
            pl.BlockSpec((heads, blk, seq), lambda i: (0, i, 0)),
            pl.BlockSpec((blk, LANES), lambda i: (i, 0)),
            pl.BlockSpec((blk, model), lambda i: (i, 0)),
            heads_whole,
            heads_whole,
            heads_whole,
        ],
        out_shape=[
            jax.ShapeDtypeStruct((seq, head_cols), BF16),
            jax.ShapeDtypeStruct((heads, seq, seq), BF16),
            jax.ShapeDtypeStruct((seq, LANES), F32),
            jax.ShapeDtypeStruct((seq, model), BF16),
        ]
        + [jax.ShapeDtypeStruct((heads, seq, LANES), BF16)] * 3,
        scratch_shapes=[
            pltpu.VMEM((heads, LANES, 2 * seq), F32),
            pltpu.VMEM((seq, model), BF16),
        ],
        compiler_params=kernel_params(48),
        cost_estimate=pl.CostEstimate(
            flops=flops * 8, bytes_accessed=12 << 20, transcendentals=heads * seq * seq
        ),
        name="attend",
    )(length, starts, table, buckets, gain, w_query, w_key, w_value, *tok)


def feed_kernel(count, blocks, scale_ref, gain_ref, w_in_ref, w_back_ref, *refs):
    ctx_refs = refs[:count]
    tok_refs = refs[count : count + len(blocks)]
    joined_refs = refs[count + len(blocks) : 2 * count + len(blocks)]
    hidden_ref, normed_ref, active_ref, dup_ref, dnormed_ref, out_ref, cot_ref, tok_now, cot_now = refs[
        2 * count + len(blocks) :
    ]
    step = pl.program_id(0)
    blk = hidden_ref.shape[0]
    for k, b in enumerate(blocks):

        @pl.when(step == k)
        def _():
            tok_now[...] = tok_refs[k][...].astype(F32)
            cot_now[...] = (joined_refs[b][:blk].astype(F32) * scale_ref[0]).astype(BF16)

    hidden = tok_now[...]
    for slot in range(count):
        hidden = hidden + dot_nn(ctx_refs[slot][...], joined_refs[slot][blk:])
    hidden_ref[...] = hidden
    normed = (hidden * norm_rows(hidden) * gain_ref[...]).astype(BF16)
    normed_ref[...] = normed
    cot = cot_now[...]
    cot_ref[...] = cot
    up = dot_nn(normed, w_in_ref[...])
    square = up * up
    bend = jnp.tanh(GELU_SCALE * up * (1.0 + GELU_CUBE * square))
    half = 0.5 * (1.0 + bend)
    active = (up * half).astype(BF16)
    slope = half + 0.5 * up * (1.0 - bend * bend) * GELU_SCALE * (1.0 + 3.0 * GELU_CUBE * square)
    active_ref[...] = active
    dup = (dot_nt(cot, w_back_ref[...]) * slope).astype(BF16)
    dup_ref[...] = dup
    dnormed_ref[...] = dot_nt(dup, w_in_ref[...]).astype(BF16)
    out_ref[...] = dot_nn(active, w_back_ref[...]).astype(BF16)


def feed(blocks, scale, gain, w_in, w_back, ctx, tok, joined):
    count = len(ctx)
    blk, model = tok[0].shape
    units = w_in.shape[1]
    head_cols = ctx[0].shape[1]
    base = blocks[0]
    rows = blk * len(blocks)

    def ctx_spec(slot):
        return pl.BlockSpec((blk, head_cols), lambda i: ((i + base) ^ slot, 0))

    def by_row(width):
        return pl.BlockSpec((blk, width), lambda i: (i, 0))

    return pl.pallas_call(
        functools.partial(feed_kernel, count, blocks),
        grid=(len(blocks),),
        in_specs=[
            pl.BlockSpec(memory_space=pltpu.SMEM),
            vmem_whole((1, model)),
            vmem_whole((model, units)),
            vmem_whole((units, model)),
        ]
        + [ctx_spec(slot) for slot in range(count)]
        + [vmem_whole((blk, model))] * len(blocks)
        + [vmem_whole(joined[0].shape)] * count,
        out_specs=[
            by_row(model),
            by_row(model),
            by_row(units),
            by_row(units),
            by_row(model),
            by_row(model),
            by_row(model),
        ],
        out_shape=[
            jax.ShapeDtypeStruct((rows, model), F32),
            jax.ShapeDtypeStruct((rows, model), BF16),
            jax.ShapeDtypeStruct((rows, units), BF16),
            jax.ShapeDtypeStruct((rows, units), BF16),
            jax.ShapeDtypeStruct((rows, model), BF16),
            jax.ShapeDtypeStruct((rows, model), BF16),
            jax.ShapeDtypeStruct((rows, model), BF16),
        ],
        scratch_shapes=[pltpu.VMEM((blk, model), F32), pltpu.VMEM((blk, model), BF16)],
        compiler_params=kernel_params(48),
        cost_estimate=pl.CostEstimate(
            flops=2 * rows * model * (model + 4 * units) * 2,
            bytes_accessed=12 << 20,
            transcendentals=rows * units,
        ),
        name="feed",
    )(scale, gain, w_in, w_back, *ctx, *[tok[b] for b in blocks], *joined)


def norm_back(dnormed, values, gain):
    spread = norm_rows(values)
    inner = jnp.mean(gain * dnormed * values, axis=-1, keepdims=True)
    dvalues = spread * (gain * dnormed - values * (spread * spread * inner))
    return dvalues, dnormed * values * spread


def attend_back_kernel(
    heads,
    count,
    bucket_count,
    scale_ref,
    starts_ref,
    buckets_ref,
    gain_ref,
    w_out_ref,
    dn_low_ref,
    dn_high_ref,
    hidden_low_ref,
    hidden_high_ref,
    cot_low_ref,
    cot_high_ref,
    ctx_ref,
    linv_ref,
    exps_ref,
    q_ref,
    k_ref,
    v_ref,
    dh_ref,
    dh_own_ref,
    dgain_ref,
    djoint_ref,
    dtable_ref,
    dk_ref,
    dv_ref,
    acc_ref,
    dh_now,
):
    step = pl.program_id(0)
    blk = dh_ref.shape[0]
    seq = blk * count
    head_cols = ctx_ref.shape[1]
    width = head_cols // heads
    wide = 2 * seq
    half = count // 2

    @pl.when(step == 0)
    def _():
        dk_ref[...] = jnp.zeros_like(dk_ref)
        dv_ref[...] = jnp.zeros_like(dv_ref)
        acc_ref[...] = jnp.zeros_like(acc_ref)

    for side in range(2):
        dn_ref = (dn_low_ref, dn_high_ref)[side]
        hidden_ref = (hidden_low_ref, hidden_high_ref)[side]
        cot_ref = (cot_low_ref, cot_high_ref)[side]

        @pl.when(step // half == side)
        def _():
            dhidden, dgain = norm_back(dn_ref[...].astype(F32), hidden_ref[...], gain_ref[...])
            dhidden = dhidden + cot_ref[...].astype(F32)
            dh_now[...] = dhidden
            if side == 0:

                @pl.when(step == 0)
                def _():
                    dgain_ref[...] = jnp.broadcast_to(
                        jnp.sum(dgain, axis=0, keepdims=True), dgain_ref.shape
                    )
                    dh_own_ref[...] = dhidden

    row0 = pl.multiple_of(step * blk, blk)
    first_row = starts_ref[step]
    dhidden = dh_now[...].astype(BF16)
    dh_ref[...] = dhidden
    dctx = dot_nt(dhidden, w_out_ref[...])
    ctx = ctx_ref[...].astype(F32)
    product = dctx * ctx
    lane = lax.broadcasted_iota(jnp.int32, (blk, LANES - width), 1)
    dquery = []
    for h in range(heads):
        cols = slice(h * width, (h + 1) * width)
        inverse = linv_ref[:, h : h + 1]
        inner = -jnp.sum(product[:, cols], axis=1, keepdims=True) * inverse
        coarse = inner.astype(BF16).astype(F32)
        extra = jnp.where(lane == 0, coarse, jnp.where(lane == 1, inner - coarse, 0.0))
        given = jnp.concatenate((dctx[:, cols] * inverse, extra), axis=1).astype(BF16)
        exps = exps_ref[h]
        dscores = exps.astype(F32) * dot_nt(given, v_ref[h])
        low = dscores.astype(BF16)
        dquery.append(dot_nn(low, k_ref[h])[:, :width])
        dk_ref[h] += dot_tn(low, q_ref[h, pl.ds(row0, blk)])
        dv_ref[h] += dot_tn(exps, given)
        for a in range(blk // LANES):
            for b in range(count):
                start = seq - LANES - a * LANES - first_row + starts_ref[b]
                place = pl.ds(pl.multiple_of(start, LANES), blk)
                acc_ref[h, :, place] += dscores[a * LANES : (a + 1) * LANES, b * blk : (b + 1) * blk]
    djoint_ref[pl.ds(row0, blk), 0:head_cols] = jnp.concatenate(dquery, axis=1).astype(BF16)

    @pl.when(step == count - 1)
    def _():
        dkeys = [dk_ref[h][:, :width] for h in range(heads)]
        dvalues = [dv_ref[h][:, :width] for h in range(heads)]
        djoint_ref[:, head_cols : 2 * head_cols] = jnp.concatenate(dkeys, axis=1).astype(BF16)
        djoint_ref[:, 2 * head_cols :] = jnp.concatenate(dvalues, axis=1).astype(BF16)
        which = buckets_ref[...]
        drel = []
        for h in range(heads):
            part = acc_ref[h]
            rows = LANES
            while rows > 1:
                rows //= 2
                part = part[:rows] + pltpu.roll(part[rows:], wide - rows, 1)
            drel.append(pltpu.roll(part, LANES - 1, 1))
        drel = jnp.concatenate(drel + [jnp.zeros((8 - heads, wide), F32)], axis=0)
        column = lax.broadcasted_iota(jnp.int32, dtable_ref.shape, 1)
        dtable = jnp.zeros(dtable_ref.shape, F32)
        for b in range(bucket_count):
            total = jnp.sum(jnp.where(which == b, drel, 0.0), axis=1, keepdims=True)
            dtable = jnp.where(column == b, total, dtable)
        dtable_ref[...] = dtable


def attend_back(bucket_count, scale, starts, buckets, gain, w_out, dn, hidden, cot, ctx, linv, exps, q, k, v):
    head_cols, model = w_out.shape
    heads, seq = exps.shape[:2]
    half_rows = hidden[0].shape[0]
    count = starts.shape[0]
    blk = seq // count
    half = count // 2
    smem = pl.BlockSpec(memory_space=pltpu.SMEM)
    low = pl.BlockSpec((blk, model), lambda i: (jnp.minimum(i, half - 1), 0))
    high = pl.BlockSpec((blk, model), lambda i: (jnp.maximum(i - half, 0), 0))
    heads_whole = vmem_whole((heads, seq, LANES))
    return pl.pallas_call(
        functools.partial(attend_back_kernel, heads, count, bucket_count),
        grid=(count,),
        in_specs=[
            smem,
            smem,
            vmem_whole((8, 2 * seq)),
            vmem_whole((1, model)),
            vmem_whole((head_cols, model)),
            low,
            high,
            low,
            high,
            low,
            high,
            pl.BlockSpec((blk, head_cols), lambda i: (i, 0)),
            pl.BlockSpec((blk, LANES), lambda i: (i, 0)),
            pl.BlockSpec((heads, blk, seq), lambda i: (0, i, 0)),
            heads_whole,
            heads_whole,
            heads_whole,
        ],
        out_specs=[
            pl.BlockSpec((blk, model), lambda i: (i, 0)),
            vmem_whole((blk, model)),
            vmem_whole((8, model)),
            vmem_whole((seq, 3 * head_cols)),
            vmem_whole((8, LANES)),
        ],
        out_shape=[
            jax.ShapeDtypeStruct((seq, model), BF16),
            jax.ShapeDtypeStruct((blk, model), F32),
            jax.ShapeDtypeStruct((8, model), F32),
            jax.ShapeDtypeStruct((seq, 3 * head_cols), BF16),
            jax.ShapeDtypeStruct((8, LANES), F32),
        ],
        scratch_shapes=[
            pltpu.VMEM((heads, seq, LANES), F32),
            pltpu.VMEM((heads, seq, LANES), F32),
            pltpu.VMEM((heads, LANES, 2 * seq), F32),
            pltpu.VMEM((blk, model), F32),
        ],
        compiler_params=kernel_params(56),
        cost_estimate=pl.CostEstimate(
            flops=2 * 4 * seq * seq * head_cols * 6, bytes_accessed=16 << 20, transcendentals=0
        ),
        name="attend_back",
    )(scale, starts, buckets, gain, w_out, *dn, *hidden, *cot, ctx, linv, exps, q, k, v)


def inputs_back_kernel(gain_ref, djoint_ref, w_ref, tok_ref, dnormed_ref, dgain_ref):
    step = pl.program_id(0)
    dnormed = dot_nt(djoint_ref[...], w_ref[...])
    dnormed_ref[...] = dnormed.astype(BF16)
    values = tok_ref[...].astype(F32)
    part = jnp.sum(dnormed * (values * norm_rows(values)), axis=0, keepdims=True)

    @pl.when(step == 0)
    def _():
        dgain_ref[...] = jnp.zeros_like(dgain_ref)

    dgain_ref[...] += jnp.broadcast_to(part, dgain_ref.shape)


def inputs_back(gain, djoint, w_joint, tok, blk):
    seq, model = tok.shape
    cols = djoint.shape[1]
    return pl.pallas_call(
        inputs_back_kernel,
        grid=(seq // blk,),
        in_specs=[
            vmem_whole((1, model)),
            pl.BlockSpec((blk, cols), lambda i: (i, 0)),
            vmem_whole((model, cols)),
            pl.BlockSpec((blk, model), lambda i: (i, 0)),
        ],
        out_specs=[pl.BlockSpec((blk, model), lambda i: (i, 0)), vmem_whole((8, model))],
        out_shape=[
            jax.ShapeDtypeStruct((seq, model), BF16),
            jax.ShapeDtypeStruct((8, model), F32),
        ],
        compiler_params=kernel_params(32),
        cost_estimate=pl.CostEstimate(
            flops=2 * seq * model * cols * 2, bytes_accessed=6 << 20, transcendentals=0
        ),
        name="inputs_back",
    )(gain, djoint, w_joint, tok)


def shards(
    tokens,
    row_lengths,
    instruction_mask,
    task_groups,
    rel_buckets,
    gain_attn,
    w_query,
    w_key,
    w_value,
    rel_table,
    w_out,
    gain_ffn,
    w_in,
    w_back,
    out_grad,
):
    blk, model = tokens.shape[1:]
    count = lax.axis_size("tensor")
    head_cols = w_query.shape[1]
    heads = rel_table.shape[1]
    seq = blk * count
    here = lax.axis_index("tensor")
    starts = (here ^ jnp.array(block_order(count), jnp.int32)) * blk
    gain_attn = gain_attn[None, :]
    gain_ffn = gain_ffn[None, :]
    buckets = jnp.broadcast_to(jnp.pad(rel_buckets, (0, 1), constant_values=-1)[None], (8, 2 * seq))

    own_group = lax.dynamic_slice_in_dim(task_groups, lax.axis_index("dp"), 1)
    scale = lax.rsqrt(jnp.sum((own_group == task_groups).astype(F32)))[None]
    positions = here * blk + jnp.arange(blk, dtype=jnp.int32)
    keep = (positions < row_lengths[0]) & (instruction_mask[0] == 0)
    masked_grad = jnp.where(keep[:, None], out_grad[0], 0).astype(BF16)

    tok = gather_tensor(tokens[0], count)
    joined = gather_tensor(jnp.concatenate((masked_grad, w_out)), count)

    ctx, exps, linv, normed, q, k, v = attend(
        row_lengths, starts, rel_table, buckets, gain_attn, w_query, w_key, w_value, tok
    )
    contexts = gather_tensor(ctx, count)
    half = count // 2
    high = feed(list(range(half, count)), scale, gain_ffn, w_in, w_back, contexts, tok, joined)
    low = feed(list(range(half)), scale, gain_ffn, w_in, w_back, contexts, tok, joined)

    def whole(index):
        return jnp.concatenate((low[index], high[index]))

    bits = tensor_bits(count)
    came = swap_tensor(high[4], bits[-1])
    summed = (low[4].astype(F32) + came.astype(F32)).astype(BF16)
    pieces = [summed[b * blk : (b + 1) * blk] for b in range(half)]
    for bit in reversed(bits[:-1]):
        flip = block_order(count).index(bit)
        came = [swap_tensor(pieces[b ^ flip], bit) for b in range(half)]
        pieces = [(a.astype(F32) + b.astype(F32)).astype(BF16) for a, b in zip(pieces, came, strict=True)]
    summed = jnp.concatenate(pieces)
    dn = (summed, swap_tensor(summed, bits[-1]))

    grad_back = dot_tn(whole(2), whole(6)).astype(BF16)
    grad_in = dot_tn(whole(1), whole(3)).astype(BF16)

    dh, dh_own, dgain_ffn, djoint, dtable = attend_back(
        rel_table.shape[0],
        scale,
        starts,
        buckets,
        gain_ffn,
        w_out,
        dn,
        (low[0], high[0]),
        (low[6], high[6]),
        ctx,
        linv,
        exps,
        q,
        k,
        v,
    )
    w_joint = jnp.concatenate((w_query, w_key, w_value), axis=1)
    grad_joint = jnp.concatenate((dot_tn(normed, djoint), dot_tn(dh, ctx)), axis=1).astype(BF16)
    dnormed, dgain_attn = inputs_back(gain_attn, djoint, w_joint, jnp.concatenate(tok), blk)

    mixed_sum = scatter_tensor(whole(5), count)
    mixed = (low[0][:blk] + mixed_sum.astype(F32)).astype(BF16)[None]
    dn_attn = scatter_tensor(dnormed, count).astype(F32)
    dinputs, _ = norm_back(dn_attn, tokens[0].astype(F32), gain_attn)
    grad_tokens = (dh_own + dinputs)[None]

    grad_back = sum_dp(grad_back).astype(F32)
    grad_in = sum_dp(grad_in).astype(F32)
    grad_joint = sum_dp(grad_joint).astype(F32)
    dtable = jnp.pad(dtable, ((0, 0), (0, model - dtable.shape[1])))
    gains = jnp.concatenate((dgain_attn[:4], dgain_ffn[:4]))
    dtable, gains = sum_small(dtable, gains, count)
    grad_table = dtable[:heads, : rel_table.shape[0]].T
    return (
        mixed,
        grad_tokens,
        gains[0],
        grad_joint[:, :head_cols],
        grad_joint[:, head_cols : 2 * head_cols],
        grad_joint[:, 2 * head_cols : 3 * head_cols],
        grad_table,
        grad_joint[:, 3 * head_cols :].T,
        gains[4],
        grad_in,
        grad_back,
    )


def solution(mesh):
    return jax.shard_map(
        shards,
        mesh=mesh,
        in_specs=(
            P("dp", "tensor", None),
            P("dp"),
            P("dp", "tensor"),
            P(),
            P(),
            P(),
            P(None, "tensor"),
            P(None, "tensor"),
            P(None, "tensor"),
            P(None, "tensor"),
            P("tensor", None),
            P(),
            P(None, "tensor"),
            P("tensor", None),
            P("dp", "tensor", None),
        ),
        out_specs=(
            P("dp", "tensor", None),
            P("dp", "tensor", None),
            P(),
            P(None, "tensor"),
            P(None, "tensor"),
            P(None, "tensor"),
            P(None, "tensor"),
            P("tensor", None),
            P(),
            P(None, "tensor"),
            P("tensor", None),
        ),
        check_vma=False,
    )
```

```python
import functools

import jax
import jax.numpy as jnp
from jax import lax
from jax.experimental import pallas as pl
from jax.experimental.pallas import tpu as pltpu
from jax.sharding import PartitionSpec as P

NORM_EPS = 1e-06
MASK_FILL = -1000000000.0
F32 = jnp.float32
BF16 = jnp.bfloat16
LANES = 128
FREE = jax.ShapeDtypeStruct
FAR = pltpu.HBM
HEAVY = pl.CostEstimate(flops=10**11, bytes_accessed=1024, transcendentals=0)
LIGHT = pl.CostEstimate(flops=1024, bytes_accessed=1024, transcendentals=0)
GELU_SCALE = 0.7978845608028654
GELU_CUBE = 0.044715


def dot_nn(left, right):
    return jnp.dot(left, right, preferred_element_type=F32)


def dot_nt(left, right):
    return lax.dot_general(left, right, (((1,), (1,)), ((), ())), preferred_element_type=F32)


def dot_tn(left, right):
    return lax.dot_general(left, right, (((0,), (0,)), ((), ())), preferred_element_type=F32)


def vmem_whole(shape):
    return pl.BlockSpec(shape, lambda i: (0,) * len(shape))


class Came:
    def __init__(self, array):
        self.array = array


def local_call(kernel, *, out_shape, grid, in_specs, out_specs, scratch_shapes=(), prefetch=0, mib, name, cost=LIGHT):
    def place(value, spec):
        if isinstance(value, Came):
            return value.array
        if value.ndim < 2 or spec.memory_space is pltpu.SMEM:
            return value
        return pltpu.with_memory_space_constraint(value, pltpu.HBM)

    def run(*args):
        given = [place(value, spec) for value, spec in zip(args[prefetch:], in_specs, strict=True)]
        return call(*args[:prefetch], *given)

    call = pl.pallas_call(
        kernel,
        grid_spec=pltpu.PrefetchScalarGridSpec(
            num_scalar_prefetch=prefetch,
            grid=grid,
            in_specs=in_specs,
            out_specs=out_specs,
            scratch_shapes=scratch_shapes,
        ),
        out_shape=out_shape,
        compiler_params=pltpu.CompilerParams(vmem_limit_bytes=mib << 20),
        cost_estimate=cost,
        name=name,
    )
    return run


class Turn:
    def __init__(self):
        self.last = None

    def __call__(self, value):
        if self.last is None:
            return value
        return lax.optimization_barrier((value, self.last))[0]

    def done(self, value):
        self.last = value[0] if isinstance(value, (list, tuple)) else value
        return value


def block_order(count):
    order = [0]
    bit = count // 2
    while bit:
        order = order + [slot | bit for slot in order]
        bit //= 2
    return order


def tensor_bits(count):
    bits = []
    bit = count // 2
    while bit:
        bits.append(bit)
        bit //= 2
    return bits


def swap_tensor(value, bit):
    size = lax.axis_size("tensor")
    return lax.ppermute(value, "tensor", [(i, i ^ bit) for i in range(size)])


def gather_tensor(value, count, ready=()):
    slots = [value]
    for bit in tensor_bits(count):
        came = [swap_tensor(piece, bit) for piece in slots]
        if ready:
            came, ready = lax.optimization_barrier((came, ready))
        slots = slots + came
    return slots, ready


def scatter_tensor(value, count, bits=None):
    for bit in reversed(tensor_bits(count) if bits is None else bits):
        half = value.shape[0] // 2
        came = swap_tensor(value[half:], bit)
        value = (value[:half].astype(F32) + came.astype(F32)).astype(BF16)
    return value


def dp_steps(count):
    bits = []
    bit = 1
    while bit < count:
        bits.append(bit)
        bit *= 2
    return list(zip(bits, bits[1::-1] + bits[2:], strict=True))


def swap_dp(value, pair):
    rows, cols = lax.axis_size("dp"), lax.axis_size("tensor")
    route = []
    for row in range(rows):
        for col in range(cols):
            route.append((row * cols + col, (row ^ pair[col % 2]) * cols + col))
    return lax.ppermute(value, ("dp", "tensor"), route)


def side_of(pair):
    row, col = lax.axis_index("dp"), lax.axis_index("tensor")
    bit = jnp.where(col % 2 == 1, pair[1], pair[0])
    return ((row & bit) != 0).astype(jnp.int32)[None]


def add_kernel(left_ref, right_ref, out_ref):
    total = left_ref[...].astype(F32) + right_ref[...].astype(F32)
    out_ref[...] = total.astype(out_ref.dtype)


def add(left, right, cost=LIGHT):
    return local_call(
        add_kernel,
        grid=(1,),
        in_specs=[vmem_whole(left.shape)] * 2,
        out_specs=vmem_whole(left.shape),
        out_shape=FAR(left.shape, left.dtype),
        mib=8,
        name="add",
        cost=cost,
    )(left, Came(right))


def add_pieces_kernel(count, *refs):
    step = pl.program_id(0)
    for k in range(count):

        @pl.when(step == k)
        def _():
            total = refs[0][...].astype(F32) + refs[1][...].astype(F32)
            refs[2 + k][...] = total.astype(BF16)


def add_pieces(left, right, count):
    rows, cols = left.shape
    part = pl.BlockSpec((rows // count, cols), lambda i: (i, 0))
    return local_call(
        functools.partial(add_pieces_kernel, count),
        grid=(count,),
        in_specs=[part, part],
        out_specs=[vmem_whole((rows // count, cols))] * count,
        out_shape=[FAR((rows // count, cols), BF16)] * count,
        mib=10,
        name="add_pieces",
    )(left, Came(right))


def add_swap_kernel(left_ref, right_ref, plain_ref, swapped_ref):
    total = (left_ref[...].astype(F32) + right_ref[...].astype(F32)).astype(BF16)
    plain_ref[...] = total
    swapped_ref[...] = total


def add_swap(left, right, count, flip):
    rows, cols = left.shape
    part = pl.BlockSpec((rows // count, cols), lambda i: (i, 0))
    return local_call(
        add_swap_kernel,
        grid=(count,),
        in_specs=[part, part],
        out_specs=[part, pl.BlockSpec((rows // count, cols), lambda i: (i ^ flip, 0))],
        out_shape=[FAR((rows, cols), BF16), FREE((rows, cols), BF16)],
        mib=10,
        name="add_swap",
    )(left, Came(right))


def fold_kernel(side_ref, kept_ref, came_ref, send_ref, keep_ref):
    total = (kept_ref[...].astype(F32) + came_ref[...].astype(F32)).astype(BF16)

    @pl.when(pl.program_id(0) == 0)
    def _():
        send_ref[...] = total

    @pl.when(pl.program_id(0) == 1)
    def _():
        keep_ref[...] = total


def fold(side, kept, came, cost=LIGHT):
    rows, cols = kept.shape
    half = rows // 2
    if half % 16:
        total = (kept.astype(F32) + came.astype(F32)).astype(BF16)
        return [lax.dynamic_slice_in_dim(total, k * half, half) for k in (1 - side[0], side[0])]
    place = pl.BlockSpec((half, cols), lambda i, side: (jnp.where(i == 0, 1 - side[0], side[0]), 0))
    whole = pl.BlockSpec((half, cols), lambda i, side: (0, 0))
    return local_call(
        fold_kernel,
        grid=(2,),
        in_specs=[place, place],
        out_specs=[whole, whole],
        out_shape=[FREE((half, cols), BF16), FAR((half, cols), BF16)],
        prefetch=1,
        mib=8,
        name="fold",
        cost=cost,
    )(side, kept, Came(came))


def join_kernel(steps, side_ref, own_ref, came_ref, out_ref):
    upper = pl.program_id(0) // steps
    mine = upper == side_ref[0]

    @pl.when(mine)
    def _():
        out_ref[...] = own_ref[...].astype(out_ref.dtype)

    @pl.when(jnp.logical_not(mine))
    def _():
        out_ref[...] = came_ref[...].astype(out_ref.dtype)


def join(side, own, came, cost=LIGHT):
    rows, cols = own.shape
    if rows % 16:
        mine = side[0] != 0
        pair = (jnp.where(mine, came, own), jnp.where(mine, own, came))
        return jnp.concatenate(pair)
    steps = 1
    part = rows // steps
    half = pl.BlockSpec((part, cols), lambda i, side: (i % steps, 0))
    return local_call(
        functools.partial(join_kernel, steps),
        grid=(2 * steps,),
        in_specs=[half, half],
        out_specs=pl.BlockSpec((part, cols), lambda i, side: (i, 0)),
        out_shape=FAR((2 * rows, cols), BF16),
        prefetch=1,
        mib=10,
        name="join",
        cost=cost,
    )(side, own, Came(came))


SMALL = 16


def split_small(value):
    coarse = value.astype(BF16)
    return jnp.concatenate((coarse, (value - coarse.astype(F32)).astype(BF16)), axis=0)


def read_small(rows):
    return rows[:SMALL].astype(F32) + rows[SMALL:].astype(F32)


def fold_small_kernel(side_ref, kept_ref, came_ref, small_came_ref, small_ref, send_ref, keep_ref, small_out_ref):
    total = (kept_ref[...].astype(F32) + came_ref[...].astype(F32)).astype(BF16)
    half = keep_ref.shape[0]

    @pl.when(pl.program_id(0) == 0)
    def _():
        small = split_small(read_small(small_ref) + read_small(small_came_ref))
        send_ref[:half] = total
        send_ref[half:] = small
        small_out_ref[...] = small

    @pl.when(pl.program_id(0) == 1)
    def _():
        keep_ref[...] = total


def fold_small(side, kept, came, small, cost=LIGHT):
    rows, cols = kept.shape
    half = rows // 2
    extra = 2 * SMALL
    if half % extra:
        send, keep = fold(side, kept, came[:rows])
        small = split_small(read_small(small) + read_small(came[rows:]))
        return jnp.concatenate((send, small)), keep, small
    place = pl.BlockSpec((half, cols), lambda i, side: (jnp.where(i == 0, 1 - side[0], side[0]), 0))

    def whole(count):
        return pl.BlockSpec((count, cols), lambda i, side: (0, 0))

    return local_call(
        fold_small_kernel,
        grid=(2,),
        in_specs=[place, place, pl.BlockSpec((extra, cols), lambda i, side: (rows // extra, 0)), whole(extra)],
        out_specs=[whole(half + extra), whole(half), whole(extra)],
        out_shape=[FREE((half + extra, cols), BF16), FAR((half, cols), BF16), FAR((extra, cols), BF16)],
        prefetch=1,
        mib=10,
        name="fold_small",
        cost=cost,
    )(side, kept, Came(came), Came(came), small)


def add_small_kernel(kept_ref, came_ref, small_ref, out_ref, small_out_ref):
    rows = kept_ref.shape[0]
    out_ref[...] = (kept_ref[...].astype(F32) + came_ref[:rows].astype(F32)).astype(BF16)
    small_out_ref[...] = read_small(small_ref) + read_small(came_ref[rows:])


def add_small(kept, came, small, cost=LIGHT):
    rows, cols = kept.shape
    if rows % (2 * SMALL):
        return add(kept, came[:rows]), read_small(small) + read_small(came[rows:])
    return local_call(
        add_small_kernel,
        grid=(1,),
        in_specs=[vmem_whole(kept.shape), vmem_whole(came.shape), vmem_whole(small.shape)],
        out_specs=[vmem_whole(kept.shape), vmem_whole((SMALL, cols))],
        out_shape=[FAR(kept.shape, BF16), FAR((SMALL, cols), F32)],
        mib=8,
        name="add_small",
        cost=cost,
    )(kept, Came(came), small)


class DpSum:
    def __init__(self, turn, send, keep, finish, small=None):
        self.turn, self.finish, self.small = turn, finish, small
        self.pairs = dp_steps(lax.axis_size("dp"))
        self.at = 0
        self.keep = keep
        self.came = swap_dp(send, self.pairs[0])

    def step(self, cost=LIGHT):
        turn, last = self.turn, len(self.pairs) - 1
        came = turn(self.came)
        if self.at < last:
            after = self.pairs[self.at + 1]
            if self.small is None:
                send, self.keep = turn.done(fold(side_of(after), self.keep, came, cost))
            else:
                results = turn.done(fold_small(side_of(after), self.keep, came, self.small, cost))
                send, self.keep, self.small = results
            self.came = swap_dp(send, after)
        elif self.at == last:
            if self.small is None:
                self.keep = turn.done(add(self.keep, came, cost))
            else:
                self.keep, self.small = turn.done(add_small(self.keep, came, self.small, cost))
            self.came = swap_dp(self.keep, self.pairs[last])
        else:
            place = 2 * last + 1 - self.at
            side = side_of(self.pairs[place])
            if place == 0:
                self.result = turn.done(self.finish(side, self.keep, came))
            else:
                self.keep = turn.done(join(side, self.keep, came, cost))
                self.came = swap_dp(self.keep, self.pairs[place - 1])
        self.at += 1

    def rest(self):
        while self.at < 2 * len(self.pairs):
            self.step()
        return self.result


def finish_feed_kernel(side_ref, own_ref, came_ref, back_ref, in_ref):
    step = pl.program_id(0)
    many = back_ref.shape[0]

    def put(source):
        back_ref[...] = source[:many].astype(F32)
        in_ref[...] = source[many:].astype(F32)

    @pl.when(step == side_ref[0])
    def _():
        put(own_ref)

    @pl.when(step != side_ref[0])
    def _():
        put(came_ref)


def finish_feed(side, own, came):
    rows, cols = own.shape
    whole = pl.BlockSpec((rows, cols), lambda i, side: (0, 0))
    return local_call(
        finish_feed_kernel,
        grid=(2,),
        in_specs=[whole, whole],
        out_specs=[pl.BlockSpec((rows // 2, cols), lambda i, side: (i, 0))] * 2,
        out_shape=[FREE((rows, cols), F32)] * 2,
        prefetch=1,
        mib=20,
        name="finish_feed",
    )(side, own, Came(came))


def finish_heads_kernel(side_ref, own_ref, came_ref, q_ref, k_ref, v_ref, out_ref):
    step = pl.program_id(0)
    cols = q_ref.shape[0]
    for half, refs in enumerate(((q_ref, k_ref), (v_ref, out_ref))):
        for source, is_own in ((own_ref, True), (came_ref, False)):

            @pl.when((step == half) & ((side_ref[0] == half) == is_own))
            def _():
                refs[0][...] = source[:cols].astype(F32)
                refs[1][...] = source[cols:].astype(F32)


def finish_heads(side, own, came):
    rows, cols = own.shape
    each = rows // 2
    whole = pl.BlockSpec((rows, cols), lambda i, side: (0, 0))
    return local_call(
        finish_heads_kernel,
        grid=(2,),
        in_specs=[whole, whole],
        out_specs=[pl.BlockSpec((each, cols), lambda i, side: (0, 0))] * 4,
        out_shape=[FREE((each, cols), F32)] * 4,
        prefetch=1,
        mib=12,
        name="finish_heads",
    )(side, own, Came(came))


def norm_rows(values):
    return lax.rsqrt(jnp.mean(values * values, axis=-1, keepdims=True) + NORM_EPS)


def norm_back(dnormed, unit, spread, gain):
    scaled = gain * dnormed
    inner = jnp.mean(scaled * unit, axis=-1, keepdims=True)
    return spread * (scaled - unit * inner), dnormed * unit


def bias_lanes(seq, first_row, first_col):
    start = seq - LANES - first_row + first_col
    return pl.multiple_of(start, LANES)


def attend_kernel(
    heads, count, length_ref, starts_ref, table_ref, buckets_ref, gain_ref, wq_ref, wk_ref, wv_ref, *refs
):
    tok_refs = refs[:count]
    (ctx_ref, exps_ref, linv_ref, normed_ref, tok_all_ref, q_ref, v_ref, k_turned_ref) = refs[count : count + 8]
    k_ref, v_turned_ref, bias_ref, all_normed, scores_ref = refs[count + 8 :]
    step = pl.program_id(0)
    blk = ctx_ref.shape[0]
    seq = blk * count
    head_cols = wq_ref.shape[0]
    width = head_cols // heads
    wide = 2 * seq

    @pl.when(step == 0)
    def _():
        which = buckets_ref[...]
        for h in range(heads):
            rel = jnp.zeros((8, wide), F32)
            for b in range(table_ref.shape[0]):
                rel = jnp.where(which == b, table_ref[b, h], rel)
            full = jnp.broadcast_to(rel[0:1], (LANES, wide))
            bias_ref[h] = pltpu.roll(full, wide - (LANES - 1), 1, stride=1, stride_axis=0)
        lane = lax.broadcasted_iota(jnp.int32, (blk, LANES - width), 1)
        row = lax.broadcasted_iota(jnp.int32, (blk, LANES - width), 0)
        first = lane == 0
        ones_q = jnp.where(first, 1.0, 0.0)
        ones_v = jnp.where(lane < 2, 1.0, 0.0)
        for b in range(count):
            values = tok_refs[b][...].astype(F32)
            normed = (values * norm_rows(values) * gain_ref[...]).astype(BF16)
            rows = slice(b * blk, (b + 1) * blk)
            all_normed[rows] = normed
            masked = first & (row + starts_ref[b] >= length_ref[0])
            fill = jnp.where(masked, MASK_FILL, 0.0)
            query = dot_nt(normed, wq_ref[...])
            keys = dot_nt(normed, wk_ref[...])
            values = dot_nt(normed, wv_ref[...])
            for h in range(heads):
                cols = slice(h * width, (h + 1) * width)
                q_ref[h, rows] = jnp.concatenate((query[:, cols], ones_q), axis=1).astype(BF16)
                own_k = jnp.concatenate((keys[:, cols], fill), axis=1)
                own_v = jnp.concatenate((values[:, cols], ones_v), axis=1)
                k_ref[h, rows] = own_k.astype(BF16)
                v_ref[h, rows] = own_v.astype(BF16)
                k_turned_ref[h, :, rows] = own_k.T.astype(BF16)
                v_turned_ref[h, :, rows] = own_v.T.astype(BF16)

    row0 = pl.multiple_of(step * blk, blk)
    first_query = starts_ref[step]
    normed_ref[...] = all_normed[pl.ds(row0, blk)]
    for b in range(count):

        @pl.when(step == b)
        def _():
            tok_all_ref[...] = tok_refs[b][...]

    outs = []
    linv = jnp.zeros((blk, LANES), F32)
    stat_lane = lax.broadcasted_iota(jnp.int32, (blk, LANES), 1)
    for h in range(heads):
        query = q_ref[h, pl.ds(row0, blk)]
        top = jnp.full((8, blk), -3.0e38, F32)
        for b in range(count):
            for a in range(blk // LANES):
                rows = slice(b * blk + a * LANES, b * blk + (a + 1) * LANES)
                start = bias_lanes(seq, starts_ref[b] + a * LANES, first_query)
                scores = dot_nt(k_ref[h, rows], query) + bias_ref[h, :, pl.ds(start, blk)]
                scores_ref[rows] = scores
                top = jnp.maximum(top, jnp.max(scores.reshape(LANES // 8, 8, blk), axis=0))
        top = jnp.max(top, axis=0, keepdims=True)
        for c in range(seq // LANES):
            rows = slice(c * LANES, (c + 1) * LANES)
            exps_ref[h, rows] = jnp.exp(scores_ref[rows] - top).astype(BF16)
        mixed = dot_nn(v_turned_ref[h], exps_ref[h]).T
        inverse = 1.0 / mixed[:, width : width + 1]
        outs.append(mixed[:, :width] * inverse)
        linv = jnp.where(stat_lane == h, inverse, linv)
    ctx_ref[...] = jnp.concatenate(outs, axis=1).astype(BF16)
    linv_ref[...] = linv


def attend(length, starts, table, buckets, gain, w_query, w_key, w_value, tok):
    count = len(tok)
    blk, model = tok[0].shape
    seq = blk * count
    heads = table.shape[1]
    head_cols = w_query.shape[0]
    smem = pl.BlockSpec(memory_space=pltpu.SMEM)
    flops = 2 * seq * (3 * model * head_cols + 2 * seq * head_cols)
    return local_call(
        functools.partial(attend_kernel, heads, count),
        grid=(count,),
        in_specs=[smem, smem, smem, vmem_whole((8, 2 * seq)), vmem_whole((1, model))]
        + [vmem_whole((head_cols, model))] * 3
        + [vmem_whole((blk, model))] * count,
        out_specs=[
            pl.BlockSpec((blk, head_cols), lambda i: (i, 0)),
            pl.BlockSpec((heads, seq, blk), lambda i: (0, 0, i)),
            pl.BlockSpec((blk, LANES), lambda i: (i, 0)),
            pl.BlockSpec((blk, model), lambda i: (i, 0)),
            pl.BlockSpec((blk, model), lambda i: (i, 0)),
            vmem_whole((heads, seq, LANES)),
            vmem_whole((heads, seq, LANES)),
            vmem_whole((heads, LANES, seq)),
        ],
        out_shape=[
            FAR((seq, head_cols), BF16),
            FAR((heads, seq, seq), BF16),
            FAR((seq, LANES), F32),
            FAR((seq, model), BF16),
            FAR((seq, model), BF16),
            FAR((heads, seq, LANES), BF16),
            FAR((heads, seq, LANES), BF16),
            FAR((heads, LANES, seq), BF16),
        ],
        scratch_shapes=[
            pltpu.VMEM((heads, seq, LANES), BF16),
            pltpu.VMEM((heads, LANES, seq), BF16),
            pltpu.VMEM((heads, LANES, 2 * seq), F32),
            pltpu.VMEM((seq, model), BF16),
            pltpu.VMEM((seq, blk), F32),
        ],
        mib=28,
        name="attend",
        cost=HEAVY,
    )(length, starts, table, buckets, gain, w_query, w_key, w_value, tok[0], *tok[1:])


def feed_kernel(count, side_ref, scale_ref, gain_ref, *refs):
    tok_far, ctx_far, refs = refs[0], refs[1 : 1 + count], refs[1 + count :]
    w_in_far, w_back_far, joined_far, refs = refs[0], refs[1], refs[2 : 2 + count], refs[2 + count :]
    hidden_ref, unit_ref, spread_ref, dn_low_ref, dn_high_ref, out_low_ref, out_high_ref, send_far, keep_far = refs[:9]
    tok_all, ctx_all, w_in_ref, w_back_ref, w_out_ref, grad_all, active_now, dup_all, active_turned = refs[9:18]
    normed_turned, hidden_now, halves, sems, out_sems = refs[18:]
    step = pl.program_id(0)
    blk = hidden_ref.shape[0]
    units = w_in_ref.shape[1]
    head_cols = ctx_all.shape[2]
    many, fewer = units // 2, normed_turned.shape[0] // 2

    def copy(far, near, sem):
        return pltpu.make_async_copy(far, near, sems.at[sem])

    def block_copies(b):
        rows = pl.ds(b * blk, blk)
        found = [copy(tok_far.at[rows], tok_all.at[rows], b)]
        for k in range(count):
            found.append(copy(ctx_far[k].at[pl.ds((b ^ k) * blk, blk)], ctx_all.at[k, rows], count * (1 + k) + b))
        return found

    first_sem = count * (1 + count)
    out_copies, grad_copies = [], []
    for k in range(count):
        place = w_out_ref.at[pl.ds(k * head_cols, head_cols)]
        out_copies.append(copy(joined_far[k].at[pl.ds(blk, head_cols)], place, first_sem + k))
        place = grad_all.at[pl.ds(k * blk, blk)]
        grad_copies.append(copy(joined_far[k].at[pl.ds(0, blk)], place, first_sem + count + k))
    in_copy = copy(w_in_far, w_in_ref, first_sem + 2 * count)
    back_copy = copy(w_back_far, w_back_ref, first_sem + 2 * count + 1)

    @pl.when(step == 0)
    def _():
        for one in [*block_copies(0), *out_copies, in_copy, grad_copies[0], back_copy]:
            one.start()
        for b in range(1, count):
            for one in [*block_copies(b), grad_copies[b]]:
                one.start()
        for one in out_copies:
            one.wait()

    for b in range(count):

        @pl.when(step == b)
        def _():
            for one in block_copies(b):
                one.wait()

    rows = pl.ds(pl.multiple_of(step * blk, blk), blk)
    hidden = tok_all[rows].astype(F32)
    for slot in range(count):
        hidden = hidden + dot_nn(ctx_all[slot, rows], w_out_ref[slot * head_cols : (slot + 1) * head_cols])
    hidden_now[...] = hidden
    strip = 32 if blk % 32 == 0 else blk
    for r in range(0, blk, strip):
        some = slice(r, r + strip)
        hidden = hidden_now[some]
        spread = norm_rows(hidden)
        unit = hidden * spread
        unit_ref[some] = unit.astype(BF16)
        spread_ref[some] = jnp.broadcast_to(spread, (strip, LANES))
        active_now[some, : unit.shape[1]] = (unit * gain_ref[...]).astype(BF16)
    normed = active_now[:, : hidden.shape[1]]
    normed_turned[:, rows] = normed.T

    @pl.when(step == 0)
    def _():
        hidden_ref[...] = hidden_now[...]
        in_copy.wait()
        back_copy.wait()

    for b in range(count):

        @pl.when(step == b)
        def _():
            grad_copies[b].wait()

    grad = grad_all[rows]
    scale = scale_ref[0]
    part = 256 if units % 256 == 0 else units
    normed = normed_turned[:, rows].T
    for c in range(units // part):
        cols = slice(c * part, (c + 1) * part)
        up = dot_nn(normed, w_in_ref[:, cols])
        dactive = dot_nt(grad, w_back_ref[cols])
        square = up * up
        bend = jnp.tanh(up * (GELU_SCALE + GELU_SCALE * GELU_CUBE * square))
        half = 0.5 + 0.5 * bend
        active = (up * half).astype(BF16)
        steep = GELU_SCALE + 3.0 * GELU_SCALE * GELU_CUBE * square
        slope = (half + (0.5 * up) * (1.0 - bend * bend) * steep) * scale
        active_now[:, cols] = active
        active_turned[cols, rows] = active.T
        dup_all[rows, cols] = (dactive * slope).astype(BF16)
    dnormed = dot_nt(dup_all[rows], w_in_ref[...]).astype(BF16)
    out = dot_nn(active_now[:, :units], w_back_ref[...]).astype(BF16)

    @pl.when(step < count // 2)
    def _():
        dn_low_ref[...] = dnormed
        out_low_ref[...] = out

    @pl.when(step >= count // 2)
    def _():
        dn_high_ref[...] = dnormed
        out_high_ref[...] = out

    @pl.when(step == count - 1)
    def _():
        going = []
        for k, (far, side) in enumerate(((send_far, 1 - side_ref[0]), (keep_far, side_ref[0]))):
            back = dot_nn(active_turned[pl.ds(side * many, many)], grad_all[...]) * scale
            halves[k, :many] = back.astype(BF16)
            halves[k, many:] = dot_nn(normed_turned[pl.ds(side * fewer, fewer)], dup_all[...]).astype(BF16)
            going.append(pltpu.make_async_copy(halves.at[k], far, out_sems.at[k]))
            going[-1].start()
        for one in going:
            one.wait()


def feed(side, scale, gain, w_in, w_back, tok, ctx, joined):
    count = len(ctx)
    rows, model = tok.shape
    blk = rows // count
    units = w_in.shape[1]
    head_cols = ctx[0].shape[1]
    half = count // 2

    by_row = pl.BlockSpec((blk, model), lambda i, side: (i, 0))
    low = pl.BlockSpec((blk, model), lambda i, side: (jnp.minimum(i, half - 1), 0))
    high = pl.BlockSpec((blk, model), lambda i, side: (jnp.maximum(i - half, 0), 0))
    anywhere = pl.BlockSpec(memory_space=pl.ANY)

    def whole(shape):
        return pl.BlockSpec(shape, lambda i, side: (0, 0))

    part_rows = FAR((rows // 2, model), BF16)
    grads = ((units + model) // 2, model)
    return local_call(
        functools.partial(feed_kernel, count),
        grid=(count,),
        in_specs=[pl.BlockSpec(memory_space=pltpu.SMEM), whole((1, model))] + [anywhere] * (3 + 2 * count),
        out_specs=[
            whole((blk, model)),
            by_row,
            pl.BlockSpec((blk, LANES), lambda i, side: (i, 0)),
            low,
            high,
            low,
            high,
            anywhere,
            anywhere,
        ],
        out_shape=[FAR((blk, model), F32), FAR((rows, model), BF16), FAR((rows, LANES), F32)]
        + [part_rows] * 4
        + [FAR(grads, BF16)] * 2,
        scratch_shapes=[
            pltpu.VMEM((rows, model), BF16),
            pltpu.VMEM((count, rows, head_cols), BF16),
            pltpu.VMEM((model, units), BF16),
            pltpu.VMEM((units, model), BF16),
            pltpu.VMEM((count * head_cols, model), BF16),
            pltpu.VMEM((rows, model), BF16),
            pltpu.VMEM((blk, max(units, model)), BF16),
            pltpu.VMEM((rows, units), BF16),
            pltpu.VMEM((units, rows), BF16),
            pltpu.VMEM((model, rows), BF16),
            pltpu.VMEM((blk, model), F32),
            pltpu.VMEM((2, *grads), BF16),
            pltpu.SemaphoreType.DMA((count * (3 + count) + 2,)),
            pltpu.SemaphoreType.DMA((2,)),
        ],
        prefetch=1,
        mib=44,
        name="feed",
        cost=HEAVY,
    )(side, scale, gain, tok, *ctx, w_in, w_back, *joined)


def finish_mixed_kernel(hidden_ref, own_ref, came_ref, out_ref):
    total = own_ref[...].astype(F32) + came_ref[...].astype(F32)
    out_ref[...] = (hidden_ref[...] + total).astype(BF16)


def finish_mixed(hidden, own, came):
    blk, model = own.shape
    place = pl.BlockSpec((blk, model), lambda i: (0, 0))
    return local_call(
        finish_mixed_kernel,
        grid=(1,),
        in_specs=[place] * 3,
        out_specs=place,
        out_shape=jax.ShapeDtypeStruct((blk, model), BF16),
        mib=10,
        name="finish_mixed",
    )(hidden, own, Came(came))


def finish_tokens_kernel(gain_ref, tok_ref, own_ref, came_ref, dh_ref, out_ref):
    dnormed = own_ref[...].astype(F32) + came_ref[...].astype(F32)
    values = tok_ref[...].astype(F32)
    spread = norm_rows(values)
    out_ref[...] = dh_ref[...].astype(F32) + norm_back(dnormed, values * spread, spread, gain_ref[...])[0]


def finish_tokens(gain, tok, own, came, dh_own):
    blk, model = own.shape
    steps = 2 if blk % 32 == 0 else 1
    place = pl.BlockSpec((blk // steps, model), lambda i: (i, 0))
    return local_call(
        finish_tokens_kernel,
        grid=(steps,),
        in_specs=[vmem_whole((1, model))] + [place] * 4,
        out_specs=place,
        out_shape=jax.ShapeDtypeStruct((blk, model), F32),
        mib=10,
        name="finish_tokens",
    )(gain, tok, own, Came(came), dh_own)


def attend_back_kernel(heads, count, bucket_count, side_ref, starts_ref, scale_ref, gain_ref, buckets_ref, *refs):
    dn_refs, refs = refs[:count], refs[count:]
    (unit_ref, spread_ref, ctx_ref, linv_ref, exps_ref), refs = refs[:5], refs[5:]
    far_refs, refs = refs[: 9 + count], refs[9 + count :]
    (dh_own_ref, small_ref, send_ref, keep_ref, in_low_ref, in_high_ref), refs = refs[:6], refs[6:]
    near_refs, refs = refs[:10], refs[10:]
    w_out_ref, q_ref, v_ref, k_turned_ref, normed_ref, wq_ref, wk_ref, wv_ref, tok_ref, grad_all = near_refs
    dk_ref, dv_ref, acc_ref, ds_ref, given_ref, dh_all, ctx_all, dn_now, dj_ref, sums_ref, sems = refs
    block, h = pl.program_id(0), pl.program_id(1)
    blk = dn_now.shape[0]
    seq = blk * count
    head_cols = ctx_ref.shape[1]
    width = head_cols // heads
    wide = acc_ref.shape[2]
    copies = [pltpu.make_async_copy(far_refs[k], near_refs[k], sems.at[k]) for k in range(9)]
    for k in range(count):
        place = grad_all.at[pl.ds(k * blk, blk)]
        copies.append(pltpu.make_async_copy(far_refs[9 + k].at[pl.ds(0, blk)], place, sems.at[9 + k]))
    soon, later, last = [*copies[9:], copies[0]], copies[1:4], copies[4:9]
    strip = 32 if blk % 32 == 0 else blk

    @pl.when((block == 0) & (h == 0))
    def _():
        for copy in [*soon, *later, *last]:
            copy.start()
        dk_ref[...] = jnp.zeros_like(dk_ref)
        dv_ref[...] = jnp.zeros_like(dv_ref)
        acc_ref[...] = jnp.zeros_like(acc_ref)
        for copy in soon:
            copy.wait()

    row0 = pl.multiple_of(block * blk, blk)
    now = pl.ds(row0, blk)

    @pl.when(h == 0)
    def _():
        for b in range(count):

            @pl.when(block == b)
            def _():
                dn_now[...] = dn_refs[b][...]

        for r in range(0, blk, strip):
            some = slice(r, r + strip)
            there = pl.ds(pl.multiple_of(row0 + r, strip), strip)
            unit = unit_ref[some].astype(F32)
            scaled = gain_ref[...] * dn_now[some].astype(F32)
            inner = jnp.mean(scaled * unit, axis=-1, keepdims=True)
            dhidden = spread_ref[some, 0:1] * (scaled - unit * inner)
            dh_all[there] = (dhidden + grad_all[there].astype(F32) * scale_ref[0]).astype(BF16)

        @pl.when(block == 0)
        def _():
            total = jnp.zeros((1, dn_now.shape[1]), F32)
            for r in range(0, blk, strip):
                some = slice(r, r + strip)
                product = unit_ref[some].astype(F32) * dn_now[some].astype(F32)
                total += jnp.sum(product, axis=0, keepdims=True)
            sums_ref[...] = jnp.zeros_like(sums_ref)
            sums_ref[12:16] = jnp.broadcast_to(total, (4, total.shape[1]))
            dh_own_ref[...] = dh_all[0:blk]

        ctx_all[now] = ctx_ref[...]
        dctx = dot_nt(dh_all[now], w_out_ref[...])
        product = dctx * ctx_ref[...].astype(F32)
        lane = lax.broadcasted_iota(jnp.int32, (blk, LANES - width), 1)
        for k in range(heads):
            cols = slice(k * width, (k + 1) * width)
            inverse = linv_ref[:, k : k + 1]
            inner = -jnp.sum(product[:, cols], axis=1, keepdims=True) * inverse
            coarse = inner.astype(BF16).astype(F32)
            extra = jnp.where(lane == 0, coarse, jnp.where(lane == 1, inner - coarse, 0.0))
            given_ref[k] = jnp.concatenate((dctx[:, cols] * inverse, extra), axis=1).astype(BF16)

    @pl.when((block == 0) & (h == 0))
    def _():
        for copy in later:
            copy.wait()

    given = given_ref[h]
    first_query = starts_ref[block]
    for b in range(count):
        for a in range(blk // LANES):
            rows = slice(b * blk + a * LANES, b * blk + (a + 1) * LANES)
            dscores = exps_ref[0, rows].astype(F32) * dot_nt(v_ref[h, rows], given)
            ds_ref[rows] = dscores.astype(BF16)
            start = bias_lanes(seq, starts_ref[b] + a * LANES, first_query)
            acc_ref[h, :, pl.ds(start, blk)] += dscores
    dk_ref[h] += dot_nn(ds_ref[...], q_ref[h, now])
    dv_ref[h] += dot_nn(exps_ref[0], given)
    dquery = dot_nn(k_turned_ref[h], ds_ref[...]).T[:, :width].astype(BF16)
    for k in range(heads):

        @pl.when(h == k)
        def _():
            dj_ref[0, now, k * width : (k + 1) * width] = dquery

    @pl.when((block == count - 1) & (h == heads - 1))
    def _():
        dj_ref[1] = jnp.concatenate([dk_ref[k][:, :width] for k in range(heads)], axis=1).astype(BF16)
        dj_ref[2] = jnp.concatenate([dv_ref[k][:, :width] for k in range(heads)], axis=1).astype(BF16)
        for copy in last:
            copy.wait()
        gain_total = jnp.zeros((1, tok_ref.shape[1]), F32)
        for b in range(count):
            rows = slice(b * blk, (b + 1) * blk)
            dnormed = dot_nn(dj_ref[0, rows], wq_ref[...])
            dnormed = dnormed + dot_nn(dj_ref[1, rows], wk_ref[...])
            dnormed = dnormed + dot_nn(dj_ref[2, rows], wv_ref[...])
            out = (in_low_ref, in_high_ref)[b // (count // 2)]
            base = (b % (count // 2)) * blk
            for r in range(0, blk, strip):
                some = slice(r, r + strip)
                values = tok_ref[b * blk + r : b * blk + r + strip].astype(F32)
                gain_total += jnp.sum(dnormed[some] * (values * norm_rows(values)), axis=0, keepdims=True)
                out[base + r : base + r + strip] = dnormed[some].astype(BF16)
        sums_ref[8:12] = jnp.broadcast_to(gain_total, (4, gain_total.shape[1]))

        which = buckets_ref[...]
        drel = []
        for k in range(heads):
            part = acc_ref[k]
            rows = LANES
            while rows > 1:
                rows //= 2
                part = part[:rows] + pltpu.roll(part[rows:], wide - rows, 1)
            drel.append(pltpu.roll(part, LANES - 1, 1))
        drel = jnp.concatenate(drel + [jnp.zeros((8 - heads, wide), F32)], axis=0)
        bucket = lax.broadcasted_iota(jnp.int32, (LANES, wide), 0)
        onehot = jnp.where(bucket == jnp.broadcast_to(which[0:1], (LANES, wide)), 1.0, 0.0).astype(BF16)
        table = jnp.zeros((8, LANES), F32)
        for _ in range(3):
            coarse = drel.astype(BF16)
            table = table + dot_nt(jnp.concatenate((coarse, jnp.zeros_like(coarse)), axis=0), onehot)[:8]
            drel = drel - coarse.astype(F32)
        sums_ref[0:8, 0:LANES] = table
        small = split_small(sums_ref[...])
        small_ref[...] = small
        for side in range(2):

            @pl.when(side_ref[0] == side)
            def _():
                near, other = (keep_ref, send_ref) if side == 0 else (send_ref, keep_ref)
                near[:head_cols] = dot_tn(dj_ref[0], normed_ref[...]).astype(BF16)
                near[head_cols : 2 * head_cols] = dot_tn(dj_ref[1], normed_ref[...]).astype(BF16)
                other[:head_cols] = dot_tn(dj_ref[2], normed_ref[...]).astype(BF16)
                other[head_cols : 2 * head_cols] = dot_tn(ctx_all[...], dh_all[...]).astype(BF16)

        send_ref[2 * head_cols :] = small


def attend_back(bucket_count, side, starts, scale, gain, w_out, buckets, dn, unit, spread, joined, ctx, linv, exps, q, v, k_turned, normed, weights, tok):
    head_cols, model = w_out.shape
    count = starts.shape[0]
    heads, seq = exps.shape[:2]
    assert bucket_count <= LANES and heads <= 8
    blk = seq // count

    def block(cols):
        return pl.BlockSpec((blk, cols), lambda i, h, side: (i, 0))

    def whole(shape):
        return pl.BlockSpec(shape, lambda i, h, side: (0,) * len(shape))

    near = [w_out, q, v, k_turned, normed, *weights, tok]
    smem = pl.BlockSpec(memory_space=pltpu.SMEM)
    extra = 2 * SMALL
    outs = [(blk, model), (extra, model), (2 * head_cols + extra, model), (2 * head_cols, model), (seq // 2, model), (seq // 2, model)]
    return local_call(
        functools.partial(attend_back_kernel, heads, count, bucket_count),
        grid=(count, heads),
        in_specs=[
            smem,
            smem,
            whole((1, model)),
            whole((8, 2 * seq)),
            *[whole((blk, model))] * count,
            block(model),
            block(LANES),
            block(head_cols),
            block(LANES),
            pl.BlockSpec((1, seq, blk), lambda i, h, side: (h, 0, i)),
            *[pl.BlockSpec(memory_space=pl.ANY)] * (len(near) + count),
        ],
        out_specs=[whole(shape) for shape in outs],
        out_shape=[FAR(shape, BF16) for shape in outs],
        scratch_shapes=[pltpu.VMEM(a.shape, a.dtype) for a in near]
        + [
            pltpu.VMEM((seq, model), BF16),
            pltpu.VMEM((heads, seq, LANES), F32),
            pltpu.VMEM((heads, seq, LANES), F32),
            pltpu.VMEM((heads, LANES, 2 * seq), F32),
            pltpu.VMEM((seq, blk), BF16),
            pltpu.VMEM((heads, blk, LANES), BF16),
            pltpu.VMEM((seq, model), BF16),
            pltpu.VMEM((seq, head_cols), BF16),
            pltpu.VMEM((blk, model), BF16),
            pltpu.VMEM((3, seq, head_cols), BF16),
            pltpu.VMEM((SMALL, model), F32),
            pltpu.SemaphoreType.DMA((len(near) + count,)),
        ],
        prefetch=1,
        mib=52,
        name="attend_back",
    )(side, starts, scale, gain, buckets, *dn, unit, spread, ctx, linv, exps, *near, *joined)


def shards(
    tokens,
    row_lengths,
    instruction_mask,
    task_groups,
    rel_buckets,
    gain_attn,
    w_query,
    w_key,
    w_value,
    rel_table,
    w_out,
    gain_ffn,
    w_in,
    w_back,
    out_grad,
):
    blk, model = tokens.shape[1:]
    count = lax.axis_size("tensor")
    head_cols = w_query.shape[1]
    bucket_count, heads = rel_table.shape
    width = head_cols // heads
    seq = blk * count
    half = count // 2
    bits = tensor_bits(count)
    here = lax.axis_index("tensor")
    starts = (here ^ jnp.array(block_order(count), jnp.int32)) * blk
    weights = (w_query.T, w_key.T, w_value.T)
    gain_attn = gain_attn[None, :]
    gain_ffn = gain_ffn[None, :]
    turned = jnp.pad(rel_buckets[::-1], (0, 1), constant_values=-1)
    buckets = jnp.broadcast_to(turned[None], (8, 2 * seq))
    first_side = side_of(dp_steps(lax.axis_size("dp"))[0])

    own_group = lax.dynamic_slice_in_dim(task_groups, lax.axis_index("dp"), 1)
    scale = lax.rsqrt(jnp.sum((own_group == task_groups).astype(F32)))[None]
    positions = here * blk + jnp.arange(blk, dtype=jnp.int32)
    keep = (positions < row_lengths[0]) & (instruction_mask[0] == 0)
    masked_grad = jnp.where(keep[:, None], out_grad[0], 0).astype(BF16)

    turn = Turn()
    low_bits = bits[:-1]

    def across(pieces):
        while len(pieces) > 1:
            bit = low_bits[len(low_bits) - len(pieces).bit_length() + 1]
            near = len(pieces) // 2
            others = [swap_tensor(piece, bit) for piece in pieces[near:]]
            pieces = list(zip(pieces[:near], others, strict=True))
            if near > 1:
                pieces = [turn.done(add(a, turn(b))) for a, b in pieces]
        return pieces[0]

    own_tok = tokens[0]
    joined = jnp.concatenate((masked_grad, w_out))
    ready = (joined, starts, scale, buckets, gain_attn, gain_ffn, rel_table)
    tok, ready = gather_tensor(own_tok, count, ready)
    joined, starts, scale, buckets, gain_attn, gain_ffn, rel_table = ready
    joined = [joined]
    for bit in low_bits:
        joined = joined + [swap_tensor(piece, bit) for piece in joined]
    ctx, exps, linv, normed, tok_all, q, v, k_turned = turn.done(
        attend(row_lengths, starts, rel_table, buckets, gain_attn, *weights, tok)
    )
    contexts, _ = gather_tensor(ctx, count)
    joined = [turn(piece) for piece in joined]
    joined = joined + [swap_tensor(piece, bits[-1]) for piece in joined]
    hidden, unit, spread, dn_low, dn_high, out_low, out_high, feed_send, feed_keep = turn.done(
        feed(first_side, scale, gain_ffn, w_in, w_back, tok_all, contexts, joined)
    )
    dn_came = swap_tensor(dn_high, bits[-1])
    out_came = swap_tensor(out_high, bits[-1])
    sum_feed = DpSum(turn, feed_send, feed_keep, finish_feed)

    assert half == 2 and len(low_bits) == 1
    flip = block_order(count).index(low_bits[0])
    dn_low, dn_sent = turn.done(add_swap(dn_low, turn(dn_came), half, flip))
    dn_came = swap_tensor(dn_sent, low_bits[0])
    out_own = turn.done(add_pieces(out_low, turn(out_came), half))
    sum_feed.step(HEAVY)
    dn_low = turn.done(add_pieces(dn_low, turn(dn_came), half))
    dn_high = [swap_tensor(piece, bits[-1]) for piece in dn_low]
    dh_own, small, heads_send, heads_keep, dn_low, dn_high = turn.done(
        attend_back(
            bucket_count,
            first_side,
            starts,
            scale,
            gain_ffn,
            w_out,
            buckets,
            [*dn_low, *[turn(piece) for piece in dn_high]],
            unit,
            spread,
            joined,
            ctx,
            linv,
            exps,
            q,
            v,
            k_turned,
            normed,
            weights,
            tok_all,
        )
    )
    sum_heads = DpSum(turn, heads_send, heads_keep, finish_heads, small)
    dn_came = swap_tensor(dn_high, bits[-1])
    out_own, out_came = across([turn(piece) for piece in out_own])
    sum_feed.step(HEAVY)
    dn_own = turn.done(add_pieces(dn_low, turn(dn_came), half))
    dn_own, dn_came = across(dn_own)
    sum_heads.step(HEAVY)
    mixed = turn.done(finish_mixed(hidden, out_own, turn(out_came)))[None]
    sum_feed.step(HEAVY)
    grad_tokens = turn.done(finish_tokens(gain_attn, own_tok, dn_own, turn(dn_came), dh_own))[None]
    sum_heads.step(HEAVY)
    sum_feed.step()
    sum_heads.step(HEAVY)
    while sum_heads.at < len(sum_heads.pairs):
        sum_heads.step(HEAVY)
    gains = sum_heads.small[SMALL // 2 :]
    gains_came = swap_tensor(gains, bits[-1])
    sum_heads.step()
    gains = turn.done(add(gains, turn(gains_came)))
    for bit in reversed(low_bits):
        gains_came = swap_tensor(gains, bit)
    sum_feed.step()
    sum_heads.step(HEAVY)
    gains = turn.done(add(gains, turn(gains_came)))
    dtable = sum_heads.small
    grad_back, grad_in = sum_feed.rest()
    grad_query, grad_key, grad_value, grad_out = sum_heads.rest()
    return (
        mixed,
        grad_tokens,
        gains[0],
        grad_query.T,
        grad_key.T,
        grad_value.T,
        dtable[:heads, :bucket_count].T,
        grad_out,
        gains[4],
        grad_in,
        grad_back,
    )


def solution(mesh):
    return jax.shard_map(
        shards,
        mesh=mesh,
        in_specs=(
            P("dp", "tensor", None),
            P("dp"),
            P("dp", "tensor"),
            P(),
            P(),
            P(),
            P(None, "tensor"),
            P(None, "tensor"),
            P(None, "tensor"),
            P(None, "tensor"),
            P("tensor", None),
            P(),
            P(None, "tensor"),
            P("tensor", None),
            P("dp", "tensor", None),
        ),
        out_specs=(
            P("dp", "tensor", None),
            P("dp", "tensor", None),
            P(),
            P(None, "tensor"),
            P(None, "tensor"),
            P(None, "tensor"),
            P(None, "tensor"),
            P("tensor", None),
            P(),
            P(None, "tensor"),
            P("tensor", None),
        ),
        check_vma=False,
    )
```

```python
import functools

import jax
import jax.numpy as jnp
from jax import lax
from jax.experimental import pallas as pl
from jax.experimental.pallas import tpu as pltpu
from jax.sharding import PartitionSpec as P

NORM_EPS = 1e-06
MASK_FILL = -1000000000.0
F32 = jnp.float32
BF16 = jnp.bfloat16
LANES = 128
FREE = jax.ShapeDtypeStruct
FAR = pltpu.HBM
HEAVY = pl.CostEstimate(flops=10**11, bytes_accessed=1024, transcendentals=0)
LIGHT = pl.CostEstimate(flops=1024, bytes_accessed=1024, transcendentals=0)
ORDER = (
    "swap_dn", "feed1", "sum_dn", "feed2", "back", "feed3",
    "swap_out", "swap_in", "two1", "feed4", "two2", "go_mixed",
    "feed5", "two3", "end_tokens", "gains_a", "two4", "end_mixed",
    "gains_b", "two5", "end_feed", "end_heads",
)
LONG = (
    "feed", "end_heads", "end_tokens", "feed4", "swap_out", "two2",
)


def cost_of(name):
    return HEAVY if name in LONG else LIGHT
GELU_SCALE = 0.7978845608028654
GELU_CUBE = 0.044715


def dot_nn(left, right):
    return jnp.dot(left, right, preferred_element_type=F32)


def dot_nt(left, right):
    return lax.dot_general(left, right, (((1,), (1,)), ((), ())), preferred_element_type=F32)


def dot_tn(left, right):
    return lax.dot_general(left, right, (((0,), (0,)), ((), ())), preferred_element_type=F32)


def vmem_whole(shape):
    return pl.BlockSpec(shape, lambda i: (0,) * len(shape))


class Came:
    def __init__(self, array):
        self.array = array


def local_call(kernel, *, out_shape, grid, in_specs, out_specs, scratch_shapes=(), prefetch=0, mib, name, cost=LIGHT):
    def place(value, spec):
        if isinstance(value, Came):
            return value.array
        if value.ndim < 2 or spec.memory_space is pltpu.SMEM:
            return value
        return pltpu.with_memory_space_constraint(value, pltpu.HBM)

    def run(*args):
        given = [place(value, spec) for value, spec in zip(args[prefetch:], in_specs, strict=True)]
        return call(*args[:prefetch], *given)

    call = pl.pallas_call(
        kernel,
        grid_spec=pltpu.PrefetchScalarGridSpec(
            num_scalar_prefetch=prefetch,
            grid=grid,
            in_specs=in_specs,
            out_specs=out_specs,
            scratch_shapes=scratch_shapes,
        ),
        out_shape=out_shape,
        compiler_params=pltpu.CompilerParams(vmem_limit_bytes=mib << 20),
        cost_estimate=cost,
        name=name,
    )
    return run


class Turn:
    def __init__(self):
        self.last = None

    def __call__(self, value):
        if self.last is None:
            return value
        return lax.optimization_barrier((value, self.last))[0]

    def done(self, value):
        self.last = value[0] if isinstance(value, (list, tuple)) else value
        return value


def block_order(count):
    order = [0]
    bit = count // 2
    while bit:
        order = order + [slot | bit for slot in order]
        bit //= 2
    return order


def tensor_bits(count):
    bits = []
    bit = count // 2
    while bit:
        bits.append(bit)
        bit //= 2
    return bits


def swap_tensor(value, bit):
    size = lax.axis_size("tensor")
    return lax.ppermute(value, "tensor", [(i, i ^ bit) for i in range(size)])


def gather_tensor(value, count, ready=()):
    slots = [value]
    for bit in tensor_bits(count):
        came = [swap_tensor(piece, bit) for piece in slots]
        if ready:
            came, ready = lax.optimization_barrier((came, ready))
        slots = slots + came
    return slots, ready


def scatter_tensor(value, count, bits=None):
    for bit in reversed(tensor_bits(count) if bits is None else bits):
        half = value.shape[0] // 2
        came = swap_tensor(value[half:], bit)
        value = (value[:half].astype(F32) + came.astype(F32)).astype(BF16)
    return value


def dp_steps(count):
    bits = []
    bit = 1
    while bit < count:
        bits.append(bit)
        bit *= 2
    return list(zip(bits, bits[1::-1] + bits[2:], strict=True))


def swap_dp(value, pair):
    rows, cols = lax.axis_size("dp"), lax.axis_size("tensor")
    route = []
    for row in range(rows):
        for col in range(cols):
            route.append((row * cols + col, (row ^ pair[col % 2]) * cols + col))
    return lax.ppermute(value, ("dp", "tensor"), route)


def side_of(pair):
    row, col = lax.axis_index("dp"), lax.axis_index("tensor")
    bit = jnp.where(col % 2 == 1, pair[1], pair[0])
    return ((row & bit) != 0).astype(jnp.int32)[None]


def add_kernel(left_ref, right_ref, out_ref):
    total = left_ref[...].astype(F32) + right_ref[...].astype(F32)
    out_ref[...] = total.astype(out_ref.dtype)


def add(left, right, cost=LIGHT):
    return local_call(
        add_kernel,
        grid=(1,),
        in_specs=[vmem_whole(left.shape)] * 2,
        out_specs=vmem_whole(left.shape),
        out_shape=FAR(left.shape, left.dtype),
        mib=8,
        name="add",
        cost=cost,
    )(left, Came(right))


def add_pieces_kernel(count, *refs):
    step = pl.program_id(0)
    for k in range(count):

        @pl.when(step == k)
        def _():
            total = refs[0][...].astype(F32) + refs[1][...].astype(F32)
            refs[2 + k][...] = total.astype(BF16)


def add_pieces(left, right, count, cost=LIGHT):
    rows, cols = left.shape
    part = pl.BlockSpec((rows // count, cols), lambda i: (i, 0))
    return local_call(
        functools.partial(add_pieces_kernel, count),
        grid=(count,),
        in_specs=[part, part],
        out_specs=[vmem_whole((rows // count, cols))] * count,
        out_shape=[FAR((rows // count, cols), BF16)] * count,
        mib=10,
        name="add_pieces",
        cost=cost,
    )(left, Came(right))


def add_swap_kernel(left_ref, right_ref, plain_ref, swapped_ref):
    total = (left_ref[...].astype(F32) + right_ref[...].astype(F32)).astype(BF16)
    plain_ref[...] = total
    swapped_ref[...] = total


def add_swap(left, right, count, flip, cost=LIGHT):
    rows, cols = left.shape
    part = pl.BlockSpec((rows // count, cols), lambda i: (i, 0))
    return local_call(
        add_swap_kernel,
        grid=(count,),
        in_specs=[part, part],
        out_specs=[part, pl.BlockSpec((rows // count, cols), lambda i: (i ^ flip, 0))],
        out_shape=[FAR((rows, cols), BF16), FREE((rows, cols), BF16)],
        mib=10,
        name="add_swap",
        cost=cost,
    )(left, Came(right))


def fold_kernel(side_ref, kept_ref, came_ref, send_ref, keep_ref):
    total = (kept_ref[...].astype(F32) + came_ref[...].astype(F32)).astype(BF16)

    @pl.when(pl.program_id(0) == 0)
    def _():
        send_ref[...] = total

    @pl.when(pl.program_id(0) == 1)
    def _():
        keep_ref[...] = total


def fold(side, kept, came, cost=LIGHT):
    rows, cols = kept.shape
    half = rows // 2
    if half % 16:
        total = (kept.astype(F32) + came.astype(F32)).astype(BF16)
        return [lax.dynamic_slice_in_dim(total, k * half, half) for k in (1 - side[0], side[0])]
    place = pl.BlockSpec((half, cols), lambda i, side: (jnp.where(i == 0, 1 - side[0], side[0]), 0))
    whole = pl.BlockSpec((half, cols), lambda i, side: (0, 0))
    return local_call(
        fold_kernel,
        grid=(2,),
        in_specs=[place, place],
        out_specs=[whole, whole],
        out_shape=[FREE((half, cols), BF16), FAR((half, cols), BF16)],
        prefetch=1,
        mib=8,
        name="fold",
        cost=cost,
    )(side, kept, Came(came))


def join_kernel(steps, side_ref, own_ref, came_ref, out_ref):
    upper = pl.program_id(0) // steps
    mine = upper == side_ref[0]

    @pl.when(mine)
    def _():
        out_ref[...] = own_ref[...].astype(out_ref.dtype)

    @pl.when(jnp.logical_not(mine))
    def _():
        out_ref[...] = came_ref[...].astype(out_ref.dtype)


def join(side, own, came, cost=LIGHT):
    rows, cols = own.shape
    if rows % 16:
        mine = side[0] != 0
        pair = (jnp.where(mine, came, own), jnp.where(mine, own, came))
        return jnp.concatenate(pair)
    steps = 1
    part = rows // steps
    half = pl.BlockSpec((part, cols), lambda i, side: (i % steps, 0))
    return local_call(
        functools.partial(join_kernel, steps),
        grid=(2 * steps,),
        in_specs=[half, half],
        out_specs=pl.BlockSpec((part, cols), lambda i, side: (i, 0)),
        out_shape=FAR((2 * rows, cols), BF16),
        prefetch=1,
        mib=10,
        name="join",
        cost=cost,
    )(side, own, Came(came))


SMALL = 16


def split_small(value):
    coarse = value.astype(BF16)
    return jnp.concatenate((coarse, (value - coarse.astype(F32)).astype(BF16)), axis=0)


def read_small(rows):
    return rows[:SMALL].astype(F32) + rows[SMALL:].astype(F32)


def fold_small_kernel(side_ref, kept_ref, came_ref, small_came_ref, small_ref, send_ref, keep_ref, small_out_ref):
    total = (kept_ref[...].astype(F32) + came_ref[...].astype(F32)).astype(BF16)
    half = keep_ref.shape[0]

    @pl.when(pl.program_id(0) == 0)
    def _():
        small = split_small(read_small(small_ref) + read_small(small_came_ref))
        send_ref[:half] = total
        send_ref[half:] = small
        small_out_ref[...] = small

    @pl.when(pl.program_id(0) == 1)
    def _():
        keep_ref[...] = total


def fold_small(side, kept, came, small, cost=LIGHT):
    rows, cols = kept.shape
    half = rows // 2
    extra = 2 * SMALL
    if half % extra:
        send, keep = fold(side, kept, came[:rows])
        small = split_small(read_small(small) + read_small(came[rows:]))
        return jnp.concatenate((send, small)), keep, small
    place = pl.BlockSpec((half, cols), lambda i, side: (jnp.where(i == 0, 1 - side[0], side[0]), 0))

    def whole(count):
        return pl.BlockSpec((count, cols), lambda i, side: (0, 0))

    return local_call(
        fold_small_kernel,
        grid=(2,),
        in_specs=[place, place, pl.BlockSpec((extra, cols), lambda i, side: (rows // extra, 0)), whole(extra)],
        out_specs=[whole(half + extra), whole(half), whole(extra)],
        out_shape=[FREE((half + extra, cols), BF16), FAR((half, cols), BF16), FAR((extra, cols), BF16)],
        prefetch=1,
        mib=10,
        name="fold_small",
        cost=cost,
    )(side, kept, Came(came), Came(came), small)


def add_small_kernel(kept_ref, came_ref, small_ref, out_ref, small_out_ref):
    rows = kept_ref.shape[0]
    out_ref[...] = (kept_ref[...].astype(F32) + came_ref[:rows].astype(F32)).astype(BF16)
    small_out_ref[...] = read_small(small_ref) + read_small(came_ref[rows:])


def add_small(kept, came, small, cost=LIGHT):
    rows, cols = kept.shape
    if rows % (2 * SMALL):
        return add(kept, came[:rows]), read_small(small) + read_small(came[rows:])
    return local_call(
        add_small_kernel,
        grid=(1,),
        in_specs=[vmem_whole(kept.shape), vmem_whole(came.shape), vmem_whole(small.shape)],
        out_specs=[vmem_whole(kept.shape), vmem_whole((SMALL, cols))],
        out_shape=[FAR(kept.shape, BF16), FAR((SMALL, cols), F32)],
        mib=8,
        name="add_small",
        cost=cost,
    )(kept, Came(came), small)


class DpSum:
    def __init__(self, turn, send, keep, finish, small=None):
        self.turn, self.finish, self.small = turn, finish, small
        self.pairs = dp_steps(lax.axis_size("dp"))
        self.at = 0
        self.keep = keep
        self.came = swap_dp(send, self.pairs[0])

    def step(self, cost=LIGHT):
        turn, last = self.turn, len(self.pairs) - 1
        came = turn(self.came)
        if self.at < last:
            after = self.pairs[self.at + 1]
            if self.small is None:
                send, self.keep = turn.done(fold(side_of(after), self.keep, came, cost))
            else:
                results = turn.done(fold_small(side_of(after), self.keep, came, self.small, cost))
                send, self.keep, self.small = results
            self.came = swap_dp(send, after)
        elif self.at == last:
            if self.small is None:
                self.keep = turn.done(add(self.keep, came, cost))
            else:
                self.keep, self.small = turn.done(add_small(self.keep, came, self.small, cost))
            self.came = swap_dp(self.keep, self.pairs[last])
        else:
            place = 2 * last + 1 - self.at
            side = side_of(self.pairs[place])
            if place == 0:
                self.result = turn.done(self.finish(side, self.keep, came))
            else:
                self.keep = turn.done(join(side, self.keep, came, cost))
                self.came = swap_dp(self.keep, self.pairs[place - 1])
        self.at += 1

    def rest(self):
        while self.at < 2 * len(self.pairs):
            self.step()
        return self.result


def finish_feed_kernel(side_ref, own_ref, came_ref, back_ref, in_ref):
    step = pl.program_id(0)
    many = back_ref.shape[0]

    def put(source):
        back_ref[...] = source[:many].astype(F32)
        in_ref[...] = source[many:].astype(F32)

    @pl.when(step == side_ref[0])
    def _():
        put(own_ref)

    @pl.when(step != side_ref[0])
    def _():
        put(came_ref)


def finish_feed(side, own, came):
    rows, cols = own.shape
    whole = pl.BlockSpec((rows, cols), lambda i, side: (0, 0))
    return local_call(
        finish_feed_kernel,
        grid=(2,),
        in_specs=[whole, whole],
        out_specs=[pl.BlockSpec((rows // 2, cols), lambda i, side: (i, 0))] * 2,
        out_shape=[FREE((rows, cols), F32)] * 2,
        prefetch=1,
        mib=20,
        name="finish_feed",
    )(side, own, Came(came))


def finish_heads_kernel(side_ref, own_ref, came_ref, q_ref, k_ref, v_ref, out_ref):
    step = pl.program_id(0)
    cols = q_ref.shape[0]
    for half, refs in enumerate(((q_ref, k_ref), (v_ref, out_ref))):
        for source, is_own in ((own_ref, True), (came_ref, False)):

            @pl.when((step == half) & ((side_ref[0] == half) == is_own))
            def _():
                refs[0][...] = source[:cols].astype(F32)
                refs[1][...] = source[cols:].astype(F32)


def finish_heads(side, own, came):
    rows, cols = own.shape
    each = rows // 2
    whole = pl.BlockSpec((rows, cols), lambda i, side: (0, 0))
    return local_call(
        finish_heads_kernel,
        grid=(2,),
        in_specs=[whole, whole],
        out_specs=[pl.BlockSpec((each, cols), lambda i, side: (0, 0))] * 4,
        out_shape=[FREE((each, cols), F32)] * 4,
        prefetch=1,
        mib=12,
        name="finish_heads",
    )(side, own, Came(came))


def group_scale(groups_ref, own_ref):
    own = groups_ref[own_ref[0]]
    alike = jnp.int32(0)
    for row in range(groups_ref.shape[0]):
        alike += (groups_ref[row] == own).astype(jnp.int32)
    return lax.rsqrt(jnp.full((1, LANES), alike.astype(F32)))[:, 0:1]


def norm_rows(values):
    return lax.rsqrt(jnp.mean(values * values, axis=-1, keepdims=True) + NORM_EPS)


def norm_back(dnormed, unit, spread, gain):
    scaled = gain * dnormed
    inner = jnp.mean(scaled * unit, axis=-1, keepdims=True)
    return spread * (scaled - unit * inner), dnormed * unit


def bias_lanes(seq, first_row, first_col):
    start = seq - LANES - first_row + first_col
    return pl.multiple_of(start, LANES)


def attend_kernel(
    heads, count, length_ref, starts_ref, table_ref, buckets_ref, gain_ref, wq_ref, wk_ref, wv_ref, *refs
):
    tok_refs = refs[:count]
    (ctx_ref, packed_ref, exps_ref, linv_ref, normed_ref, tok_all_ref) = refs[count : count + 6]
    (q_ref, v_ref, k_turned_ref, k_ref, v_turned_ref, bias_ref, all_normed, scores_ref) = refs[count + 6 :]
    step = pl.program_id(0)
    blk = ctx_ref.shape[0]
    seq = blk * count
    head_cols = wq_ref.shape[0]
    width = head_cols // heads
    wide = 2 * seq

    @pl.when(step == 0)
    def _():
        which = buckets_ref[...]
        for h in range(heads):
            rel = jnp.zeros((8, wide), F32)
            for b in range(table_ref.shape[0]):
                rel = jnp.where(which == b, table_ref[b, h], rel)
            full = jnp.broadcast_to(rel[0:1], (LANES, wide))
            bias_ref[h] = pltpu.roll(full, wide - (LANES - 1), 1, stride=1, stride_axis=0)
        lane = lax.broadcasted_iota(jnp.int32, (blk, LANES - width), 1)
        row = lax.broadcasted_iota(jnp.int32, (blk, LANES - width), 0)
        first = lane == 0
        ones_q = jnp.where(first, 1.0, 0.0)
        ones_v = jnp.where(lane < 2, 1.0, 0.0)
        for b in range(count):
            values = tok_refs[b][...].astype(F32)
            normed = (values * norm_rows(values) * gain_ref[0:1]).astype(BF16)
            rows = slice(b * blk, (b + 1) * blk)
            all_normed[rows] = normed
            masked = first & (row + starts_ref[b] >= length_ref[0])
            fill = jnp.where(masked, MASK_FILL, 0.0)
            query = dot_nt(normed, wq_ref[...])
            keys = dot_nt(normed, wk_ref[...])
            values = dot_nt(normed, wv_ref[...])
            for h in range(heads):
                cols = slice(h * width, (h + 1) * width)
                q_ref[h, rows] = jnp.concatenate((query[:, cols], ones_q), axis=1).astype(BF16)
                own_k = jnp.concatenate((keys[:, cols], fill), axis=1)
                own_v = jnp.concatenate((values[:, cols], ones_v), axis=1)
                k_ref[h, rows] = own_k.astype(BF16)
                v_ref[h, rows] = own_v.astype(BF16)
                k_turned_ref[h, :, rows] = own_k.T.astype(BF16)
                v_turned_ref[h, :, rows] = own_v.T.astype(BF16)

    row0 = pl.multiple_of(step * blk, blk)
    first_query = starts_ref[step]
    normed_ref[...] = all_normed[pl.ds(row0, blk)]
    for b in range(count):

        @pl.when(step == b)
        def _():
            tok_all_ref[...] = tok_refs[b][...]

    outs = []
    linv = jnp.zeros((blk, LANES), F32)
    stat_lane = lax.broadcasted_iota(jnp.int32, (blk, LANES), 1)
    for h in range(heads):
        query = q_ref[h, pl.ds(row0, blk)]
        top = jnp.full((8, blk), -3.0e38, F32)
        for b in range(count):
            for a in range(blk // LANES):
                rows = slice(b * blk + a * LANES, b * blk + (a + 1) * LANES)
                start = bias_lanes(seq, starts_ref[b] + a * LANES, first_query)
                scores = dot_nt(k_ref[h, rows], query) + bias_ref[h, :, pl.ds(start, blk)]
                scores_ref[rows] = scores
                top = jnp.maximum(top, jnp.max(scores.reshape(LANES // 8, 8, blk), axis=0))
        top = jnp.max(top, axis=0, keepdims=True)
        for c in range(seq // LANES):
            rows = slice(c * LANES, (c + 1) * LANES)
            exps_ref[h, rows] = jnp.exp(scores_ref[rows] - top).astype(BF16)
        mixed = dot_nn(v_turned_ref[h], exps_ref[h]).T
        inverse = 1.0 / mixed[:, width : width + 1]
        outs.append(mixed[:, :width] * inverse)
        linv = jnp.where(stat_lane == h, inverse, linv)
    ctx = jnp.concatenate(outs, axis=1).astype(BF16)
    ctx_ref[...] = ctx
    linv_ref[...] = linv
    packed_ref[pl.ds(row0, blk)] = ctx[:, :LANES]
    rest = head_cols - LANES
    for k in range(count):

        @pl.when(step == k)
        def _():
            place = seq + (k % (count // 2)) * blk
            lanes = (k // (count // 2)) * rest
            packed_ref[place : place + blk, lanes : lanes + rest] = ctx[:, LANES:]


def attend(length, starts, table, buckets, gain, w_query, w_key, w_value, tok):
    count = len(tok)
    blk, model = tok[0].shape
    seq = blk * count
    heads = table.shape[1]
    head_cols = w_query.shape[0]
    smem = pl.BlockSpec(memory_space=pltpu.SMEM)
    assert 2 * (head_cols - LANES) == LANES
    return local_call(
        functools.partial(attend_kernel, heads, count),
        grid=(count,),
        in_specs=[smem, smem, smem, vmem_whole((8, 2 * seq)), vmem_whole((2, model))]
        + [vmem_whole((head_cols, model))] * 3
        + [vmem_whole((blk, model))] * count,
        out_specs=[
            pl.BlockSpec((blk, head_cols), lambda i: (i, 0)),
            vmem_whole((seq * 3 // 2, LANES)),
            pl.BlockSpec((heads, seq, blk), lambda i: (0, 0, i)),
            pl.BlockSpec((blk, LANES), lambda i: (i, 0)),
            pl.BlockSpec((blk, model), lambda i: (i, 0)),
            pl.BlockSpec((blk, model), lambda i: (i, 0)),
            vmem_whole((heads, seq, LANES)),
            vmem_whole((heads, seq, LANES)),
            vmem_whole((heads, LANES, seq)),
        ],
        out_shape=[
            FAR((seq, head_cols), BF16),
            FAR((seq * 3 // 2, LANES), BF16),
            FAR((heads, seq, seq), BF16),
            FAR((seq, LANES), F32),
            FAR((seq, model), BF16),
            FAR((seq, model), BF16),
            FAR((heads, seq, LANES), BF16),
            FAR((heads, seq, LANES), BF16),
            FAR((heads, LANES, seq), BF16),
        ],
        scratch_shapes=[
            pltpu.VMEM((heads, seq, LANES), BF16),
            pltpu.VMEM((heads, LANES, seq), BF16),
            pltpu.VMEM((heads, LANES, 2 * seq), F32),
            pltpu.VMEM((seq, model), BF16),
            pltpu.VMEM((seq, blk), F32),
        ],
        mib=28,
        name="attend",
        cost=HEAVY,
    )(length, starts, table, buckets, gain, w_query, w_key, w_value, tok[0], *tok[1:])


def feed_kernel(count, side_ref, groups_ref, own_ref, gain_ref, *refs):
    tok_far, ctx_far, refs = refs[0], refs[1 : 1 + count], refs[1 + count :]
    w_in_far, w_back_far, joined_far, refs = refs[0], refs[1], refs[2 : 2 + count], refs[2 + count :]
    hidden_ref, unit_ref, spread_ref, dn_low_ref, dn_high_ref, out_low_ref, out_high_ref, send_far, keep_far = refs[:9]
    tok_all, ctx_all, w_in_ref, w_back_ref, w_out_ref, grad_all, active_now, dup_all, active_turned = refs[9:18]
    normed_turned, hidden_now, halves, sems, out_sems = refs[18:]
    step = pl.program_id(0)
    blk = hidden_ref.shape[0]
    half = count // 2
    span = blk * half
    units, model = w_back_ref.shape
    rest = LANES // 2
    many, fewer = units // 2, model // 2
    used = 0

    def copy(far, near):
        nonlocal used
        used += 1
        return pltpu.make_async_copy(far, near, sems.at[used - 1])

    row_copies, out_copies, grad_copies = [], [], []
    for b in range(count):
        rows = pl.ds(b * blk, blk)
        found = [copy(tok_far.at[rows], tok_all.at[rows])]
        for k in range(count):
            c = b ^ k
            found.append(copy(ctx_far[k].at[pl.ds(c * blk, blk)], ctx_all.at[k, rows, pl.ds(0, LANES)]))
            place = pl.ds(count * blk + (c % half) * blk, blk)
            found.append(copy(ctx_far[k].at[place], ctx_all.at[k, rows, pl.ds(LANES, LANES)]))
        row_copies.append(found)
        grad_copies.append(copy(joined_far[b].at[pl.ds(0, blk)], grad_all.at[rows]))
    for k in range(count):
        for side in range(2):
            place = w_out_ref.at[side, k, pl.ds(0, LANES)]
            out_copies.append(copy(joined_far[k].at[pl.ds(blk, LANES)], place))
            place = w_out_ref.at[side, k, pl.ds(LANES + side * rest, rest)]
            out_copies.append(copy(joined_far[k].at[pl.ds(blk + LANES, rest)], place))
    in_copy = copy(w_in_far, w_in_ref)
    back_copy = copy(w_back_far, w_back_ref)

    @pl.when(step == 0)
    def _():
        early = [one for b in range(half) for one in row_copies[b]]
        late = [one for b in range(half, count) for one in row_copies[b]]
        for one in [*out_copies, *early, in_copy, *grad_copies[:half], back_copy, *late, *grad_copies[half:]]:
            one.start()
        for side in range(2):
            for k in range(count):
                other = LANES + (1 - side) * rest
                w_out_ref[side, k, other : other + rest] = jnp.zeros((rest, model), BF16)
        for one in out_copies:
            one.wait()

    for part in range(2):

        @pl.when(step == part)
        def _():
            for b in range(part * half, (part + 1) * half):
                for one in row_copies[b]:
                    one.wait()

    rows = pl.ds(pl.multiple_of(step * span, span), span)
    for b in range(half):
        now = slice(b * blk, (b + 1) * blk)
        block = step * half + b
        there = pl.ds(pl.multiple_of(block * blk, blk), blk)
        hidden = tok_all[there].astype(F32)
        for k in range(count):
            side = (block ^ k) // half
            hidden = hidden + dot_nn(ctx_all[k, there], w_out_ref[side, k])
        hidden_now[now] = hidden
    strip = 32 if blk % 32 == 0 else blk
    for r in range(0, span, strip):
        some = slice(r, r + strip)
        hidden = hidden_now[some]
        spread = norm_rows(hidden)
        unit = hidden * spread
        unit_ref[some] = unit.astype(BF16)
        spread_ref[some] = jnp.broadcast_to(spread, (strip, LANES))
        active_now[some, :model] = (unit * gain_ref[1:2]).astype(BF16)
    normed = active_now[:, :model]
    normed_turned[:, rows] = normed.T

    @pl.when(step == 0)
    def _():
        hidden_ref[...] = hidden_now[0:blk]
        in_copy.wait()
        back_copy.wait()

    for part in range(2):

        @pl.when(step == part)
        def _():
            for b in range(part * half, (part + 1) * half):
                grad_copies[b].wait()

    grad = grad_all[rows]
    scale = group_scale(groups_ref, own_ref)
    part = 256 if units % 256 == 0 else units
    ups = [dot_nn(normed, w_in_ref[:, c : c + part]) for c in range(0, units, part)]
    for c, up in zip(range(0, units, part), ups, strict=True):
        cols = slice(c, c + part)
        dactive = dot_nt(grad, w_back_ref[cols])
        square = up * up
        bend = jnp.tanh(up * (GELU_SCALE + GELU_SCALE * GELU_CUBE * square))
        bell = 0.5 + 0.5 * bend
        active = (up * bell).astype(BF16)
        steep = GELU_SCALE + 3.0 * GELU_SCALE * GELU_CUBE * square
        slope = (bell + (0.5 * up) * (1.0 - bend * bend) * steep) * scale
        active_now[:, cols] = active
        active_turned[cols, rows] = active.T
        dup_all[rows, cols] = (dactive * slope).astype(BF16)
    dnormed = dot_nt(dup_all[rows], w_in_ref[...]).astype(BF16)
    out = dot_nn(active_now[:, :units], w_back_ref[...]).astype(BF16)

    @pl.when(step == 0)
    def _():
        dn_low_ref[...] = dnormed
        out_low_ref[...] = out

    @pl.when(step == 1)
    def _():
        dn_high_ref[...] = dnormed
        out_high_ref[...] = out
        going = []
        for k, (far, side) in enumerate(((send_far, 1 - side_ref[0]), (keep_far, side_ref[0]))):
            back = dot_nn(active_turned[pl.ds(side * many, many)], grad_all[...]) * scale
            halves[k, :many] = back.astype(BF16)
            halves[k, many:] = dot_nn(normed_turned[pl.ds(side * fewer, fewer)], dup_all[...]).astype(BF16)
            going.append(pltpu.make_async_copy(halves.at[k], far, out_sems.at[k]))
            going[-1].start()
        for one in going:
            one.wait()


def feed(side, groups, own, gain, w_in, w_back, tok, ctx, joined):
    count = len(ctx)
    rows, model = tok.shape
    blk = rows // count
    units = w_in.shape[1]
    span = rows // 2
    by_row = pl.BlockSpec((span, model), lambda i, side: (i, 0))
    anywhere = pl.BlockSpec(memory_space=pl.ANY)
    smem = pl.BlockSpec(memory_space=pltpu.SMEM)

    def whole(shape):
        return pl.BlockSpec(shape, lambda i, side: (0, 0))

    grads = ((units + model) // 2, model)
    copies = count * (4 + 2 * count) + 2 + 2 * count
    return local_call(
        functools.partial(feed_kernel, count),
        grid=(2,),
        in_specs=[smem, smem, whole((2, model))] + [anywhere] * (3 + 2 * count),
        out_specs=[
            whole((blk, model)),
            by_row,
            pl.BlockSpec((span, LANES), lambda i, side: (i, 0)),
            *[whole((span, model))] * 4,
            anywhere,
            anywhere,
        ],
        out_shape=[FAR((blk, model), F32), FAR((rows, model), BF16), FAR((rows, LANES), F32)]
        + [FAR((span, model), BF16)] * 4
        + [FAR(grads, BF16)] * 2,
        scratch_shapes=[
            pltpu.VMEM((rows, model), BF16),
            pltpu.VMEM((count, rows, 2 * LANES), BF16),
            pltpu.VMEM((model, units), BF16),
            pltpu.VMEM((units, model), BF16),
            pltpu.VMEM((2, count, 2 * LANES, model), BF16),
            pltpu.VMEM((rows, model), BF16),
            pltpu.VMEM((span, max(units, model)), BF16),
            pltpu.VMEM((rows, units), BF16),
            pltpu.VMEM((units, rows), BF16),
            pltpu.VMEM((model, rows), BF16),
            pltpu.VMEM((span, model), F32),
            pltpu.VMEM((2, *grads), BF16),
            pltpu.SemaphoreType.DMA((copies,)),
            pltpu.SemaphoreType.DMA((2,)),
        ],
        prefetch=1,
        mib=52,
        name="feed",
        cost=cost_of("feed"),
    )(side, groups, own, gain, tok, *ctx, w_in, w_back, *joined)


def finish_mixed_kernel(hidden_ref, own_ref, came_ref, out_ref):
    total = own_ref[...].astype(F32) + came_ref[...].astype(F32)
    out_ref[...] = (hidden_ref[...] + total).astype(BF16)


def finish_mixed(hidden, own, came, cost=LIGHT):
    blk, model = own.shape
    place = pl.BlockSpec((blk, model), lambda i: (0, 0))
    return local_call(
        finish_mixed_kernel,
        grid=(1,),
        in_specs=[place] * 3,
        out_specs=place,
        out_shape=jax.ShapeDtypeStruct((blk, model), BF16),
        mib=10,
        name="finish_mixed",
        cost=cost,
    )(hidden, own, Came(came))


def finish_tokens_kernel(gain_ref, tok_ref, own_ref, came_ref, dh_ref, out_ref):
    dnormed = own_ref[...].astype(F32) + came_ref[...].astype(F32)
    values = tok_ref[...].astype(F32)
    spread = norm_rows(values)
    out_ref[...] = dh_ref[...].astype(F32) + norm_back(dnormed, values * spread, spread, gain_ref[0:1])[0]


def finish_tokens(gain, tok, own, came, dh_own, cost=LIGHT):
    blk, model = own.shape
    steps = 2 if blk % 32 == 0 else 1
    place = pl.BlockSpec((blk // steps, model), lambda i: (i, 0))
    return local_call(
        finish_tokens_kernel,
        grid=(steps,),
        in_specs=[vmem_whole((2, model))] + [place] * 4,
        out_specs=place,
        out_shape=jax.ShapeDtypeStruct((blk, model), F32),
        mib=10,
        name="finish_tokens",
        cost=cost,
    )(gain, tok, own, Came(came), dh_own)


def attend_back_kernel(heads, count, side_ref, starts_ref, groups_ref, own_ref, gain_ref, buckets_ref, *refs):
    dn_far, joined_far, refs = refs[:count], refs[count : 2 * count], refs[2 * count :]
    unit_far, spread_far, ctx_far, linv_far, exps_far, w_out_far, refs = *refs[:6], refs[6:]
    late_far, refs = refs[:8], refs[8:]
    dh_own_far, small_far, send_far, keep_far, in_low_far, in_high_far, refs = *refs[:6], refs[6:]
    dn_all, grad_all, unit_all, spread_all, ctx_all, linv_all, exps_all, w_out_ref, refs = *refs[:8], refs[8:]
    late_near, refs = refs[:8], refs[8:]
    v_ref, q_ref, k_turned_ref, normed_ref, tok_ref, wq_ref, wk_ref, wv_ref = late_near
    dk_ref, dv_ref, acc_ref, ds_ref, given_ref, dh_all, dj_ref, sums_ref, in_all, halves, sems, out_sems = refs
    block = pl.program_id(0)
    seq, model = dh_all.shape
    blk = seq // count
    head_cols = ctx_all.shape[1]
    width = head_cols // heads
    wide = acc_ref.shape[2]
    half_cols = 2 * head_cols
    strip = 32 if blk % 32 == 0 else blk

    def first_copies(b):
        rows = pl.ds(b * blk, blk)
        pairs = [
            (dn_far[b], dn_all.at[rows]),
            (unit_far.at[rows], unit_all.at[rows]),
            (spread_far.at[rows], spread_all.at[rows]),
            (joined_far[b].at[pl.ds(0, blk)], grad_all.at[rows]),
            (ctx_far.at[rows], ctx_all.at[rows]),
            (linv_far.at[rows], linv_all.at[rows]),
        ]
        return [pltpu.make_async_copy(far, near, sems.at[7 * b + k]) for k, (far, near) in enumerate(pairs)]

    def exps_copy(b):
        cols = pl.ds(b * blk, blk)
        return pltpu.make_async_copy(exps_far.at[:, :, cols], exps_all.at[b % 2], sems.at[7 * b + 6])

    out_copy = pltpu.make_async_copy(w_out_far, w_out_ref, sems.at[7 * count])
    late = [pltpu.make_async_copy(late_far[k], late_near[k], sems.at[7 * count + 1 + k]) for k in range(8)]

    @pl.when(block == 0)
    def _():
        for copy in [*first_copies(0), out_copy, late[0], exps_copy(0), late[1], late[2], *first_copies(1)]:
            copy.start()
        dk_ref[...] = jnp.zeros_like(dk_ref)
        dv_ref[...] = jnp.zeros_like(dv_ref)
        acc_ref[...] = jnp.zeros_like(acc_ref)

    for b in range(count):

        @pl.when(block == b)
        def _():
            if b + 1 < count:
                exps_copy(b + 1).start()
            if b == 0:
                for k in range(2, count):
                    for copy in first_copies(k):
                        copy.start()
                for copy in late[3:]:
                    copy.start()
            for copy in first_copies(b):
                copy.wait()
            if b == 0:
                out_copy.wait()

    row0 = pl.multiple_of(block * blk, blk)
    now = pl.ds(row0, blk)
    scale = group_scale(groups_ref, own_ref)
    for r in range(0, blk, strip):
        there = pl.ds(pl.multiple_of(row0 + r, strip), strip)
        unit = unit_all[there].astype(F32)
        scaled = gain_ref[1:2] * dn_all[there].astype(F32)
        inner = jnp.mean(scaled * unit, axis=-1, keepdims=True)
        dhidden = spread_all[there, 0:1] * (scaled - unit * inner)
        dh_all[there] = (dhidden + grad_all[there].astype(F32) * scale).astype(BF16)

    dctx = dot_nt(dh_all[now], w_out_ref[...])
    product = dctx * ctx_all[now].astype(F32)
    lane = lax.broadcasted_iota(jnp.int32, (blk, LANES - width), 1)
    for h in range(heads):
        cols = slice(h * width, (h + 1) * width)
        inverse = linv_all[now, h : h + 1]
        inner = -jnp.sum(product[:, cols], axis=1, keepdims=True) * inverse
        coarse = inner.astype(BF16).astype(F32)
        extra = jnp.where(lane == 0, coarse, jnp.where(lane == 1, inner - coarse, 0.0))
        given_ref[h] = jnp.concatenate((dctx[:, cols] * inverse, extra), axis=1).astype(BF16)

    @pl.when(block == 0)
    def _():
        total = jnp.zeros((1, model), F32)
        for r in range(0, blk, strip):
            product = unit_all[r : r + strip].astype(F32) * dn_all[r : r + strip].astype(F32)
            total += jnp.sum(product, axis=0, keepdims=True)
        sums_ref[...] = jnp.zeros_like(sums_ref)
        sums_ref[12:16] = jnp.broadcast_to(total, (4, model))
        pltpu.make_async_copy(dh_all.at[pl.ds(0, blk)], dh_own_far, out_sems.at[0]).start()
        for copy in late[:3]:
            copy.wait()

    for b in range(count):

        @pl.when(block == b)
        def _():
            exps_copy(b).wait()

    slot = lax.rem(block, 2)
    first_query = starts_ref[block]
    dquery = []
    for h in range(heads):
        given = given_ref[h]
        for b in range(count):
            for a in range(blk // LANES):
                rows = slice(b * blk + a * LANES, b * blk + (a + 1) * LANES)
                dscores = exps_all[slot, h, rows].astype(F32) * dot_nt(v_ref[h, rows], given)
                ds_ref[h, rows] = dscores.astype(BF16)
                start = bias_lanes(seq, starts_ref[b] + a * LANES, first_query)
                acc_ref[h, :, pl.ds(start, blk)] += dscores
        dk_ref[h] += dot_nn(ds_ref[h], q_ref[h, now])
        dv_ref[h] += dot_nn(exps_all[slot, h], given)
        dquery.append(dot_nn(k_turned_ref[h], ds_ref[h]).T[:, :width])
    dj_ref[0, now] = jnp.concatenate(dquery, axis=1).astype(BF16)

    @pl.when(block == count - 1)
    def _():
        dj_ref[1] = jnp.concatenate([dk_ref[h][:, :width] for h in range(heads)], axis=1).astype(BF16)
        dj_ref[2] = jnp.concatenate([dv_ref[h][:, :width] for h in range(heads)], axis=1).astype(BF16)
        going = [pltpu.make_async_copy(dh_all.at[pl.ds(0, blk)], dh_own_far, out_sems.at[0])]

        def send_out(near, far):
            going.append(pltpu.make_async_copy(near, far, out_sems.at[len(going)]))
            going[-1].start()

        for copy in late[3:]:
            copy.wait()
        gain_total = jnp.zeros((1, model), F32)
        for b in range(count):
            rows = slice(b * blk, (b + 1) * blk)
            dnormed = dot_nn(dj_ref[0, rows], wq_ref[...])
            dnormed = dnormed + dot_nn(dj_ref[1, rows], wk_ref[...])
            dnormed = dnormed + dot_nn(dj_ref[2, rows], wv_ref[...])
            in_all[rows] = dnormed.astype(BF16)
            for r in range(0, blk, strip):
                values = tok_ref[b * blk + r : b * blk + r + strip].astype(F32)
                product = dnormed[r : r + strip] * (values * norm_rows(values))
                gain_total += jnp.sum(product, axis=0, keepdims=True)
        send_out(in_all.at[pl.ds(0, seq // 2)], in_low_far)
        send_out(in_all.at[pl.ds(seq // 2, seq // 2)], in_high_far)
        sums_ref[8:12] = jnp.broadcast_to(gain_total, (4, model))

        drel = []
        for h in range(heads):
            part = acc_ref[h]
            rows = LANES
            while rows > 1:
                rows //= 2
                part = part[:rows] + pltpu.roll(part[rows:], wide - rows, 1)
            drel.append(pltpu.roll(part, LANES - 1, 1))
        drel = jnp.concatenate(drel + [jnp.zeros((8 - heads, wide), F32)], axis=0)
        bucket = lax.broadcasted_iota(jnp.int32, (LANES, wide), 0)
        onehot = jnp.where(bucket == jnp.broadcast_to(buckets_ref[0:1], (LANES, wide)), 1.0, 0.0).astype(BF16)
        table = jnp.zeros((8, LANES), F32)
        for _ in range(3):
            coarse = drel.astype(BF16)
            table = table + dot_nt(jnp.concatenate((coarse, jnp.zeros_like(coarse)), axis=0), onehot)[:8]
            drel = drel - coarse.astype(F32)
        sums_ref[0:8, 0:LANES] = table
        halves[0, half_cols:] = split_small(sums_ref[...])
        send_out(halves.at[0, pl.ds(half_cols, 2 * SMALL)], small_far)
        side = side_ref[0]
        for k in range(2):

            @pl.when((side == 0) == (k == 1))
            def _():
                halves[k, :head_cols] = dot_tn(dj_ref[0], normed_ref[...]).astype(BF16)
                halves[k, head_cols:half_cols] = dot_tn(dj_ref[1], normed_ref[...]).astype(BF16)

            @pl.when((side == 0) == (k == 0))
            def _():
                halves[k, :head_cols] = dot_tn(dj_ref[2], normed_ref[...]).astype(BF16)
                halves[k, head_cols:half_cols] = dot_tn(ctx_all[...], dh_all[...]).astype(BF16)

            if k == 0:
                send_out(halves.at[0], send_far)
            else:
                send_out(halves.at[1, pl.ds(0, half_cols)], keep_far)
        for copy in going:
            copy.wait()


def attend_back(cost, bucket_count, side, starts, groups, own, gain, w_out, buckets, dn, unit, spread, joined, ctx, linv, exps, q, v, k_turned, normed, weights, tok):
    head_cols, model = w_out.shape
    count = starts.shape[0]
    heads, seq = exps.shape[:2]
    assert bucket_count <= LANES and heads <= 8
    blk = seq // count

    def whole(shape):
        return pl.BlockSpec(shape, lambda i, side: (0,) * len(shape))

    def room(value):
        return pltpu.VMEM(value.shape, value.dtype)

    first = [unit, spread, ctx, linv]
    late = [v, q, k_turned, normed, tok, *weights]
    smem = pl.BlockSpec(memory_space=pltpu.SMEM)
    anywhere = pl.BlockSpec(memory_space=pl.ANY)
    extra = 2 * SMALL
    outs = [(blk, model), (extra, model), (2 * head_cols + extra, model), (2 * head_cols, model), (seq // 2, model), (seq // 2, model)]
    return local_call(
        functools.partial(attend_back_kernel, heads, count),
        grid=(count,),
        in_specs=[smem, smem, smem, whole((2, model)), whole((8, 2 * seq))] + [anywhere] * (2 * count + 6 + len(late)),
        out_specs=[anywhere] * len(outs),
        out_shape=[FAR(shape, BF16) for shape in outs],
        scratch_shapes=[pltpu.VMEM((seq, model), BF16), pltpu.VMEM((seq, model), BF16)]
        + [room(a) for a in first]
        + [pltpu.VMEM((2, heads, seq, blk), BF16), room(w_out)]
        + [room(a) for a in late]
        + [
            pltpu.VMEM((heads, seq, LANES), F32),
            pltpu.VMEM((heads, seq, LANES), F32),
            pltpu.VMEM((heads, LANES, 2 * seq), F32),
            pltpu.VMEM((heads, seq, blk), BF16),
            pltpu.VMEM((heads, blk, LANES), BF16),
            pltpu.VMEM((seq, model), BF16),
            pltpu.VMEM((3, seq, head_cols), BF16),
            pltpu.VMEM((SMALL, model), F32),
            pltpu.VMEM((seq, model), BF16),
            pltpu.VMEM((2, 2 * head_cols + extra, model), BF16),
            pltpu.SemaphoreType.DMA((7 * count + 1 + len(late),)),
            pltpu.SemaphoreType.DMA((6,)),
        ],
        prefetch=1,
        mib=52,
        name="attend_back",
        cost=cost,
    )(side, starts, groups, own, gain, buckets, *dn, *joined, *first, exps, w_out, *late)


def shards(
    tokens,
    row_lengths,
    instruction_mask,
    task_groups,
    rel_buckets,
    gain_attn,
    w_query,
    w_key,
    w_value,
    rel_table,
    w_out,
    gain_ffn,
    w_in,
    w_back,
    out_grad,
):
    blk, model = tokens.shape[1:]
    count = lax.axis_size("tensor")
    head_cols = w_query.shape[1]
    bucket_count, heads = rel_table.shape
    width = head_cols // heads
    seq = blk * count
    half = count // 2
    bits = tensor_bits(count)
    here = lax.axis_index("tensor")
    starts = (here ^ jnp.array(block_order(count), jnp.int32)) * blk
    weights = (w_query.T, w_key.T, w_value.T)
    gains = jnp.stack((gain_attn, gain_ffn))
    own_row = lax.axis_index("dp")[None]
    turned = jnp.pad(rel_buckets[::-1], (0, 1), constant_values=-1)
    buckets = jnp.broadcast_to(turned[None], (8, 2 * seq))
    first_side = side_of(dp_steps(lax.axis_size("dp"))[0])

    positions = here * blk + jnp.arange(blk, dtype=jnp.int32)
    keep = (positions < row_lengths[0]) & (instruction_mask[0] == 0)
    masked_grad = jnp.where(keep[:, None], out_grad[0], 0).astype(BF16)

    turn = Turn()
    low_bits = bits[:-1]

    def across(pieces):
        while len(pieces) > 1:
            bit = low_bits[len(low_bits) - len(pieces).bit_length() + 1]
            near = len(pieces) // 2
            others = [swap_tensor(piece, bit) for piece in pieces[near:]]
            pieces = list(zip(pieces[:near], others, strict=True))
            if near > 1:
                pieces = [turn.done(add(a, turn(b))) for a, b in pieces]
        return pieces[0]

    own_tok = tokens[0]
    joined = jnp.concatenate((masked_grad, w_out))
    ready = (joined, starts, buckets, gains, own_row, rel_table)
    tok, ready = gather_tensor(own_tok, count, ready)
    joined, starts, buckets, both_gains, own_row, rel_table = ready
    joined = [joined]
    for bit in low_bits:
        joined = joined + [swap_tensor(piece, bit) for piece in joined]
    ctx, packed, exps, linv, normed, tok_all, q, v, k_turned = turn.done(
        attend(row_lengths, starts, rel_table, buckets, both_gains, *weights, tok)
    )
    contexts, _ = gather_tensor(packed, count)
    joined = [turn(piece) for piece in joined]
    joined = joined + [swap_tensor(piece, bits[-1]) for piece in joined]
    hidden, unit, spread, dn_low, dn_high, out_low, out_high, feed_send, feed_keep = turn.done(
        feed(first_side, task_groups, own_row, both_gains, w_in, w_back, tok_all, contexts, joined)
    )
    dn_came = swap_tensor(dn_high, bits[-1])
    out_came = swap_tensor(out_high, bits[-1])
    sum_feed = DpSum(turn, feed_send, feed_keep, finish_feed)
    assert half == 2 and len(low_bits) == 1
    flip = block_order(count).index(low_bits[0])
    got = {}

    def swap_dn(cost):
        got["dn"], sent = turn.done(add_swap(dn_low, turn(dn_came), half, flip, cost))
        got["dn_came"] = swap_tensor(sent, low_bits[0])

    def sum_dn(cost):
        got["dn"] = turn.done(add_pieces(got["dn"], turn(got["dn_came"]), half, cost))
        got["dn_far"] = [swap_tensor(piece, bits[-1]) for piece in got["dn"]]

    def back(cost):
        dn = [*got["dn"], *[turn(piece) for piece in got["dn_far"]]]
        results = attend_back(
            cost,
            bucket_count,
            first_side,
            starts,
            task_groups,
            own_row,
            both_gains,
            w_out,
            buckets,
            dn,
            unit,
            spread,
            joined,
            ctx,
            linv,
            exps,
            q,
            v,
            k_turned,
            normed,
            weights,
            tok_all,
        )
        got["dh"], small, send, keep, got["in_low"], in_high = turn.done(results)
        got["two"] = DpSum(turn, send, keep, finish_heads, small)
        got["in_came"] = swap_tensor(in_high, bits[-1])

    def swap_in(cost):
        own, other = turn.done(add_pieces(got["in_low"], turn(got["in_came"]), half, cost))
        got["in_own"], got["in_came"] = own, swap_tensor(other, low_bits[0])

    def end_tokens(cost):
        args = (both_gains, own_tok, got["in_own"], turn(got["in_came"]), got["dh"], cost)
        got["tokens"] = turn.done(finish_tokens(*args))[None]

    def swap_out(cost):
        got["out_own"], got["out_other"] = turn.done(add_pieces(out_low, turn(out_came), half, cost))

    def go_mixed(cost):
        got["out_came"] = swap_tensor(turn(got["out_other"]), low_bits[0])

    def end_mixed(cost):
        got["mixed"] = turn.done(finish_mixed(hidden, got["out_own"], turn(got["out_came"]), cost))[None]

    def start_gains():
        while got["two"].at < len(got["two"].pairs):
            got["two"].step()
        got["gains"] = got["two"].small[SMALL // 2 :]
        got["gains_came"] = swap_tensor(got["gains"], bits[-1])

    def gains_a(cost):
        got["gains"] = turn.done(add(got["gains"], turn(got["gains_came"]), cost))
        got["gains_came"] = swap_tensor(got["gains"], low_bits[0])

    def gains_b(cost):
        got["gains"] = turn.done(add(got["gains"], turn(got["gains_came"]), cost))

    stages = dict(
        swap_dn=swap_dn,
        sum_dn=sum_dn,
        back=back,
        swap_in=swap_in,
        end_tokens=end_tokens,
        swap_out=swap_out,
        go_mixed=go_mixed,
        end_mixed=end_mixed,
        gains_a=gains_a,
        gains_b=gains_b,
        end_heads=lambda cost: got["two"].rest(),
        end_feed=lambda cost: sum_feed.rest(),
    )
    for name in ORDER:
        cost = cost_of(name)
        if name in stages:
            stages[name](cost)
        elif name.startswith("feed"):
            sum_feed.step(cost)
        else:
            got["two"].step(cost)
            if name == "two3":
                start_gains()
    grad_query, grad_key, grad_value, grad_out = got["two"].result
    grad_back, grad_in = sum_feed.result
    return (
        got["mixed"],
        got["tokens"],
        got["gains"][0],
        grad_query.T,
        grad_key.T,
        grad_value.T,
        got["two"].small[:heads, :bucket_count].T,
        grad_out,
        got["gains"][4],
        grad_in,
        grad_back,
    )


def solution(mesh):
    return jax.shard_map(
        shards,
        mesh=mesh,
        in_specs=(
            P("dp", "tensor", None),
            P("dp"),
            P("dp", "tensor"),
            P(),
            P(),
            P(),
            P(None, "tensor"),
            P(None, "tensor"),
            P(None, "tensor"),
            P(None, "tensor"),
            P("tensor", None),
            P(),
            P(None, "tensor"),
            P("tensor", None),
            P("dp", "tensor", None),
        ),
        out_specs=(
            P("dp", "tensor", None),
            P("dp", "tensor", None),
            P(),
            P(None, "tensor"),
            P(None, "tensor"),
            P(None, "tensor"),
            P(None, "tensor"),
            P("tensor", None),
            P(),
            P(None, "tensor"),
            P("tensor", None),
        ),
        check_vma=False,
    )
```

```python
import functools

import jax
import jax.numpy as jnp
from jax import lax
from jax.experimental import pallas as pl
from jax.experimental.pallas import tpu as pltpu
from jax.sharding import PartitionSpec as P

NORM_EPS = 1e-06
MASK_FILL = -1000000000.0
F32 = jnp.float32
BF16 = jnp.bfloat16
LANES = 128
FREE = jax.ShapeDtypeStruct
FAR = pltpu.HBM
HEAVY = pl.CostEstimate(flops=10**11, bytes_accessed=1024, transcendentals=0)
LIGHT = pl.CostEstimate(flops=1024, bytes_accessed=1024, transcendentals=0)
ORDER = (
    "swap_dn", "out_part", "feed1", "swap_out", "sum_dn", "feed2", "back",
    "feed3", "swap_in", "two1", "feed4", "two2", "go_mixed",
    "feed5", "two3", "end_tokens", "gains_a", "two4", "end_mixed",
    "gains_b", "two5", "end_feed", "end_heads",
)
LONG = (
    "feed", "end_tokens", "feed3", "feed4", "two2",
)


def cost_of(name):
    return HEAVY if name in LONG else LIGHT
GELU_SCALE = 0.7978845608028654
GELU_CUBE = 0.044715


def dot_nn(left, right):
    return jnp.dot(left, right, preferred_element_type=F32)


def dot_nt(left, right):
    return lax.dot_general(left, right, (((1,), (1,)), ((), ())), preferred_element_type=F32)


def dot_tn(left, right):
    return lax.dot_general(left, right, (((0,), (0,)), ((), ())), preferred_element_type=F32)


def vmem_whole(shape):
    return pl.BlockSpec(shape, lambda i: (0,) * len(shape))


class Came:
    def __init__(self, array):
        self.array = array


def local_call(kernel, *, out_shape, grid, in_specs, out_specs, scratch_shapes=(), prefetch=0, mib, name, cost=LIGHT):
    def place(value, spec):
        if isinstance(value, Came):
            return value.array
        if value.ndim < 2 or spec.memory_space is pltpu.SMEM:
            return value
        return pltpu.with_memory_space_constraint(value, pltpu.HBM)

    def run(*args):
        given = [place(value, spec) for value, spec in zip(args[prefetch:], in_specs, strict=True)]
        return call(*args[:prefetch], *given)

    call = pl.pallas_call(
        kernel,
        grid_spec=pltpu.PrefetchScalarGridSpec(
            num_scalar_prefetch=prefetch,
            grid=grid,
            in_specs=in_specs,
            out_specs=out_specs,
            scratch_shapes=scratch_shapes,
        ),
        out_shape=out_shape,
        compiler_params=pltpu.CompilerParams(vmem_limit_bytes=mib << 20),
        cost_estimate=cost,
        name=name,
    )
    return run


class Turn:
    def __init__(self):
        self.last = None

    def __call__(self, value):
        if self.last is None:
            return value
        return lax.optimization_barrier((value, self.last))[0]

    def done(self, value):
        self.last = value[0] if isinstance(value, (list, tuple)) else value
        return value


def block_order(count):
    order = [0]
    bit = count // 2
    while bit:
        order = order + [slot | bit for slot in order]
        bit //= 2
    return order


def tensor_bits(count):
    bits = []
    bit = count // 2
    while bit:
        bits.append(bit)
        bit //= 2
    return bits


def swap_tensor(value, bit):
    size = lax.axis_size("tensor")
    return lax.ppermute(value, "tensor", [(i, i ^ bit) for i in range(size)])


def gather_tensor(value, count, ready=()):
    slots = [value]
    for bit in tensor_bits(count):
        came = [swap_tensor(piece, bit) for piece in slots]
        if ready:
            came, ready = lax.optimization_barrier((came, ready))
        slots = slots + came
    return slots, ready


def scatter_tensor(value, count, bits=None):
    for bit in reversed(tensor_bits(count) if bits is None else bits):
        half = value.shape[0] // 2
        came = swap_tensor(value[half:], bit)
        value = (value[:half].astype(F32) + came.astype(F32)).astype(BF16)
    return value


def dp_steps(count):
    bits = []
    bit = 1
    while bit < count:
        bits.append(bit)
        bit *= 2
    return list(zip(bits, bits[1::-1] + bits[2:], strict=True))


def swap_dp(value, pair):
    rows, cols = lax.axis_size("dp"), lax.axis_size("tensor")
    route = []
    for row in range(rows):
        for col in range(cols):
            route.append((row * cols + col, (row ^ pair[col % 2]) * cols + col))
    return lax.ppermute(value, ("dp", "tensor"), route)


def side_of(pair):
    row, col = lax.axis_index("dp"), lax.axis_index("tensor")
    bit = jnp.where(col % 2 == 1, pair[1], pair[0])
    return ((row & bit) != 0).astype(jnp.int32)[None]


def add_kernel(left_ref, right_ref, out_ref):
    total = left_ref[...].astype(F32) + right_ref[...].astype(F32)
    out_ref[...] = total.astype(out_ref.dtype)


def add(left, right, cost=LIGHT):
    return local_call(
        add_kernel,
        grid=(1,),
        in_specs=[vmem_whole(left.shape)] * 2,
        out_specs=vmem_whole(left.shape),
        out_shape=FAR(left.shape, left.dtype),
        mib=8,
        name="add",
        cost=cost,
    )(left, Came(right))


def add_pieces_kernel(count, *refs):
    step = pl.program_id(0)
    for k in range(count):

        @pl.when(step == k)
        def _():
            total = refs[0][...].astype(F32) + refs[1][...].astype(F32)
            refs[2 + k][...] = total.astype(BF16)


def add_pieces(left, right, count, cost=LIGHT):
    rows, cols = left.shape
    part = pl.BlockSpec((rows // count, cols), lambda i: (i, 0))
    return local_call(
        functools.partial(add_pieces_kernel, count),
        grid=(count,),
        in_specs=[part, part],
        out_specs=[vmem_whole((rows // count, cols))] * count,
        out_shape=[FAR((rows // count, cols), BF16)] * count,
        mib=10,
        name="add_pieces",
        cost=cost,
    )(left, Came(right))


def add_swap_kernel(left_ref, right_ref, plain_ref, swapped_ref):
    total = (left_ref[...].astype(F32) + right_ref[...].astype(F32)).astype(BF16)
    plain_ref[...] = total
    swapped_ref[...] = total


def add_swap(left, right, count, flip, cost=LIGHT):
    rows, cols = left.shape
    part = pl.BlockSpec((rows // count, cols), lambda i: (i, 0))
    return local_call(
        add_swap_kernel,
        grid=(count,),
        in_specs=[part, part],
        out_specs=[part, pl.BlockSpec((rows // count, cols), lambda i: (i ^ flip, 0))],
        out_shape=[FAR((rows, cols), BF16), FREE((rows, cols), BF16)],
        mib=10,
        name="add_swap",
        cost=cost,
    )(left, Came(right))


def fold_kernel(side_ref, kept_ref, came_ref, send_ref, keep_ref):
    total = (kept_ref[...].astype(F32) + came_ref[...].astype(F32)).astype(BF16)

    @pl.when(pl.program_id(0) == 0)
    def _():
        send_ref[...] = total

    @pl.when(pl.program_id(0) == 1)
    def _():
        keep_ref[...] = total


def fold(side, kept, came, cost=LIGHT):
    rows, cols = kept.shape
    half = rows // 2
    if half % 16:
        total = (kept.astype(F32) + came.astype(F32)).astype(BF16)
        return [lax.dynamic_slice_in_dim(total, k * half, half) for k in (1 - side[0], side[0])]
    place = pl.BlockSpec((half, cols), lambda i, side: (jnp.where(i == 0, 1 - side[0], side[0]), 0))
    whole = pl.BlockSpec((half, cols), lambda i, side: (0, 0))
    return local_call(
        fold_kernel,
        grid=(2,),
        in_specs=[place, place],
        out_specs=[whole, whole],
        out_shape=[FREE((half, cols), BF16), FAR((half, cols), BF16)],
        prefetch=1,
        mib=8,
        name="fold",
        cost=cost,
    )(side, kept, Came(came))


def join_kernel(steps, side_ref, own_ref, came_ref, out_ref):
    upper = pl.program_id(0) // steps
    mine = upper == side_ref[0]

    @pl.when(mine)
    def _():
        out_ref[...] = own_ref[...].astype(out_ref.dtype)

    @pl.when(jnp.logical_not(mine))
    def _():
        out_ref[...] = came_ref[...].astype(out_ref.dtype)


def join(side, own, came, cost=LIGHT):
    rows, cols = own.shape
    if rows % 16:
        mine = side[0] != 0
        pair = (jnp.where(mine, came, own), jnp.where(mine, own, came))
        return jnp.concatenate(pair)
    steps = 1
    part = rows // steps
    half = pl.BlockSpec((part, cols), lambda i, side: (i % steps, 0))
    return local_call(
        functools.partial(join_kernel, steps),
        grid=(2 * steps,),
        in_specs=[half, half],
        out_specs=pl.BlockSpec((part, cols), lambda i, side: (i, 0)),
        out_shape=FAR((2 * rows, cols), BF16),
        prefetch=1,
        mib=10,
        name="join",
        cost=cost,
    )(side, own, Came(came))


SMALL = 16


def split_small(value):
    coarse = value.astype(BF16)
    return jnp.concatenate((coarse, (value - coarse.astype(F32)).astype(BF16)), axis=0)


def read_small(rows):
    return rows[:SMALL].astype(F32) + rows[SMALL:].astype(F32)


def fold_small_kernel(side_ref, kept_ref, came_ref, small_came_ref, small_ref, send_ref, keep_ref, small_out_ref):
    total = (kept_ref[...].astype(F32) + came_ref[...].astype(F32)).astype(BF16)
    half = keep_ref.shape[0]

    @pl.when(pl.program_id(0) == 0)
    def _():
        small = split_small(read_small(small_ref) + read_small(small_came_ref))
        send_ref[:half] = total
        send_ref[half:] = small
        small_out_ref[...] = small

    @pl.when(pl.program_id(0) == 1)
    def _():
        keep_ref[...] = total


def fold_small(side, kept, came, small, cost=LIGHT):
    rows, cols = kept.shape
    half = rows // 2
    extra = 2 * SMALL
    if half % extra:
        send, keep = fold(side, kept, came[:rows])
        small = split_small(read_small(small) + read_small(came[rows:]))
        return jnp.concatenate((send, small)), keep, small
    place = pl.BlockSpec((half, cols), lambda i, side: (jnp.where(i == 0, 1 - side[0], side[0]), 0))

    def whole(count):
        return pl.BlockSpec((count, cols), lambda i, side: (0, 0))

    return local_call(
        fold_small_kernel,
        grid=(2,),
        in_specs=[place, place, pl.BlockSpec((extra, cols), lambda i, side: (rows // extra, 0)), whole(extra)],
        out_specs=[whole(half + extra), whole(half), whole(extra)],
        out_shape=[FREE((half + extra, cols), BF16), FAR((half, cols), BF16), FAR((extra, cols), BF16)],
        prefetch=1,
        mib=10,
        name="fold_small",
        cost=cost,
    )(side, kept, Came(came), Came(came), small)


def add_small_kernel(kept_ref, came_ref, small_ref, out_ref, small_out_ref):
    rows = kept_ref.shape[0]
    out_ref[...] = (kept_ref[...].astype(F32) + came_ref[:rows].astype(F32)).astype(BF16)
    small_out_ref[...] = read_small(small_ref) + read_small(came_ref[rows:])


def add_small(kept, came, small, cost=LIGHT):
    rows, cols = kept.shape
    if rows % (2 * SMALL):
        return add(kept, came[:rows]), read_small(small) + read_small(came[rows:])
    return local_call(
        add_small_kernel,
        grid=(1,),
        in_specs=[vmem_whole(kept.shape), vmem_whole(came.shape), vmem_whole(small.shape)],
        out_specs=[vmem_whole(kept.shape), vmem_whole((SMALL, cols))],
        out_shape=[FAR(kept.shape, BF16), FAR((SMALL, cols), F32)],
        mib=8,
        name="add_small",
        cost=cost,
    )(kept, Came(came), small)


class DpSum:
    def __init__(self, turn, send, keep, finish, small=None):
        self.turn, self.finish, self.small = turn, finish, small
        self.pairs = dp_steps(lax.axis_size("dp"))
        self.at = 0
        self.keep = keep
        self.came = swap_dp(send, self.pairs[0])

    def step(self, cost=LIGHT):
        turn, last = self.turn, len(self.pairs) - 1
        came = turn(self.came)
        if self.at < last:
            after = self.pairs[self.at + 1]
            if self.small is None:
                send, self.keep = turn.done(fold(side_of(after), self.keep, came, cost))
            else:
                results = turn.done(fold_small(side_of(after), self.keep, came, self.small, cost))
                send, self.keep, self.small = results
            self.came = swap_dp(send, after)
        elif self.at == last:
            if self.small is None:
                self.keep = turn.done(add(self.keep, came, cost))
            else:
                self.keep, self.small = turn.done(add_small(self.keep, came, self.small, cost))
            self.came = swap_dp(self.keep, self.pairs[last])
        else:
            place = 2 * last + 1 - self.at
            side = side_of(self.pairs[place])
            if place == 0:
                self.result = turn.done(self.finish(side, self.keep, came))
            else:
                self.keep = turn.done(join(side, self.keep, came, cost))
                self.came = swap_dp(self.keep, self.pairs[place - 1])
        self.at += 1

    def rest(self):
        while self.at < 2 * len(self.pairs):
            self.step()
        return self.result


def finish_feed_kernel(side_ref, own_ref, came_ref, back_ref, in_ref):
    step = pl.program_id(0)
    many = back_ref.shape[0]

    def put(source):
        back_ref[...] = source[:many].astype(F32)
        in_ref[...] = source[many:].astype(F32)

    @pl.when(step == side_ref[0])
    def _():
        put(own_ref)

    @pl.when(step != side_ref[0])
    def _():
        put(came_ref)


def finish_feed(side, own, came):
    rows, cols = own.shape
    whole = pl.BlockSpec((rows, cols), lambda i, side: (0, 0))
    return local_call(
        finish_feed_kernel,
        grid=(2,),
        in_specs=[whole, whole],
        out_specs=[pl.BlockSpec((rows // 2, cols), lambda i, side: (i, 0))] * 2,
        out_shape=[FREE((rows, cols), F32)] * 2,
        prefetch=1,
        mib=20,
        name="finish_feed",
    )(side, own, Came(came))


def finish_heads_kernel(side_ref, own_ref, came_ref, q_ref, k_ref, v_ref, out_ref):
    step = pl.program_id(0)
    cols = q_ref.shape[0]
    for half, refs in enumerate(((q_ref, k_ref), (v_ref, out_ref))):
        for source, is_own in ((own_ref, True), (came_ref, False)):

            @pl.when((step == half) & ((side_ref[0] == half) == is_own))
            def _():
                refs[0][...] = source[:cols].astype(F32)
                refs[1][...] = source[cols:].astype(F32)


def finish_heads(side, own, came):
    rows, cols = own.shape
    each = rows // 2
    whole = pl.BlockSpec((rows, cols), lambda i, side: (0, 0))
    return local_call(
        finish_heads_kernel,
        grid=(2,),
        in_specs=[whole, whole],
        out_specs=[pl.BlockSpec((each, cols), lambda i, side: (0, 0))] * 4,
        out_shape=[FREE((each, cols), F32)] * 4,
        prefetch=1,
        mib=12,
        name="finish_heads",
    )(side, own, Came(came))


def group_scale(groups_ref, own_ref):
    own = groups_ref[own_ref[0]]
    alike = jnp.int32(0)
    for row in range(groups_ref.shape[0]):
        alike += (groups_ref[row] == own).astype(jnp.int32)
    return lax.rsqrt(jnp.full((1, LANES), alike.astype(F32)))[:, 0:1]


def row_of(ref):
    return ref[...].reshape(1, ref.shape[0])


def norm_rows(values):
    return lax.rsqrt(jnp.mean(values * values, axis=-1, keepdims=True) + NORM_EPS)


def norm_back(dnormed, unit, spread, gain):
    scaled = gain * dnormed
    inner = jnp.mean(scaled * unit, axis=-1, keepdims=True)
    return spread * (scaled - unit * inner), dnormed * unit


def bias_lanes(seq, first_row, first_col):
    start = seq - LANES - first_row + first_col
    return pl.multiple_of(start, LANES)


def bias_kernel(table_ref, buckets_ref, bias_ref):
    which = buckets_ref[...]
    heads, _, wide = bias_ref.shape
    for h in range(heads):
        rel = jnp.zeros((8, wide), F32)
        for b in range(table_ref.shape[0]):
            rel = jnp.where(which == b, table_ref[b, h], rel)
        full = jnp.broadcast_to(rel[0:1], (LANES, wide))
        bias_ref[h] = pltpu.roll(full, wide - (LANES - 1), 1, stride=1, stride_axis=0)


def bias_tiles(table, buckets):
    shape = (table.shape[1], LANES, buckets.shape[1])
    return local_call(
        bias_kernel,
        grid=(1,),
        in_specs=[pl.BlockSpec(memory_space=pltpu.SMEM), vmem_whole(buckets.shape)],
        out_specs=vmem_whole(shape),
        out_shape=FAR(shape, F32),
        mib=16,
        name="bias_tiles",
        cost=HEAVY,
    )(table, buckets)


def attend_kernel(heads, count, length_ref, starts_ref, gain_ref, wq_ref, wk_ref, wv_ref, *refs):
    tok_refs, bias_far, refs = refs[:count], refs[count], refs[count + 1 :]
    (ctx_ref, packed_ref, exps_ref, linv_ref, normed_ref, tok_all_ref) = refs[:6]
    (q_ref, v_ref, k_turned_ref, k_ref, v_turned_ref, bias_ref, all_normed, scores_ref, sem) = refs[6:]
    step = pl.program_id(0)
    blk = ctx_ref.shape[0]
    seq = blk * count
    head_cols = wq_ref.shape[0]
    width = head_cols // heads

    @pl.when(step == 0)
    def _():
        bias_copy = pltpu.make_async_copy(bias_far, bias_ref, sem)
        bias_copy.start()
        lane = lax.broadcasted_iota(jnp.int32, (blk, LANES - width), 1)
        row = lax.broadcasted_iota(jnp.int32, (blk, LANES - width), 0)
        line = lax.broadcasted_iota(jnp.int32, (LANES - width, blk), 0)
        place = lax.broadcasted_iota(jnp.int32, (LANES - width, blk), 1)
        ones_q = jnp.where(lane == 0, 1.0, 0.0)
        ones_v = jnp.where(lane < 2, 1.0, 0.0)
        ones_turned = jnp.where(line < 2, 1.0, 0.0)
        for b in range(count):
            values = tok_refs[b][...].astype(F32)
            normed = (values * norm_rows(values) * row_of(gain_ref)).astype(BF16)
            rows = slice(b * blk, (b + 1) * blk)
            all_normed[rows] = normed
            used = length_ref[0] - starts_ref[b]
            fill = jnp.where((lane == 0) & (row >= used), MASK_FILL, 0.0)
            fill_turned = jnp.where((line == 0) & (place >= used), MASK_FILL, 0.0)
            query = dot_nt(normed, wq_ref[...])
            keys = dot_nt(normed, wk_ref[...])
            values = dot_nt(normed, wv_ref[...])
            keys_turned = dot_nt(wk_ref[...], normed)
            values_turned = dot_nt(wv_ref[...], normed)
            for h in range(heads):
                cols = slice(h * width, (h + 1) * width)
                q_ref[h, rows] = jnp.concatenate((query[:, cols], ones_q), axis=1).astype(BF16)
                k_ref[h, rows] = jnp.concatenate((keys[:, cols], fill), axis=1).astype(BF16)
                v_ref[h, rows] = jnp.concatenate((values[:, cols], ones_v), axis=1).astype(BF16)
                k_turned_ref[h, :, rows] = jnp.concatenate((keys_turned[cols], fill_turned), axis=0).astype(BF16)
                v_turned_ref[h, :, rows] = jnp.concatenate((values_turned[cols], ones_turned), axis=0).astype(BF16)
        bias_copy.wait()

    row0 = pl.multiple_of(step * blk, blk)
    first_query = starts_ref[step]
    normed_ref[...] = all_normed[pl.ds(row0, blk)]
    for b in range(count):

        @pl.when(step == b)
        def _():
            tok_all_ref[...] = tok_refs[b][...]

    outs = []
    linv = jnp.zeros((blk, LANES), F32)
    stat_lane = lax.broadcasted_iota(jnp.int32, (blk, LANES), 1)
    for h in range(heads):
        query = q_ref[h, pl.ds(row0, blk)]
        top = jnp.full((8, blk), -3.0e38, F32)
        for b in range(count):
            for a in range(blk // LANES):
                rows = slice(b * blk + a * LANES, b * blk + (a + 1) * LANES)
                start = bias_lanes(seq, starts_ref[b] + a * LANES, first_query)
                scores = dot_nt(k_ref[h, rows], query) + bias_ref[h, :, pl.ds(start, blk)]
                scores_ref[rows] = scores
                top = jnp.maximum(top, jnp.max(scores.reshape(LANES // 8, 8, blk), axis=0))
        top = jnp.max(top, axis=0, keepdims=True)
        for c in range(seq // LANES):
            rows = slice(c * LANES, (c + 1) * LANES)
            exps_ref[h, rows] = jnp.exp(scores_ref[rows] - top).astype(BF16)
        mixed = dot_nn(v_turned_ref[h], exps_ref[h]).T
        inverse = 1.0 / mixed[:, width : width + 1]
        outs.append(mixed[:, :width] * inverse)
        linv = jnp.where(stat_lane == h, inverse, linv)
    ctx = jnp.concatenate(outs, axis=1).astype(BF16)
    ctx_ref[...] = ctx
    linv_ref[...] = linv
    packed_ref[pl.ds(row0, blk)] = ctx[:, :LANES]
    rest = head_cols - LANES
    for k in range(count):

        @pl.when(step == k)
        def _():
            place = seq + (k % (count // 2)) * blk
            lanes = (k // (count // 2)) * rest
            packed_ref[place : place + blk, lanes : lanes + rest] = ctx[:, LANES:]


def attend(length, starts, bias, gain, w_query, w_key, w_value, tok):
    count = len(tok)
    blk, model = tok[0].shape
    seq = blk * count
    heads = bias.shape[0]
    head_cols = w_query.shape[0]
    smem = pl.BlockSpec(memory_space=pltpu.SMEM)
    assert 2 * (head_cols - LANES) == LANES
    return local_call(
        functools.partial(attend_kernel, heads, count),
        grid=(count,),
        in_specs=[smem, smem, vmem_whole((model,))]
        + [vmem_whole((head_cols, model))] * 3
        + [vmem_whole((blk, model))] * count
        + [pl.BlockSpec(memory_space=pl.ANY)],
        out_specs=[
            pl.BlockSpec((blk, head_cols), lambda i: (i, 0)),
            vmem_whole((seq * 3 // 2, LANES)),
            pl.BlockSpec((heads, seq, blk), lambda i: (0, 0, i)),
            pl.BlockSpec((blk, LANES), lambda i: (i, 0)),
            pl.BlockSpec((blk, model), lambda i: (i, 0)),
            pl.BlockSpec((blk, model), lambda i: (i, 0)),
            vmem_whole((heads, seq, LANES)),
            vmem_whole((heads, seq, LANES)),
            vmem_whole((heads, LANES, seq)),
        ],
        out_shape=[
            FAR((seq, head_cols), BF16),
            FAR((seq * 3 // 2, LANES), BF16),
            FAR((heads, seq, seq), BF16),
            FAR((seq, LANES), F32),
            FAR((seq, model), BF16),
            FAR((seq, model), BF16),
            FAR((heads, seq, LANES), BF16),
            FAR((heads, seq, LANES), BF16),
            FAR((heads, LANES, seq), BF16),
        ],
        scratch_shapes=[
            pltpu.VMEM((heads, seq, LANES), BF16),
            pltpu.VMEM((heads, LANES, seq), BF16),
            pltpu.VMEM((heads, LANES, 2 * seq), F32),
            pltpu.VMEM((seq, model), BF16),
            pltpu.VMEM((seq, blk), F32),
            pltpu.SemaphoreType.DMA,
        ],
        mib=28,
        name="attend",
        cost=HEAVY,
    )(length, starts, gain, w_query, w_key, w_value, *[Came(piece) for piece in tok], bias)


def feed_kernel(count, side_ref, groups_ref, own_ref, gain_ref, *refs):
    tok_far, ctx_far, refs = refs[0], refs[1 : 1 + count], refs[1 + count :]
    w_in_far, w_back_far, joined_far, refs = refs[0], refs[1], refs[2 : 2 + count], refs[2 + count :]
    hidden_ref, unit_ref, spread_ref, active_ref, dn_low_ref, dn_high_ref, send_far, keep_far = refs[:8]
    tok_all, ctx_all, w_in_ref, w_back_ref, w_out_ref, grad_all, normed_now, dup_all, active_turned = refs[8:17]
    normed_turned, hidden_now, halves, sems, out_sems = refs[17:]
    step = pl.program_id(0)
    blk = hidden_ref.shape[0]
    half = count // 2
    span = blk * half
    units, model = w_back_ref.shape
    rest = LANES // 2
    many, fewer = units // 2, model // 2
    used = 0

    def copy(far, near):
        nonlocal used
        used += 1
        return pltpu.make_async_copy(far, near, sems.at[used - 1])

    row_copies, out_copies, grad_copies = [], [], []
    for b in range(count):
        rows = pl.ds(b * blk, blk)
        found = [copy(tok_far.at[rows], tok_all.at[rows])]
        for k in range(count):
            c = b ^ k
            lanes = 2 * k * LANES
            found.append(copy(ctx_far[k].at[pl.ds(c * blk, blk)], ctx_all.at[rows, pl.ds(lanes, LANES)]))
            place = pl.ds(count * blk + (c % half) * blk, blk)
            found.append(copy(ctx_far[k].at[place], ctx_all.at[rows, pl.ds(lanes + LANES, LANES)]))
        row_copies.append(found)
        grad_copies.append(copy(joined_far[b].at[pl.ds(0, blk)], grad_all.at[rows]))
    for k in range(count):
        for part in range(2):
            top = 2 * k * LANES
            out_copies.append(copy(joined_far[k].at[pl.ds(blk, LANES)], w_out_ref.at[part, pl.ds(top, LANES)]))
            place = w_out_ref.at[part, pl.ds(top + LANES + (part ^ (k // half)) * rest, rest)]
            out_copies.append(copy(joined_far[k].at[pl.ds(blk + LANES, rest)], place))
    in_copy = copy(w_in_far, w_in_ref)
    back_copy = copy(w_back_far, w_back_ref)

    @pl.when(step == 0)
    def _():
        early = [one for b in range(half) for one in row_copies[b]]
        late = [one for b in range(half, count) for one in row_copies[b]]
        for one in [*out_copies, *early, in_copy, *grad_copies[:half], back_copy, *late, *grad_copies[half:]]:
            one.start()
        for part in range(2):
            for k in range(count):
                other = 2 * k * LANES + LANES + (1 - (part ^ (k // half))) * rest
                w_out_ref[part, other : other + rest] = jnp.zeros((rest, model), BF16)
        for one in out_copies:
            one.wait()

    for part in range(2):

        @pl.when(step == part)
        def _():
            for b in range(part * half, (part + 1) * half):
                for one in row_copies[b]:
                    one.wait()

    rows = pl.ds(pl.multiple_of(step * span, span), span)
    for b in range(half):
        there = pl.ds(pl.multiple_of(step * span + b * blk, blk), blk)
        hidden_now[b * blk : (b + 1) * blk] = tok_all[there].astype(F32) + dot_nn(ctx_all[there], w_out_ref[step])
    strip = 32 if blk % 32 == 0 else blk
    for r in range(0, span, strip):
        some = slice(r, r + strip)
        hidden = hidden_now[some]
        spread = norm_rows(hidden)
        unit = hidden * spread
        unit_ref[some] = unit.astype(BF16)
        spread_ref[some] = jnp.broadcast_to(spread, (strip, LANES))
        normed_now[some] = (unit * row_of(gain_ref)).astype(BF16)
    normed = normed_now[...]
    normed_turned[:, rows] = normed.T

    @pl.when(step == 0)
    def _():
        hidden_ref[...] = hidden_now[0:blk]
        in_copy.wait()
        back_copy.wait()

    for part in range(2):

        @pl.when(step == part)
        def _():
            for b in range(part * half, (part + 1) * half):
                grad_copies[b].wait()

    grad = grad_all[rows]
    scale = group_scale(groups_ref, own_ref)
    part = 256 if units % 256 == 0 else units
    for b in range(0, span, 256):
        near = slice(b, b + 256)
        there = pl.ds(pl.multiple_of(step * span + b, 256), 256)
        for c in range(0, units, part):
            cols = slice(c, c + part)
            up = dot_nn(normed[near], w_in_ref[:, cols])
            dactive = dot_nt(grad[near], w_back_ref[cols])
            square = up * up
            bend = jnp.tanh(up * (GELU_SCALE + GELU_SCALE * GELU_CUBE * square))
            bell = 0.5 + 0.5 * bend
            active = (up * bell).astype(BF16)
            steep = GELU_SCALE + 3.0 * GELU_SCALE * GELU_CUBE * square
            slope = (bell + (0.5 * up) * (1.0 - bend * bend) * steep) * scale
            active_ref[near, cols] = active
            active_turned[cols, there] = active.T
            dup_all[there, cols] = (dactive * slope).astype(BF16)

    def put(dn_ref):
        for b in range(0, span, 256):
            near = slice(b, b + 256)
            there = pl.ds(pl.multiple_of(step * span + b, 256), 256)
            dn_ref[near] = dot_nt(dup_all[there], w_in_ref[...]).astype(BF16)

    @pl.when(step == 0)
    def _():
        put(dn_low_ref)

    @pl.when(step == 1)
    def _():
        put(dn_high_ref)
        going = []
        for k, (far, side) in enumerate(((send_far, 1 - side_ref[0]), (keep_far, side_ref[0]))):
            back = dot_nn(active_turned[pl.ds(side * many, many)], grad_all[...]) * scale
            halves[k, :many] = back.astype(BF16)
            halves[k, many:] = dot_nn(normed_turned[pl.ds(side * fewer, fewer)], dup_all[...]).astype(BF16)
            going.append(pltpu.make_async_copy(halves.at[k], far, out_sems.at[k]))
            going[-1].start()
        for one in going:
            one.wait()


def feed(side, groups, own, gain, w_in, w_back, tok, ctx, joined):
    count = len(ctx)
    rows, model = tok.shape
    blk = rows // count
    units = w_in.shape[1]
    span = rows // 2
    by_row = pl.BlockSpec((span, model), lambda i, side: (i, 0))
    anywhere = pl.BlockSpec(memory_space=pl.ANY)
    smem = pl.BlockSpec(memory_space=pltpu.SMEM)

    def whole(shape):
        return pl.BlockSpec(shape, lambda i, side: (0, 0))

    grads = ((units + model) // 2, model)
    copies = count * (4 + 2 * count) + 2 + 2 * count
    return local_call(
        functools.partial(feed_kernel, count),
        grid=(2,),
        in_specs=[smem, smem, pl.BlockSpec((model,), lambda i, side: (0,))] + [anywhere] * (3 + 2 * count),
        out_specs=[
            whole((blk, model)),
            by_row,
            pl.BlockSpec((span, LANES), lambda i, side: (i, 0)),
            pl.BlockSpec((span, units), lambda i, side: (i, 0)),
            *[whole((span, model))] * 2,
            anywhere,
            anywhere,
        ],
        out_shape=[FAR((blk, model), F32), FAR((rows, model), BF16), FAR((rows, LANES), F32), FAR((rows, units), BF16)]
        + [FAR((span, model), BF16)] * 2
        + [FAR(grads, BF16)] * 2,
        scratch_shapes=[
            pltpu.VMEM((rows, model), BF16),
            pltpu.VMEM((rows, 2 * count * LANES), BF16),
            pltpu.VMEM((model, units), BF16),
            pltpu.VMEM((units, model), BF16),
            pltpu.VMEM((2, 2 * count * LANES, model), BF16),
            pltpu.VMEM((rows, model), BF16),
            pltpu.VMEM((span, model), BF16),
            pltpu.VMEM((rows, units), BF16),
            pltpu.VMEM((units, rows), BF16),
            pltpu.VMEM((model, rows), BF16),
            pltpu.VMEM((span, model), F32),
            pltpu.VMEM((2, *grads), BF16),
            pltpu.SemaphoreType.DMA((copies,)),
            pltpu.SemaphoreType.DMA((2,)),
        ],
        prefetch=1,
        mib=52,
        name="feed",
        cost=cost_of("feed"),
    )(side, groups, own, gain, tok, ctx[0], *[Came(a) for a in ctx[1:]], w_in, w_back, *joined)


def feed_out_kernel(active_ref, w_back_ref, *out_refs):
    for k, ref in enumerate(out_refs):

        @pl.when(pl.program_id(0) == k)
        def _():
            ref[...] = dot_nn(active_ref[...], w_back_ref[...]).astype(BF16)


def feed_out(active, w_back, count, cost):
    rows, units = active.shape
    model = w_back.shape[1]
    blk = rows // count
    return local_call(
        feed_out_kernel,
        grid=(count,),
        in_specs=[pl.BlockSpec((blk, units), lambda i: (i, 0)), vmem_whole(w_back.shape)],
        out_specs=[vmem_whole((blk, model))] * count,
        out_shape=[FAR((blk, model), BF16)] * count,
        mib=16,
        name="feed_out",
        cost=cost,
    )(active, w_back)


def finish_mixed_kernel(hidden_ref, own_ref, came_ref, out_ref):
    total = own_ref[...].astype(F32) + came_ref[...].astype(F32)
    out_ref[...] = (hidden_ref[...] + total).astype(BF16)


def finish_mixed(hidden, own, came, cost=LIGHT):
    blk, model = own.shape
    place = pl.BlockSpec((blk, model), lambda i: (0, 0))
    return local_call(
        finish_mixed_kernel,
        grid=(1,),
        in_specs=[place] * 3,
        out_specs=place,
        out_shape=jax.ShapeDtypeStruct((blk, model), BF16),
        mib=10,
        name="finish_mixed",
        cost=cost,
    )(hidden, own, Came(came))


def finish_tokens_kernel(gain_ref, tok_ref, own_ref, came_ref, dh_ref, out_ref):
    dnormed = own_ref[...].astype(F32) + came_ref[...].astype(F32)
    values = tok_ref[...].astype(F32)
    spread = norm_rows(values)
    out_ref[...] = dh_ref[...].astype(F32) + norm_back(dnormed, values * spread, spread, row_of(gain_ref))[0]


def finish_tokens(gain, tok, own, came, dh_own, cost=LIGHT):
    blk, model = own.shape
    steps = 2 if blk % 32 == 0 else 1
    place = pl.BlockSpec((blk // steps, model), lambda i: (i, 0))
    return local_call(
        finish_tokens_kernel,
        grid=(steps,),
        in_specs=[vmem_whole((model,))] + [place] * 4,
        out_specs=place,
        out_shape=jax.ShapeDtypeStruct((blk, model), F32),
        mib=10,
        name="finish_tokens",
        cost=cost,
    )(gain, tok, own, Came(came), dh_own)


def attend_back_kernel(heads, count, side_ref, starts_ref, groups_ref, own_ref, gain_ref, buckets_ref, *refs):
    dn_far, joined_far, refs = refs[:count], refs[count : 2 * count], refs[2 * count :]
    unit_far, spread_far, ctx_far, linv_far, exps_far, w_out_far, refs = *refs[:6], refs[6:]
    late_far, refs = refs[:8], refs[8:]
    dh_own_far, small_far, send_far, keep_far, in_low_far, in_high_far, refs = *refs[:6], refs[6:]
    dn_all, grad_all, unit_all, spread_all, ctx_all, linv_all, exps_all, w_out_ref, refs = *refs[:8], refs[8:]
    late_near, refs = refs[:8], refs[8:]
    v_ref, q_ref, k_turned_ref, normed_ref, tok_ref, wq_ref, wk_ref, wv_ref = late_near
    dk_ref, dv_ref, acc_ref, ds_ref, given_ref, dh_all, dj_ref, sums_ref, in_all, halves, sems, out_sems = refs
    block = pl.program_id(0)
    seq, model = dh_all.shape
    blk = seq // count
    head_cols = ctx_all.shape[1]
    width = head_cols // heads
    wide = acc_ref.shape[2]
    half_cols = 2 * head_cols
    strip = 32 if blk % 32 == 0 else blk

    def first_copies(b):
        rows = pl.ds(b * blk, blk)
        pairs = [
            (dn_far[b], dn_all.at[rows]),
            (unit_far.at[rows], unit_all.at[rows]),
            (spread_far.at[rows], spread_all.at[rows]),
            (joined_far[b].at[pl.ds(0, blk)], grad_all.at[rows]),
            (ctx_far.at[rows], ctx_all.at[rows]),
            (linv_far.at[rows], linv_all.at[rows]),
        ]
        return [pltpu.make_async_copy(far, near, sems.at[7 * b + k]) for k, (far, near) in enumerate(pairs)]

    def exps_copy(b):
        cols = pl.ds(b * blk, blk)
        return pltpu.make_async_copy(exps_far.at[:, :, cols], exps_all.at[b % 2], sems.at[7 * b + 6])

    out_copy = pltpu.make_async_copy(w_out_far, w_out_ref, sems.at[7 * count])
    late = [pltpu.make_async_copy(late_far[k], late_near[k], sems.at[7 * count + 1 + k]) for k in range(8)]

    @pl.when(block == 0)
    def _():
        for copy in [*first_copies(0), out_copy, late[0], exps_copy(0), late[1], late[2], *first_copies(1)]:
            copy.start()
        dk_ref[...] = jnp.zeros_like(dk_ref)
        dv_ref[...] = jnp.zeros_like(dv_ref)
        acc_ref[...] = jnp.zeros_like(acc_ref)

    for b in range(count):

        @pl.when(block == b)
        def _():
            if b + 1 < count:
                exps_copy(b + 1).start()
            if b == 0:
                for k in range(2, count):
                    for copy in first_copies(k):
                        copy.start()
                for copy in late[3:]:
                    copy.start()
            for copy in first_copies(b):
                copy.wait()
            if b == 0:
                out_copy.wait()

    row0 = pl.multiple_of(block * blk, blk)
    now = pl.ds(row0, blk)
    scale = group_scale(groups_ref, own_ref)
    for r in range(0, blk, strip):
        there = pl.ds(pl.multiple_of(row0 + r, strip), strip)
        unit = unit_all[there].astype(F32)
        scaled = row_of(gain_ref) * dn_all[there].astype(F32)
        inner = jnp.mean(scaled * unit, axis=-1, keepdims=True)
        dhidden = spread_all[there, 0:1] * (scaled - unit * inner)
        dh_all[there] = (dhidden + grad_all[there].astype(F32) * scale).astype(BF16)

    dctx = dot_nt(dh_all[now], w_out_ref[...])
    product = dctx * ctx_all[now].astype(F32)
    lane = lax.broadcasted_iota(jnp.int32, (blk, LANES - width), 1)
    for h in range(heads):
        cols = slice(h * width, (h + 1) * width)
        inverse = linv_all[now, h : h + 1]
        inner = -jnp.sum(product[:, cols], axis=1, keepdims=True) * inverse
        coarse = inner.astype(BF16).astype(F32)
        extra = jnp.where(lane == 0, coarse, jnp.where(lane == 1, inner - coarse, 0.0))
        given_ref[h] = jnp.concatenate((dctx[:, cols] * inverse, extra), axis=1).astype(BF16)

    @pl.when(block == 0)
    def _():
        total = jnp.zeros((1, model), F32)
        for r in range(0, blk, strip):
            product = unit_all[r : r + strip].astype(F32) * dn_all[r : r + strip].astype(F32)
            total += jnp.sum(product, axis=0, keepdims=True)
        sums_ref[...] = jnp.zeros_like(sums_ref)
        sums_ref[12:16] = jnp.broadcast_to(total, (4, model))
        pltpu.make_async_copy(dh_all.at[pl.ds(0, blk)], dh_own_far, out_sems.at[0]).start()
        for copy in late[:3]:
            copy.wait()

    for b in range(count):

        @pl.when(block == b)
        def _():
            exps_copy(b).wait()

    slot = lax.rem(block, 2)
    first_query = starts_ref[block]
    dquery = []
    for h in range(heads):
        given = given_ref[h]
        for b in range(count):
            for a in range(blk // LANES):
                rows = slice(b * blk + a * LANES, b * blk + (a + 1) * LANES)
                dscores = exps_all[slot, h, rows].astype(F32) * dot_nt(v_ref[h, rows], given)
                ds_ref[h, rows] = dscores.astype(BF16)
                start = bias_lanes(seq, starts_ref[b] + a * LANES, first_query)
                acc_ref[h, :, pl.ds(start, blk)] += dscores
        dk_ref[h] += dot_nn(ds_ref[h], q_ref[h, now])
        dv_ref[h] += dot_nn(exps_all[slot, h], given)
        dquery.append(dot_nn(k_turned_ref[h], ds_ref[h]).T[:, :width])
    dj_ref[0, now] = jnp.concatenate(dquery, axis=1).astype(BF16)

    @pl.when(block == count - 1)
    def _():
        dj_ref[1] = jnp.concatenate([dk_ref[h][:, :width] for h in range(heads)], axis=1).astype(BF16)
        dj_ref[2] = jnp.concatenate([dv_ref[h][:, :width] for h in range(heads)], axis=1).astype(BF16)
        going = [pltpu.make_async_copy(dh_all.at[pl.ds(0, blk)], dh_own_far, out_sems.at[0])]

        def send_out(near, far):
            going.append(pltpu.make_async_copy(near, far, out_sems.at[len(going)]))
            going[-1].start()

        for copy in late[3:]:
            copy.wait()
        gain_total = jnp.zeros((1, model), F32)
        for b in range(count):
            rows = slice(b * blk, (b + 1) * blk)
            dnormed = dot_nn(dj_ref[0, rows], wq_ref[...])
            dnormed = dnormed + dot_nn(dj_ref[1, rows], wk_ref[...])
            dnormed = dnormed + dot_nn(dj_ref[2, rows], wv_ref[...])
            in_all[rows] = dnormed.astype(BF16)
            for r in range(0, blk, strip):
                values = tok_ref[b * blk + r : b * blk + r + strip].astype(F32)
                product = dnormed[r : r + strip] * (values * norm_rows(values))
                gain_total += jnp.sum(product, axis=0, keepdims=True)
        send_out(in_all.at[pl.ds(0, seq // 2)], in_low_far)
        send_out(in_all.at[pl.ds(seq // 2, seq // 2)], in_high_far)
        sums_ref[8:12] = jnp.broadcast_to(gain_total, (4, model))

        drel = []
        for h in range(heads):
            part = acc_ref[h]
            rows = LANES
            while rows > 1:
                rows //= 2
                part = part[:rows] + pltpu.roll(part[rows:], wide - rows, 1)
            drel.append(pltpu.roll(part, LANES - 1, 1))
        drel = jnp.concatenate(drel + [jnp.zeros((8 - heads, wide), F32)], axis=0)
        bucket = lax.broadcasted_iota(jnp.int32, (LANES, wide), 0)
        onehot = jnp.where(bucket == jnp.broadcast_to(buckets_ref[0:1], (LANES, wide)), 1.0, 0.0).astype(BF16)
        table = jnp.zeros((8, LANES), F32)
        for _ in range(3):
            coarse = drel.astype(BF16)
            table = table + dot_nt(jnp.concatenate((coarse, jnp.zeros_like(coarse)), axis=0), onehot)[:8]
            drel = drel - coarse.astype(F32)
        sums_ref[0:8, 0:LANES] = table
        halves[0, half_cols:] = split_small(sums_ref[...])
        send_out(halves.at[0, pl.ds(half_cols, 2 * SMALL)], small_far)
        side = side_ref[0]
        for k in range(2):

            @pl.when((side == 0) == (k == 1))
            def _():
                halves[k, :head_cols] = dot_tn(dj_ref[0], normed_ref[...]).astype(BF16)
                halves[k, head_cols:half_cols] = dot_tn(dj_ref[1], normed_ref[...]).astype(BF16)

            @pl.when((side == 0) == (k == 0))
            def _():
                halves[k, :head_cols] = dot_tn(dj_ref[2], normed_ref[...]).astype(BF16)
                halves[k, head_cols:half_cols] = dot_tn(ctx_all[...], dh_all[...]).astype(BF16)

            if k == 0:
                send_out(halves.at[0], send_far)
            else:
                send_out(halves.at[1, pl.ds(0, half_cols)], keep_far)
        for copy in going:
            copy.wait()


def attend_back(cost, bucket_count, side, starts, groups, own, gain, w_out, buckets, dn, unit, spread, joined, ctx, linv, exps, q, v, k_turned, normed, weights, tok):
    head_cols, model = w_out.shape
    count = starts.shape[0]
    heads, seq = exps.shape[:2]
    assert bucket_count <= LANES and heads <= 8
    blk = seq // count

    def whole(shape):
        return pl.BlockSpec(shape, lambda i, side: (0,) * len(shape))

    def room(value):
        return pltpu.VMEM(value.shape, value.dtype)

    first = [unit, spread, ctx, linv]
    late = [v, q, k_turned, normed, tok, *weights]
    smem = pl.BlockSpec(memory_space=pltpu.SMEM)
    anywhere = pl.BlockSpec(memory_space=pl.ANY)
    extra = 2 * SMALL
    outs = [(blk, model), (extra, model), (2 * head_cols + extra, model), (2 * head_cols, model), (seq // 2, model), (seq // 2, model)]
    return local_call(
        functools.partial(attend_back_kernel, heads, count),
        grid=(count,),
        in_specs=[smem, smem, smem, whole((model,)), whole((8, 2 * seq))] + [anywhere] * (2 * count + 6 + len(late)),
        out_specs=[anywhere] * len(outs),
        out_shape=[FAR(shape, BF16) for shape in outs],
        scratch_shapes=[pltpu.VMEM((seq, model), BF16), pltpu.VMEM((seq, model), BF16)]
        + [room(a) for a in first]
        + [pltpu.VMEM((2, heads, seq, blk), BF16), room(w_out)]
        + [room(a) for a in late]
        + [
            pltpu.VMEM((heads, seq, LANES), F32),
            pltpu.VMEM((heads, seq, LANES), F32),
            pltpu.VMEM((heads, LANES, 2 * seq), F32),
            pltpu.VMEM((heads, seq, blk), BF16),
            pltpu.VMEM((heads, blk, LANES), BF16),
            pltpu.VMEM((seq, model), BF16),
            pltpu.VMEM((3, seq, head_cols), BF16),
            pltpu.VMEM((SMALL, model), F32),
            pltpu.VMEM((seq, model), BF16),
            pltpu.VMEM((2, 2 * head_cols + extra, model), BF16),
            pltpu.SemaphoreType.DMA((7 * count + 1 + len(late),)),
            pltpu.SemaphoreType.DMA((6,)),
        ],
        prefetch=1,
        mib=52,
        name="attend_back",
        cost=cost,
    )(side, starts, groups, own, gain, buckets, *[Came(a) for a in dn], *joined, *first, exps, w_out, *late)


def shards(
    tokens,
    row_lengths,
    instruction_mask,
    task_groups,
    rel_buckets,
    gain_attn,
    w_query,
    w_key,
    w_value,
    rel_table,
    w_out,
    gain_ffn,
    w_in,
    w_back,
    out_grad,
):
    blk, model = tokens.shape[1:]
    count = lax.axis_size("tensor")
    head_cols = w_query.shape[1]
    bucket_count, heads = rel_table.shape
    width = head_cols // heads
    seq = blk * count
    half = count // 2
    bits = tensor_bits(count)
    here = lax.axis_index("tensor")
    starts = (here ^ jnp.array(block_order(count), jnp.int32)) * blk
    weights = (w_query.T, w_key.T, w_value.T)
    own_row = lax.axis_index("dp")[None]
    turned = jnp.pad(rel_buckets[::-1], (0, 1), constant_values=-1)
    buckets = jnp.broadcast_to(turned[None], (8, 2 * seq))
    first_side = side_of(dp_steps(lax.axis_size("dp"))[0])

    positions = here * blk + jnp.arange(blk, dtype=jnp.int32)
    keep = (positions < row_lengths[0]) & (instruction_mask[0] == 0)
    masked_grad = jnp.where(keep[:, None], out_grad[0], 0).astype(BF16)

    turn = Turn()
    low_bits = bits[:-1]

    def across(pieces):
        while len(pieces) > 1:
            bit = low_bits[len(low_bits) - len(pieces).bit_length() + 1]
            near = len(pieces) // 2
            others = [swap_tensor(piece, bit) for piece in pieces[near:]]
            pieces = list(zip(pieces[:near], others, strict=True))
            if near > 1:
                pieces = [turn.done(add(a, turn(b))) for a, b in pieces]
        return pieces[0]

    own_tok = tokens[0]
    joined = jnp.concatenate((masked_grad, w_out))
    bias = bias_tiles(rel_table, buckets)
    ready = (joined, starts, own_row, bias)
    assert count == 4
    far_tok = swap_tensor(own_tok, 2)
    near_tok = swap_tensor(own_tok, 1)
    far_tok, ready = lax.optimization_barrier((far_tok, ready))
    joined, starts, own_row, bias = ready
    tok = [own_tok, far_tok, near_tok, swap_tensor(far_tok, 1)]
    joined = [joined, swap_tensor(joined, 2)]
    ctx, packed, exps, linv, normed, tok_all, q, v, k_turned = turn.done(
        attend(row_lengths, starts, bias, gain_attn, *weights, tok)
    )
    contexts, _ = gather_tensor(packed, count)
    joined = [turn(piece) for piece in joined]
    joined = joined + [swap_tensor(piece, bits[-1]) for piece in joined]
    hidden, unit, spread, active, dn_low, dn_high, feed_send, feed_keep = turn.done(
        feed(first_side, task_groups, own_row, gain_ffn, w_in, w_back, tok_all, contexts, joined)
    )
    dn_came = swap_tensor(dn_high, bits[-1])
    sum_feed = DpSum(turn, feed_send, feed_keep, finish_feed)
    assert half == 2 and len(low_bits) == 1
    flip = block_order(count).index(low_bits[0])
    got = {}

    def swap_dn(cost):
        got["dn"], sent = turn.done(add_swap(dn_low, turn(dn_came), half, flip, cost))
        got["dn_came"] = swap_tensor(sent, low_bits[0])

    def sum_dn(cost):
        got["dn"] = turn.done(add_pieces(got["dn"], turn(got["dn_came"]), half, cost))
        got["dn_far"] = [swap_tensor(piece, bits[-1]) for piece in got["dn"]]

    def back(cost):
        dn = [*got["dn"], *[turn(piece) for piece in got["dn_far"]]]
        results = attend_back(
            cost,
            bucket_count,
            first_side,
            starts,
            task_groups,
            own_row,
            gain_ffn,
            w_out,
            buckets,
            dn,
            unit,
            spread,
            joined,
            ctx,
            linv,
            exps,
            q,
            v,
            k_turned,
            normed,
            weights,
            tok_all,
        )
        got["dh"], small, send, keep, got["in_low"], in_high = turn.done(results)
        got["two"] = DpSum(turn, send, keep, finish_heads, small)
        got["in_came"] = swap_tensor(in_high, bits[-1])

    def swap_in(cost):
        own, other = turn.done(add_pieces(got["in_low"], turn(got["in_came"]), half, cost))
        got["in_own"], got["in_came"] = own, swap_tensor(other, low_bits[0])

    def end_tokens(cost):
        args = (gain_attn, own_tok, got["in_own"], turn(got["in_came"]), got["dh"], cost)
        got["tokens"] = turn.done(finish_tokens(*args))[None]

    def out_part(cost):
        parts = turn.done(feed_out(turn(active), w_back, count, cost))
        got["out_low"] = parts[:half]
        got["out_came"] = [swap_tensor(part, bits[-1]) for part in parts[half:]]

    def swap_out(cost):
        pairs = zip(got["out_low"], got["out_came"], strict=True)
        got["out_own"], got["out_other"] = [turn.done(add(own, turn(came), cost)) for own, came in pairs]

    def go_mixed(cost):
        got["out_came"] = swap_tensor(turn(got["out_other"]), low_bits[0])

    def end_mixed(cost):
        got["mixed"] = turn.done(finish_mixed(hidden, got["out_own"], turn(got["out_came"]), cost))[None]

    def start_gains():
        while got["two"].at < len(got["two"].pairs):
            got["two"].step()
        got["gains"] = got["two"].small[SMALL // 2 :]
        got["gains_came"] = swap_tensor(got["gains"], bits[-1])

    def gains_a(cost):
        got["gains"] = turn.done(add(got["gains"], turn(got["gains_came"]), cost))
        got["gains_came"] = swap_tensor(got["gains"], low_bits[0])

    def gains_b(cost):
        got["gains"] = turn.done(add(got["gains"], turn(got["gains_came"]), cost))

    stages = dict(
        swap_dn=swap_dn,
        sum_dn=sum_dn,
        back=back,
        swap_in=swap_in,
        end_tokens=end_tokens,
        out_part=out_part,
        swap_out=swap_out,
        go_mixed=go_mixed,
        end_mixed=end_mixed,
        gains_a=gains_a,
        gains_b=gains_b,
        end_heads=lambda cost: got["two"].rest(),
        end_feed=lambda cost: sum_feed.rest(),
    )
    for name in ORDER:
        cost = cost_of(name)
        if name in stages:
            stages[name](cost)
        elif name.startswith("feed"):
            sum_feed.step(cost)
        else:
            got["two"].step(cost)
            if name == "two3":
                start_gains()
    grad_query, grad_key, grad_value, grad_out = got["two"].result
    grad_back, grad_in = sum_feed.result
    return (
        got["mixed"],
        got["tokens"],
        got["gains"][0],
        grad_query.T,
        grad_key.T,
        grad_value.T,
        got["two"].small[:heads, :bucket_count].T,
        grad_out,
        got["gains"][4],
        grad_in,
        grad_back,
    )


def solution(mesh):
    return jax.shard_map(
        shards,
        mesh=mesh,
        in_specs=(
            P("dp", "tensor", None),
            P("dp"),
            P("dp", "tensor"),
            P(),
            P(),
            P(),
            P(None, "tensor"),
            P(None, "tensor"),
            P(None, "tensor"),
            P(None, "tensor"),
            P("tensor", None),
            P(),
            P(None, "tensor"),
            P("tensor", None),
            P("dp", "tensor", None),
        ),
        out_specs=(
            P("dp", "tensor", None),
            P("dp", "tensor", None),
            P(),
            P(None, "tensor"),
            P(None, "tensor"),
            P(None, "tensor"),
            P(None, "tensor"),
            P("tensor", None),
            P(),
            P(None, "tensor"),
            P("tensor", None),
        ),
        check_vma=False,
    )
```

```python
import functools

import jax
import jax.numpy as jnp
from jax import lax
from jax.experimental import pallas as pl
from jax.experimental.pallas import tpu as pltpu
from jax.sharding import PartitionSpec as P

NORM_EPS = 1e-06
MASK_FILL = -1000000000.0
F32 = jnp.float32
BF16 = jnp.bfloat16
LANES = 128
FREE = jax.ShapeDtypeStruct
FAR = pltpu.HBM
HEAVY = pl.CostEstimate(flops=10**11, bytes_accessed=1024, transcendentals=0)
LIGHT = pl.CostEstimate(flops=1024, bytes_accessed=1024, transcendentals=0)
ORDER = (
    "swap_dn", "out_part", "feed1", "swap_out", "sum_dn", "feed2", "back",
    "feed3", "swap_in", "two1", "feed4", "two2", "go_mixed",
    "feed5", "two3", "end_tokens", "gains_a", "two4", "end_mixed",
    "gains_b", "two5", "end_feed", "end_heads",
)
LONG = (
    "feed", "end_tokens", "feed3", "feed4", "two2",
)


def cost_of(name):
    return HEAVY if name in LONG else LIGHT
GELU_SCALE = 0.7978845608028654
GELU_CUBE = 0.044715


def dot_nn(left, right):
    return jnp.dot(left, right, preferred_element_type=F32)


def dot_nt(left, right):
    return lax.dot_general(left, right, (((1,), (1,)), ((), ())), preferred_element_type=F32)


def dot_tn(left, right):
    return lax.dot_general(left, right, (((0,), (0,)), ((), ())), preferred_element_type=F32)


def vmem_whole(shape):
    return pl.BlockSpec(shape, lambda i: (0,) * len(shape))


class Came:
    def __init__(self, array):
        self.array = array


def local_call(kernel, *, out_shape, grid, in_specs, out_specs, scratch_shapes=(), prefetch=0, mib, name, cost=LIGHT):
    def place(value, spec):
        if isinstance(value, Came):
            return value.array
        if value.ndim < 2 or spec.memory_space is pltpu.SMEM:
            return value
        return pltpu.with_memory_space_constraint(value, pltpu.HBM)

    def run(*args):
        given = [place(value, spec) for value, spec in zip(args[prefetch:], in_specs, strict=True)]
        return call(*args[:prefetch], *given)

    call = pl.pallas_call(
        kernel,
        grid_spec=pltpu.PrefetchScalarGridSpec(
            num_scalar_prefetch=prefetch,
            grid=grid,
            in_specs=in_specs,
            out_specs=out_specs,
            scratch_shapes=scratch_shapes,
        ),
        out_shape=out_shape,
        compiler_params=pltpu.CompilerParams(vmem_limit_bytes=mib << 20),
        cost_estimate=cost,
        name=name,
    )
    return run


class Turn:
    def __init__(self):
        self.last = None

    def __call__(self, value):
        if self.last is None:
            return value
        return lax.optimization_barrier((value, self.last))[0]

    def done(self, value):
        self.last = value[0] if isinstance(value, (list, tuple)) else value
        return value


def block_order(count):
    order = [0]
    bit = count // 2
    while bit:
        order = order + [slot | bit for slot in order]
        bit //= 2
    return order


def tensor_bits(count):
    bits = []
    bit = count // 2
    while bit:
        bits.append(bit)
        bit //= 2
    return bits


def swap_tensor(value, bit):
    size = lax.axis_size("tensor")
    return lax.ppermute(value, "tensor", [(i, i ^ bit) for i in range(size)])


def gather_tensor(value, count, ready=()):
    slots = [value]
    for bit in tensor_bits(count):
        came = [swap_tensor(piece, bit) for piece in slots]
        if ready:
            came, ready = lax.optimization_barrier((came, ready))
        slots = slots + came
    return slots, ready


def scatter_tensor(value, count, bits=None):
    for bit in reversed(tensor_bits(count) if bits is None else bits):
        half = value.shape[0] // 2
        came = swap_tensor(value[half:], bit)
        value = (value[:half].astype(F32) + came.astype(F32)).astype(BF16)
    return value


def dp_steps(count):
    bits = []
    bit = 1
    while bit < count:
        bits.append(bit)
        bit *= 2
    return list(zip(bits, bits[1::-1] + bits[2:], strict=True))


def swap_dp(value, pair):
    rows, cols = lax.axis_size("dp"), lax.axis_size("tensor")
    route = []
    for row in range(rows):
        for col in range(cols):
            route.append((row * cols + col, (row ^ pair[col % 2]) * cols + col))
    return lax.ppermute(value, ("dp", "tensor"), route)


def side_of(pair):
    row, col = lax.axis_index("dp"), lax.axis_index("tensor")
    bit = jnp.where(col % 2 == 1, pair[1], pair[0])
    return ((row & bit) != 0).astype(jnp.int32)[None]


def add_kernel(left_ref, right_ref, out_ref):
    total = left_ref[...].astype(F32) + right_ref[...].astype(F32)
    out_ref[...] = total.astype(out_ref.dtype)


def add(left, right, cost=LIGHT):
    return local_call(
        add_kernel,
        grid=(1,),
        in_specs=[vmem_whole(left.shape)] * 2,
        out_specs=vmem_whole(left.shape),
        out_shape=FAR(left.shape, left.dtype),
        mib=8,
        name="add",
        cost=cost,
    )(left, Came(right))


def add_pieces_kernel(count, *refs):
    step = pl.program_id(0)
    for k in range(count):

        @pl.when(step == k)
        def _():
            total = refs[0][...].astype(F32) + refs[1][...].astype(F32)
            refs[2 + k][...] = total.astype(BF16)


def add_pieces(left, right, count, cost=LIGHT):
    rows, cols = left.shape
    part = pl.BlockSpec((rows // count, cols), lambda i: (i, 0))
    return local_call(
        functools.partial(add_pieces_kernel, count),
        grid=(count,),
        in_specs=[part, part],
        out_specs=[vmem_whole((rows // count, cols))] * count,
        out_shape=[FAR((rows // count, cols), BF16)] * count,
        mib=10,
        name="add_pieces",
        cost=cost,
    )(left, Came(right))


def add_swap_kernel(left_ref, right_ref, plain_ref, swapped_ref):
    total = (left_ref[...].astype(F32) + right_ref[...].astype(F32)).astype(BF16)
    plain_ref[...] = total
    swapped_ref[...] = total


def add_swap(left, right, count, flip, cost=LIGHT):
    rows, cols = left.shape
    part = pl.BlockSpec((rows // count, cols), lambda i: (i, 0))
    return local_call(
        add_swap_kernel,
        grid=(count,),
        in_specs=[part, part],
        out_specs=[part, pl.BlockSpec((rows // count, cols), lambda i: (i ^ flip, 0))],
        out_shape=[FAR((rows, cols), BF16), FREE((rows, cols), BF16)],
        mib=10,
        name="add_swap",
        cost=cost,
    )(left, Came(right))


def fold_kernel(side_ref, kept_ref, came_ref, send_ref, keep_ref):
    total = (kept_ref[...].astype(F32) + came_ref[...].astype(F32)).astype(BF16)

    @pl.when(pl.program_id(0) == 0)
    def _():
        send_ref[...] = total

    @pl.when(pl.program_id(0) == 1)
    def _():
        keep_ref[...] = total


def fold(side, kept, came, cost=LIGHT):
    rows, cols = kept.shape
    half = rows // 2
    if half % 16:
        total = (kept.astype(F32) + came.astype(F32)).astype(BF16)
        return [lax.dynamic_slice_in_dim(total, k * half, half) for k in (1 - side[0], side[0])]
    place = pl.BlockSpec((half, cols), lambda i, side: (jnp.where(i == 0, 1 - side[0], side[0]), 0))
    whole = pl.BlockSpec((half, cols), lambda i, side: (0, 0))
    return local_call(
        fold_kernel,
        grid=(2,),
        in_specs=[place, place],
        out_specs=[whole, whole],
        out_shape=[FREE((half, cols), BF16), FAR((half, cols), BF16)],
        prefetch=1,
        mib=8,
        name="fold",
        cost=cost,
    )(side, kept, Came(came))


def join_kernel(steps, side_ref, own_ref, came_ref, out_ref):
    upper = pl.program_id(0) // steps
    mine = upper == side_ref[0]

    @pl.when(mine)
    def _():
        out_ref[...] = own_ref[...].astype(out_ref.dtype)

    @pl.when(jnp.logical_not(mine))
    def _():
        out_ref[...] = came_ref[...].astype(out_ref.dtype)


def join(side, own, came, cost=LIGHT):
    rows, cols = own.shape
    if rows % 16:
        mine = side[0] != 0
        pair = (jnp.where(mine, came, own), jnp.where(mine, own, came))
        return jnp.concatenate(pair)
    steps = 1
    part = rows // steps
    half = pl.BlockSpec((part, cols), lambda i, side: (i % steps, 0))
    return local_call(
        functools.partial(join_kernel, steps),
        grid=(2 * steps,),
        in_specs=[half, half],
        out_specs=pl.BlockSpec((part, cols), lambda i, side: (i, 0)),
        out_shape=FAR((2 * rows, cols), BF16),
        prefetch=1,
        mib=10,
        name="join",
        cost=cost,
    )(side, own, Came(came))


SMALL = 16


def split_small(value):
    coarse = value.astype(BF16)
    return jnp.concatenate((coarse, (value - coarse.astype(F32)).astype(BF16)), axis=0)


def read_small(rows):
    return rows[:SMALL].astype(F32) + rows[SMALL:].astype(F32)


def fold_small_kernel(side_ref, kept_ref, came_ref, small_came_ref, small_ref, send_ref, keep_ref, small_out_ref):
    total = (kept_ref[...].astype(F32) + came_ref[...].astype(F32)).astype(BF16)
    half = keep_ref.shape[0]

    @pl.when(pl.program_id(0) == 0)
    def _():
        small = split_small(read_small(small_ref) + read_small(small_came_ref))
        send_ref[:half] = total
        send_ref[half:] = small
        small_out_ref[...] = small

    @pl.when(pl.program_id(0) == 1)
    def _():
        keep_ref[...] = total


def fold_small(side, kept, came, small, cost=LIGHT):
    rows, cols = kept.shape
    half = rows // 2
    extra = 2 * SMALL
    if half % extra:
        send, keep = fold(side, kept, came[:rows])
        small = split_small(read_small(small) + read_small(came[rows:]))
        return jnp.concatenate((send, small)), keep, small
    place = pl.BlockSpec((half, cols), lambda i, side: (jnp.where(i == 0, 1 - side[0], side[0]), 0))

    def whole(count):
        return pl.BlockSpec((count, cols), lambda i, side: (0, 0))

    return local_call(
        fold_small_kernel,
        grid=(2,),
        in_specs=[place, place, pl.BlockSpec((extra, cols), lambda i, side: (rows // extra, 0)), whole(extra)],
        out_specs=[whole(half + extra), whole(half), whole(extra)],
        out_shape=[FREE((half + extra, cols), BF16), FAR((half, cols), BF16), FAR((extra, cols), BF16)],
        prefetch=1,
        mib=10,
        name="fold_small",
        cost=cost,
    )(side, kept, Came(came), Came(came), small)


def add_small_kernel(kept_ref, came_ref, small_ref, out_ref, small_out_ref):
    rows = kept_ref.shape[0]
    out_ref[...] = (kept_ref[...].astype(F32) + came_ref[:rows].astype(F32)).astype(BF16)
    small_out_ref[...] = read_small(small_ref) + read_small(came_ref[rows:])


def add_small(kept, came, small, cost=LIGHT):
    rows, cols = kept.shape
    if rows % (2 * SMALL):
        return add(kept, came[:rows]), read_small(small) + read_small(came[rows:])
    return local_call(
        add_small_kernel,
        grid=(1,),
        in_specs=[vmem_whole(kept.shape), vmem_whole(came.shape), vmem_whole(small.shape)],
        out_specs=[vmem_whole(kept.shape), vmem_whole((SMALL, cols))],
        out_shape=[FAR(kept.shape, BF16), FAR((SMALL, cols), F32)],
        mib=8,
        name="add_small",
        cost=cost,
    )(kept, Came(came), small)


class DpSum:
    def __init__(self, turn, send, keep, finish, small=None):
        self.turn, self.finish, self.small = turn, finish, small
        self.pairs = dp_steps(lax.axis_size("dp"))
        self.at = 0
        self.keep = keep
        self.came = swap_dp(send, self.pairs[0])

    def step(self, cost=LIGHT):
        turn, last = self.turn, len(self.pairs) - 1
        came = turn(self.came)
        if self.at < last:
            after = self.pairs[self.at + 1]
            if self.small is None:
                send, self.keep = turn.done(fold(side_of(after), self.keep, came, cost))
            else:
                results = turn.done(fold_small(side_of(after), self.keep, came, self.small, cost))
                send, self.keep, self.small = results
            self.came = swap_dp(send, after)
        elif self.at == last:
            if self.small is None:
                self.keep = turn.done(add(self.keep, came, cost))
            else:
                self.keep, self.small = turn.done(add_small(self.keep, came, self.small, cost))
            self.came = swap_dp(self.keep, self.pairs[last])
        else:
            place = 2 * last + 1 - self.at
            side = side_of(self.pairs[place])
            if place == 0:
                self.result = turn.done(self.finish(side, self.keep, came))
            else:
                self.keep = turn.done(join(side, self.keep, came, cost))
                self.came = swap_dp(self.keep, self.pairs[place - 1])
        self.at += 1

    def rest(self):
        while self.at < 2 * len(self.pairs):
            self.step()
        return self.result


def finish_feed_kernel(side_ref, own_ref, came_ref, back_ref, in_ref):
    step = pl.program_id(0)
    many = back_ref.shape[0]

    def put(source):
        back_ref[...] = source[:many].astype(F32)
        in_ref[...] = source[many:].astype(F32)

    @pl.when(step == side_ref[0])
    def _():
        put(own_ref)

    @pl.when(step != side_ref[0])
    def _():
        put(came_ref)


def finish_feed(side, own, came):
    rows, cols = own.shape
    whole = pl.BlockSpec((rows, cols), lambda i, side: (0, 0))
    return local_call(
        finish_feed_kernel,
        grid=(2,),
        in_specs=[whole, whole],
        out_specs=[pl.BlockSpec((rows // 2, cols), lambda i, side: (i, 0))] * 2,
        out_shape=[FREE((rows, cols), F32)] * 2,
        prefetch=1,
        mib=20,
        name="finish_feed",
    )(side, own, Came(came))


def finish_heads_kernel(side_ref, own_ref, came_ref, q_ref, k_ref, v_ref, out_ref):
    step = pl.program_id(0)
    cols = q_ref.shape[0]
    for half, refs in enumerate(((q_ref, k_ref), (v_ref, out_ref))):
        for source, is_own in ((own_ref, True), (came_ref, False)):

            @pl.when((step == half) & ((side_ref[0] == half) == is_own))
            def _():
                refs[0][...] = source[:cols].astype(F32)
                refs[1][...] = source[cols:].astype(F32)


def finish_heads(side, own, came):
    rows, cols = own.shape
    each = rows // 2
    whole = pl.BlockSpec((rows, cols), lambda i, side: (0, 0))
    return local_call(
        finish_heads_kernel,
        grid=(2,),
        in_specs=[whole, whole],
        out_specs=[pl.BlockSpec((each, cols), lambda i, side: (0, 0))] * 4,
        out_shape=[FREE((each, cols), F32)] * 4,
        prefetch=1,
        mib=12,
        name="finish_heads",
    )(side, own, Came(came))


def group_scale(groups_ref, own_ref):
    own = groups_ref[own_ref[0]]
    alike = jnp.int32(0)
    for row in range(groups_ref.shape[0]):
        alike += (groups_ref[row] == own).astype(jnp.int32)
    return lax.rsqrt(jnp.full((1, LANES), alike.astype(F32)))[:, 0:1]


def row_of(ref):
    return ref[...].reshape(1, ref.shape[0])


def norm_rows(values):
    return lax.rsqrt(jnp.mean(values * values, axis=-1, keepdims=True) + NORM_EPS)


def norm_back(dnormed, unit, spread, gain):
    scaled = gain * dnormed
    inner = jnp.mean(scaled * unit, axis=-1, keepdims=True)
    return spread * (scaled - unit * inner), dnormed * unit


def bias_lanes(seq, first_row, first_col):
    start = seq - LANES - first_row + first_col
    return pl.multiple_of(start, LANES)


def bias_kernel(table_ref, buckets_ref, bias_ref):
    which = buckets_ref[...]
    heads, _, wide = bias_ref.shape
    for h in range(heads):
        rel = jnp.zeros((8, wide), F32)
        for b in range(table_ref.shape[0]):
            rel = jnp.where(which == b, table_ref[b, h], rel)
        full = jnp.broadcast_to(rel[0:1], (LANES, wide))
        bias_ref[h] = pltpu.roll(full, wide - (LANES - 1), 1, stride=1, stride_axis=0)


def bias_tiles(table, buckets):
    shape = (table.shape[1], LANES, buckets.shape[1])
    return local_call(
        bias_kernel,
        grid=(1,),
        in_specs=[pl.BlockSpec(memory_space=pltpu.SMEM), vmem_whole(buckets.shape)],
        out_specs=vmem_whole(shape),
        out_shape=FAR(shape, F32),
        mib=16,
        name="bias_tiles",
        cost=HEAVY,
    )(table, buckets)


def attend_kernel(heads, count, length_ref, starts_ref, gain_ref, wq_ref, wk_ref, wv_ref, *refs):
    tok_refs, bias_far, refs = refs[:count], refs[count], refs[count + 1 :]
    (ctx_ref, packed_ref, exps_ref, linv_ref, normed_ref, tok_all_ref) = refs[:6]
    (q_ref, v_ref, k_turned_ref, k_ref, v_turned_ref, bias_ref, all_normed, scores_ref, sem) = refs[6:]
    step = pl.program_id(0)
    blk = ctx_ref.shape[0]
    seq = blk * count
    head_cols = wq_ref.shape[0]
    width = head_cols // heads

    @pl.when(step == 0)
    def _():
        bias_copy = pltpu.make_async_copy(bias_far, bias_ref, sem)
        bias_copy.start()
        lane = lax.broadcasted_iota(jnp.int32, (blk, LANES - width), 1)
        row = lax.broadcasted_iota(jnp.int32, (blk, LANES - width), 0)
        line = lax.broadcasted_iota(jnp.int32, (LANES - width, blk), 0)
        place = lax.broadcasted_iota(jnp.int32, (LANES - width, blk), 1)
        ones_q = jnp.where(lane == 0, 1.0, 0.0)
        ones_v = jnp.where(lane < 2, 1.0, 0.0)
        ones_turned = jnp.where(line < 2, 1.0, 0.0)
        for b in range(count):
            values = tok_refs[b][...].astype(F32)
            normed = (values * norm_rows(values) * row_of(gain_ref)).astype(BF16)
            rows = slice(b * blk, (b + 1) * blk)
            all_normed[rows] = normed
            used = length_ref[0] - starts_ref[b]
            fill = jnp.where((lane == 0) & (row >= used), MASK_FILL, 0.0)
            fill_turned = jnp.where((line == 0) & (place >= used), MASK_FILL, 0.0)
            query = dot_nt(normed, wq_ref[...])
            keys = dot_nt(normed, wk_ref[...])
            values = dot_nt(normed, wv_ref[...])
            keys_turned = dot_nt(wk_ref[...], normed)
            values_turned = dot_nt(wv_ref[...], normed)
            for h in range(heads):
                cols = slice(h * width, (h + 1) * width)
                q_ref[h, rows] = jnp.concatenate((query[:, cols], ones_q), axis=1).astype(BF16)
                k_ref[h, rows] = jnp.concatenate((keys[:, cols], fill), axis=1).astype(BF16)
                v_ref[h, rows] = jnp.concatenate((values[:, cols], ones_v), axis=1).astype(BF16)
                k_turned_ref[h, :, rows] = jnp.concatenate((keys_turned[cols], fill_turned), axis=0).astype(BF16)
                v_turned_ref[h, :, rows] = jnp.concatenate((values_turned[cols], ones_turned), axis=0).astype(BF16)
        bias_copy.wait()

    row0 = pl.multiple_of(step * blk, blk)
    first_query = starts_ref[step]
    normed_ref[...] = all_normed[pl.ds(row0, blk)]
    for b in range(count):

        @pl.when(step == b)
        def _():
            tok_all_ref[...] = tok_refs[b][...]

    outs = []
    linv = jnp.zeros((blk, LANES), F32)
    stat_lane = lax.broadcasted_iota(jnp.int32, (blk, LANES), 1)
    for h in range(heads):
        query = q_ref[h, pl.ds(row0, blk)]
        top = jnp.full((8, blk), -3.0e38, F32)
        for b in range(count):
            for a in range(blk // LANES):
                rows = slice(b * blk + a * LANES, b * blk + (a + 1) * LANES)
                start = bias_lanes(seq, starts_ref[b] + a * LANES, first_query)
                scores = dot_nt(k_ref[h, rows], query) + bias_ref[h, :, pl.ds(start, blk)]
                scores_ref[rows] = scores
                top = jnp.maximum(top, jnp.max(scores.reshape(LANES // 8, 8, blk), axis=0))
        top = jnp.max(top, axis=0, keepdims=True)
        for c in range(seq // LANES):
            rows = slice(c * LANES, (c + 1) * LANES)
            exps_ref[h, rows] = jnp.exp(scores_ref[rows] - top).astype(BF16)
        mixed = dot_nn(v_turned_ref[h], exps_ref[h]).T
        inverse = 1.0 / mixed[:, width : width + 1]
        outs.append(mixed[:, :width] * inverse)
        linv = jnp.where(stat_lane == h, inverse, linv)
    ctx = jnp.concatenate(outs, axis=1).astype(BF16)
    ctx_ref[...] = ctx
    linv_ref[...] = linv
    packed_ref[pl.ds(row0, blk)] = ctx[:, :LANES]
    rest = head_cols - LANES
    for k in range(count):

        @pl.when(step == k)
        def _():
            place = seq + (k % (count // 2)) * blk
            lanes = (k // (count // 2)) * rest
            packed_ref[place : place + blk, lanes : lanes + rest] = ctx[:, LANES:]


def attend(length, starts, bias, gain, w_query, w_key, w_value, tok):
    count = len(tok)
    blk, model = tok[0].shape
    seq = blk * count
    heads = bias.shape[0]
    head_cols = w_query.shape[0]
    smem = pl.BlockSpec(memory_space=pltpu.SMEM)
    assert 2 * (head_cols - LANES) == LANES
    return local_call(
        functools.partial(attend_kernel, heads, count),
        grid=(count,),
        in_specs=[smem, smem, vmem_whole((model,))]
        + [vmem_whole((head_cols, model))] * 3
        + [vmem_whole((blk, model))] * count
        + [pl.BlockSpec(memory_space=pl.ANY)],
        out_specs=[
            pl.BlockSpec((blk, head_cols), lambda i: (i, 0)),
            vmem_whole((seq * 3 // 2, LANES)),
            pl.BlockSpec((heads, seq, blk), lambda i: (0, 0, i)),
            pl.BlockSpec((blk, LANES), lambda i: (i, 0)),
            pl.BlockSpec((blk, model), lambda i: (i, 0)),
            pl.BlockSpec((blk, model), lambda i: (i, 0)),
            vmem_whole((heads, seq, LANES)),
            vmem_whole((heads, seq, LANES)),
            vmem_whole((heads, LANES, seq)),
        ],
        out_shape=[
            FAR((seq, head_cols), BF16),
            FAR((seq * 3 // 2, LANES), BF16),
            FAR((heads, seq, seq), BF16),
            FAR((seq, LANES), F32),
            FAR((seq, model), BF16),
            FAR((seq, model), BF16),
            FAR((heads, seq, LANES), BF16),
            FAR((heads, seq, LANES), BF16),
            FAR((heads, LANES, seq), BF16),
        ],
        scratch_shapes=[
            pltpu.VMEM((heads, seq, LANES), BF16),
            pltpu.VMEM((heads, LANES, seq), BF16),
            pltpu.VMEM((heads, LANES, 2 * seq), F32),
            pltpu.VMEM((seq, model), BF16),
            pltpu.VMEM((seq, blk), F32),
            pltpu.SemaphoreType.DMA,
        ],
        mib=28,
        name="attend",
        cost=HEAVY,
    )(length, starts, gain, w_query, w_key, w_value, *[Came(piece) for piece in tok], bias)


def feed_kernel(count, side_ref, groups_ref, own_ref, gain_ref, *refs):
    tok_far, ctx_far, refs = refs[0], refs[1 : 1 + count], refs[1 + count :]
    w_in_far, w_back_far, joined_far, refs = refs[0], refs[1], refs[2 : 2 + count], refs[2 + count :]
    hidden_ref, unit_ref, spread_ref, active_ref, dn_low_ref, dn_high_ref, send_far, keep_far = refs[:8]
    tok_all, ctx_all, w_in_ref, w_back_ref, w_out_ref, grad_all, normed_now, dup_all, active_turned = refs[8:17]
    normed_turned, hidden_now, halves, sems, out_sems = refs[17:]
    step = pl.program_id(0)
    blk = hidden_ref.shape[0]
    half = count // 2
    span = blk * half
    units, model = w_back_ref.shape
    rest = LANES // 2
    many, fewer = units // 2, model // 2
    used = 0

    def copy(far, near):
        nonlocal used
        used += 1
        return pltpu.make_async_copy(far, near, sems.at[used - 1])

    row_copies, out_copies, grad_copies = [], [], []
    for b in range(count):
        rows = pl.ds(b * blk, blk)
        found = [copy(tok_far.at[rows], tok_all.at[rows])]
        for k in range(count):
            c = b ^ k
            lanes = 2 * k * LANES
            found.append(copy(ctx_far[k].at[pl.ds(c * blk, blk)], ctx_all.at[rows, pl.ds(lanes, LANES)]))
            place = pl.ds(count * blk + (c % half) * blk, blk)
            found.append(copy(ctx_far[k].at[place], ctx_all.at[rows, pl.ds(lanes + LANES, LANES)]))
        row_copies.append(found)
        grad_copies.append(copy(joined_far[b].at[pl.ds(0, blk)], grad_all.at[rows]))
    for k in range(count):
        for part in range(2):
            top = 2 * k * LANES
            out_copies.append(copy(joined_far[k].at[pl.ds(blk, LANES)], w_out_ref.at[part, pl.ds(top, LANES)]))
            place = w_out_ref.at[part, pl.ds(top + LANES + (part ^ (k // half)) * rest, rest)]
            out_copies.append(copy(joined_far[k].at[pl.ds(blk + LANES, rest)], place))
    in_copy = copy(w_in_far, w_in_ref)
    back_copy = copy(w_back_far, w_back_ref)

    @pl.when(step == 0)
    def _():
        early = [one for b in range(half) for one in row_copies[b]]
        late = [one for b in range(half, count) for one in row_copies[b]]
        for one in [*out_copies, *early, in_copy, *grad_copies[:half], back_copy, *late, *grad_copies[half:]]:
            one.start()
        for part in range(2):
            for k in range(count):
                other = 2 * k * LANES + LANES + (1 - (part ^ (k // half))) * rest
                w_out_ref[part, other : other + rest] = jnp.zeros((rest, model), BF16)
        for one in out_copies:
            one.wait()

    for part in range(2):

        @pl.when(step == part)
        def _():
            for b in range(part * half, (part + 1) * half):
                for one in row_copies[b]:
                    one.wait()

    rows = pl.ds(pl.multiple_of(step * span, span), span)
    for b in range(half):
        there = pl.ds(pl.multiple_of(step * span + b * blk, blk), blk)
        hidden_now[b * blk : (b + 1) * blk] = tok_all[there].astype(F32) + dot_nn(ctx_all[there], w_out_ref[step])
    strip = 32 if blk % 32 == 0 else blk
    for r in range(0, span, strip):
        some = slice(r, r + strip)
        hidden = hidden_now[some]
        spread = norm_rows(hidden)
        unit = hidden * spread
        unit_ref[some] = unit.astype(BF16)
        spread_ref[some] = jnp.broadcast_to(spread, (strip, LANES))
        normed_now[some] = (unit * row_of(gain_ref)).astype(BF16)
    normed = normed_now[...]
    normed_turned[:, rows] = normed.T

    @pl.when(step == 0)
    def _():
        hidden_ref[...] = hidden_now[0:blk]
        in_copy.wait()
        back_copy.wait()

    for part in range(2):

        @pl.when(step == part)
        def _():
            for b in range(part * half, (part + 1) * half):
                grad_copies[b].wait()

    grad = grad_all[rows]
    scale = group_scale(groups_ref, own_ref)
    part = 256 if units % 256 == 0 else units
    for b in range(0, span, 256):
        near = slice(b, b + 256)
        there = pl.ds(pl.multiple_of(step * span + b, 256), 256)
        for c in range(0, units, part):
            cols = slice(c, c + part)
            up = dot_nn(normed[near], w_in_ref[:, cols])
            dactive = dot_nt(grad[near], w_back_ref[cols])
            square = up * up
            bend = jnp.tanh(up * (GELU_SCALE + GELU_SCALE * GELU_CUBE * square))
            bell = 0.5 + 0.5 * bend
            active = (up * bell).astype(BF16)
            steep = GELU_SCALE + 3.0 * GELU_SCALE * GELU_CUBE * square
            slope = (bell + (0.5 * up) * (1.0 - bend * bend) * steep) * scale
            active_ref[near, cols] = active
            active_turned[cols, there] = active.T
            dup_all[there, cols] = (dactive * slope).astype(BF16)

    def put(dn_ref):
        for b in range(0, span, 256):
            near = slice(b, b + 256)
            there = pl.ds(pl.multiple_of(step * span + b, 256), 256)
            dn_ref[near] = dot_nt(dup_all[there], w_in_ref[...]).astype(BF16)

    @pl.when(step == 0)
    def _():
        put(dn_low_ref)

    @pl.when(step == 1)
    def _():
        put(dn_high_ref)
        going = []
        for k, (far, side) in enumerate(((send_far, 1 - side_ref[0]), (keep_far, side_ref[0]))):
            back = dot_nn(active_turned[pl.ds(side * many, many)], grad_all[...]) * scale
            halves[k, :many] = back.astype(BF16)
            halves[k, many:] = dot_nn(normed_turned[pl.ds(side * fewer, fewer)], dup_all[...]).astype(BF16)
            going.append(pltpu.make_async_copy(halves.at[k], far, out_sems.at[k]))
            going[-1].start()
        for one in going:
            one.wait()


def feed(side, groups, own, gain, w_in, w_back, tok, ctx, joined):
    count = len(ctx)
    rows, model = tok.shape
    blk = rows // count
    units = w_in.shape[1]
    span = rows // 2
    by_row = pl.BlockSpec((span, model), lambda i, side: (i, 0))
    anywhere = pl.BlockSpec(memory_space=pl.ANY)
    smem = pl.BlockSpec(memory_space=pltpu.SMEM)

    def whole(shape):
        return pl.BlockSpec(shape, lambda i, side: (0, 0))

    grads = ((units + model) // 2, model)
    copies = count * (4 + 2 * count) + 2 + 2 * count
    return local_call(
        functools.partial(feed_kernel, count),
        grid=(2,),
        in_specs=[smem, smem, pl.BlockSpec((model,), lambda i, side: (0,))] + [anywhere] * (3 + 2 * count),
        out_specs=[
            whole((blk, model)),
            by_row,
            pl.BlockSpec((span, LANES), lambda i, side: (i, 0)),
            pl.BlockSpec((span, units), lambda i, side: (i, 0)),
            *[whole((span, model))] * 2,
            anywhere,
            anywhere,
        ],
        out_shape=[FAR((blk, model), F32), FAR((rows, model), BF16), FAR((rows, LANES), F32), FAR((rows, units), BF16)]
        + [FAR((span, model), BF16)] * 2
        + [FAR(grads, BF16)] * 2,
        scratch_shapes=[
            pltpu.VMEM((rows, model), BF16),
            pltpu.VMEM((rows, 2 * count * LANES), BF16),
            pltpu.VMEM((model, units), BF16),
            pltpu.VMEM((units, model), BF16),
            pltpu.VMEM((2, 2 * count * LANES, model), BF16),
            pltpu.VMEM((rows, model), BF16),
            pltpu.VMEM((span, model), BF16),
            pltpu.VMEM((rows, units), BF16),
            pltpu.VMEM((units, rows), BF16),
            pltpu.VMEM((model, rows), BF16),
            pltpu.VMEM((span, model), F32),
            pltpu.VMEM((2, *grads), BF16),
            pltpu.SemaphoreType.DMA((copies,)),
            pltpu.SemaphoreType.DMA((2,)),
        ],
        prefetch=1,
        mib=52,
        name="feed",
        cost=cost_of("feed"),
    )(side, groups, own, gain, tok, ctx[0], *[Came(a) for a in ctx[1:]], w_in, w_back, *joined)


def feed_out_kernel(active_ref, w_back_ref, *out_refs):
    for k, ref in enumerate(out_refs):

        @pl.when(pl.program_id(0) == k)
        def _():
            ref[...] = dot_nn(active_ref[...], w_back_ref[...]).astype(BF16)


def feed_out(active, w_back, count, cost):
    rows, units = active.shape
    model = w_back.shape[1]
    blk = rows // count
    return local_call(
        feed_out_kernel,
        grid=(count,),
        in_specs=[pl.BlockSpec((blk, units), lambda i: (i, 0)), vmem_whole(w_back.shape)],
        out_specs=[vmem_whole((blk, model))] * count,
        out_shape=[FAR((blk, model), BF16)] * count,
        mib=16,
        name="feed_out",
        cost=cost,
    )(active, w_back)


def finish_mixed_kernel(hidden_ref, own_ref, came_ref, out_ref):
    total = own_ref[...].astype(F32) + came_ref[...].astype(F32)
    out_ref[...] = (hidden_ref[...] + total).astype(BF16)


def finish_mixed(hidden, own, came, cost=LIGHT):
    blk, model = own.shape
    place = pl.BlockSpec((blk, model), lambda i: (0, 0))
    return local_call(
        finish_mixed_kernel,
        grid=(1,),
        in_specs=[place] * 3,
        out_specs=place,
        out_shape=jax.ShapeDtypeStruct((blk, model), BF16),
        mib=10,
        name="finish_mixed",
        cost=cost,
    )(hidden, own, Came(came))


def finish_tokens_kernel(gain_ref, tok_ref, own_ref, came_ref, dh_ref, out_ref):
    dnormed = own_ref[...].astype(F32) + came_ref[...].astype(F32)
    values = tok_ref[...].astype(F32)
    spread = norm_rows(values)
    out_ref[...] = dh_ref[...].astype(F32) + norm_back(dnormed, values * spread, spread, row_of(gain_ref))[0]


def finish_tokens(gain, tok, own, came, dh_own, cost=LIGHT):
    blk, model = own.shape
    steps = 2 if blk % 32 == 0 else 1
    place = pl.BlockSpec((blk // steps, model), lambda i: (i, 0))
    return local_call(
        finish_tokens_kernel,
        grid=(steps,),
        in_specs=[vmem_whole((model,))] + [place] * 4,
        out_specs=place,
        out_shape=jax.ShapeDtypeStruct((blk, model), F32),
        mib=10,
        name="finish_tokens",
        cost=cost,
    )(gain, tok, own, Came(came), dh_own)


def attend_back_kernel(heads, count, side_ref, starts_ref, groups_ref, own_ref, gain_ref, buckets_ref, *refs):
    dn_far, joined_far, refs = refs[:count], refs[count : 2 * count], refs[2 * count :]
    unit_far, spread_far, ctx_far, linv_far, exps_far, w_out_far, refs = *refs[:6], refs[6:]
    late_far, refs = refs[:8], refs[8:]
    dh_own_far, small_far, send_far, keep_far, in_low_far, in_high_far, refs = *refs[:6], refs[6:]
    dn_all, grad_all, unit_all, spread_all, ctx_all, linv_all, exps_all, w_out_ref, refs = *refs[:8], refs[8:]
    late_near, refs = refs[:8], refs[8:]
    v_ref, q_ref, k_turned_ref, normed_ref, tok_ref, wq_ref, wk_ref, wv_ref = late_near
    dk_ref, dv_ref, acc_ref, ds_ref, given_ref, dh_all, dj_ref, sums_ref, in_all, halves, sems, out_sems = refs
    block = pl.program_id(0)
    seq, model = dh_all.shape
    blk = seq // count
    head_cols = ctx_all.shape[1]
    width = head_cols // heads
    wide = acc_ref.shape[2]
    half_cols = 2 * head_cols
    strip = 32 if blk % 32 == 0 else blk

    def first_copies(b):
        rows = pl.ds(b * blk, blk)
        pairs = [
            (dn_far[b], dn_all.at[rows]),
            (unit_far.at[rows], unit_all.at[rows]),
            (spread_far.at[rows], spread_all.at[rows]),
            (joined_far[b].at[pl.ds(0, blk)], grad_all.at[rows]),
            (ctx_far.at[rows], ctx_all.at[rows]),
            (linv_far.at[rows], linv_all.at[rows]),
        ]
        return [pltpu.make_async_copy(far, near, sems.at[7 * b + k]) for k, (far, near) in enumerate(pairs)]

    def exps_copy(b):
        cols = pl.ds(b * blk, blk)
        return pltpu.make_async_copy(exps_far.at[:, :, cols], exps_all.at[b % 2], sems.at[7 * b + 6])

    out_copy = pltpu.make_async_copy(w_out_far, w_out_ref, sems.at[7 * count])
    late = [pltpu.make_async_copy(late_far[k], late_near[k], sems.at[7 * count + 1 + k]) for k in range(8)]

    @pl.when(block == 0)
    def _():
        for copy in [*first_copies(0), out_copy, late[0], exps_copy(0), late[1], late[2], *first_copies(1)]:
            copy.start()
        dk_ref[...] = jnp.zeros_like(dk_ref)
        dv_ref[...] = jnp.zeros_like(dv_ref)
        acc_ref[...] = jnp.zeros_like(acc_ref)

    for b in range(count):

        @pl.when(block == b)
        def _():
            if b + 1 < count:
                exps_copy(b + 1).start()
            if b == 0:
                for k in range(2, count):
                    for copy in first_copies(k):
                        copy.start()
                for copy in late[3:]:
                    copy.start()
            for copy in first_copies(b):
                copy.wait()
            if b == 0:
                out_copy.wait()
                for copy in late[:3]:
                    copy.wait()
            exps_copy(b).wait()

    row0 = pl.multiple_of(block * blk, blk)
    now = pl.ds(row0, blk)
    scale = group_scale(groups_ref, own_ref)
    for r in range(0, blk, strip):
        there = pl.ds(pl.multiple_of(row0 + r, strip), strip)
        unit = unit_all[there].astype(F32)
        scaled = row_of(gain_ref) * dn_all[there].astype(F32)
        inner = jnp.mean(scaled * unit, axis=-1, keepdims=True)
        dhidden = spread_all[there, 0:1] * (scaled - unit * inner)
        dh_all[there] = (dhidden + grad_all[there].astype(F32) * scale).astype(BF16)

    dctx = dot_nt(dh_all[now], w_out_ref[...])
    product = dctx * ctx_all[now].astype(F32)
    lane = lax.broadcasted_iota(jnp.int32, (blk, LANES - width), 1)
    for h in range(heads):
        cols = slice(h * width, (h + 1) * width)
        inverse = linv_all[now, h : h + 1]
        inner = -jnp.sum(product[:, cols], axis=1, keepdims=True) * inverse
        coarse = inner.astype(BF16).astype(F32)
        extra = jnp.where(lane == 0, coarse, jnp.where(lane == 1, inner - coarse, 0.0))
        given_ref[h] = jnp.concatenate((dctx[:, cols] * inverse, extra), axis=1).astype(BF16)

    slot = lax.rem(block, 2)
    first_query = starts_ref[block]
    dquery = []
    for h in range(heads):
        given = given_ref[h]
        for b in range(count):
            for a in range(blk // LANES):
                rows = slice(b * blk + a * LANES, b * blk + (a + 1) * LANES)
                dscores = exps_all[slot, h, rows].astype(F32) * dot_nt(v_ref[h, rows], given)
                ds_ref[h, rows] = dscores.astype(BF16)
                start = bias_lanes(seq, starts_ref[b] + a * LANES, first_query)
                acc_ref[h, :, pl.ds(start, blk)] += dscores
        dk_ref[h] += dot_nn(ds_ref[h], q_ref[h, now])
        dv_ref[h] += dot_nn(exps_all[slot, h], given)
        dquery.append(dot_nn(k_turned_ref[h], ds_ref[h]).T[:, :width])
    dj_ref[0, now] = jnp.concatenate(dquery, axis=1).astype(BF16)

    @pl.when(block == 0)
    def _():
        total = jnp.zeros((1, model), F32)
        for r in range(0, blk, strip):
            product = unit_all[r : r + strip].astype(F32) * dn_all[r : r + strip].astype(F32)
            total += jnp.sum(product, axis=0, keepdims=True)
        sums_ref[...] = jnp.zeros_like(sums_ref)
        sums_ref[12:16] = jnp.broadcast_to(total, (4, model))
        pltpu.make_async_copy(dh_all.at[pl.ds(0, blk)], dh_own_far, out_sems.at[0]).start()

    @pl.when(block == count - 1)
    def _():
        dj_ref[1] = jnp.concatenate([dk_ref[h][:, :width] for h in range(heads)], axis=1).astype(BF16)
        dj_ref[2] = jnp.concatenate([dv_ref[h][:, :width] for h in range(heads)], axis=1).astype(BF16)
        going = [pltpu.make_async_copy(dh_all.at[pl.ds(0, blk)], dh_own_far, out_sems.at[0])]

        def send_out(near, far):
            going.append(pltpu.make_async_copy(near, far, out_sems.at[len(going)]))
            going[-1].start()

        for copy in late[3:]:
            copy.wait()
        gain_total = jnp.zeros((1, model), F32)
        for b in range(count):
            rows = slice(b * blk, (b + 1) * blk)
            dnormed = dot_nn(dj_ref[0, rows], wq_ref[...])
            dnormed = dnormed + dot_nn(dj_ref[1, rows], wk_ref[...])
            dnormed = dnormed + dot_nn(dj_ref[2, rows], wv_ref[...])
            in_all[rows] = dnormed.astype(BF16)
            for r in range(0, blk, strip):
                values = tok_ref[b * blk + r : b * blk + r + strip].astype(F32)
                product = dnormed[r : r + strip] * (values * norm_rows(values))
                gain_total += jnp.sum(product, axis=0, keepdims=True)
        send_out(in_all.at[pl.ds(0, seq // 2)], in_low_far)
        send_out(in_all.at[pl.ds(seq // 2, seq // 2)], in_high_far)
        sums_ref[8:12] = jnp.broadcast_to(gain_total, (4, model))

        drel = []
        for h in range(heads):
            part = acc_ref[h]
            rows = LANES
            while rows > 1:
                rows //= 2
                part = part[:rows] + pltpu.roll(part[rows:], wide - rows, 1)
            drel.append(pltpu.roll(part, LANES - 1, 1))
        drel = jnp.concatenate(drel + [jnp.zeros((8 - heads, wide), F32)], axis=0)
        bucket = lax.broadcasted_iota(jnp.int32, (LANES, wide), 0)
        onehot = jnp.where(bucket == jnp.broadcast_to(buckets_ref[0:1], (LANES, wide)), 1.0, 0.0).astype(BF16)
        table = jnp.zeros((8, LANES), F32)
        for _ in range(3):
            coarse = drel.astype(BF16)
            table = table + dot_nt(jnp.concatenate((coarse, jnp.zeros_like(coarse)), axis=0), onehot)[:8]
            drel = drel - coarse.astype(F32)
        sums_ref[0:8, 0:LANES] = table
        halves[0, half_cols:] = split_small(sums_ref[...])
        send_out(halves.at[0, pl.ds(half_cols, 2 * SMALL)], small_far)
        side = side_ref[0]
        for k in range(2):

            @pl.when((side == 0) == (k == 1))
            def _():
                halves[k, :head_cols] = dot_tn(dj_ref[0], normed_ref[...]).astype(BF16)
                halves[k, head_cols:half_cols] = dot_tn(dj_ref[1], normed_ref[...]).astype(BF16)

            @pl.when((side == 0) == (k == 0))
            def _():
                halves[k, :head_cols] = dot_tn(dj_ref[2], normed_ref[...]).astype(BF16)
                halves[k, head_cols:half_cols] = dot_tn(ctx_all[...], dh_all[...]).astype(BF16)

            if k == 0:
                send_out(halves.at[0], send_far)
            else:
                send_out(halves.at[1, pl.ds(0, half_cols)], keep_far)
        for copy in going:
            copy.wait()


def attend_back(cost, bucket_count, side, starts, groups, own, gain, w_out, buckets, dn, unit, spread, joined, ctx, linv, exps, q, v, k_turned, normed, weights, tok):
    head_cols, model = w_out.shape
    count = starts.shape[0]
    heads, seq = exps.shape[:2]
    assert bucket_count <= LANES and heads <= 8
    blk = seq // count

    def whole(shape):
        return pl.BlockSpec(shape, lambda i, side: (0,) * len(shape))

    def room(value):
        return pltpu.VMEM(value.shape, value.dtype)

    first = [unit, spread, ctx, linv]
    late = [v, q, k_turned, normed, tok, *weights]
    smem = pl.BlockSpec(memory_space=pltpu.SMEM)
    anywhere = pl.BlockSpec(memory_space=pl.ANY)
    extra = 2 * SMALL
    outs = [(blk, model), (extra, model), (2 * head_cols + extra, model), (2 * head_cols, model), (seq // 2, model), (seq // 2, model)]
    return local_call(
        functools.partial(attend_back_kernel, heads, count),
        grid=(count,),
        in_specs=[smem, smem, smem, whole((model,)), whole((8, 2 * seq))] + [anywhere] * (2 * count + 6 + len(late)),
        out_specs=[anywhere] * len(outs),
        out_shape=[FAR(shape, BF16) for shape in outs],
        scratch_shapes=[pltpu.VMEM((seq, model), BF16), pltpu.VMEM((seq, model), BF16)]
        + [room(a) for a in first]
        + [pltpu.VMEM((2, heads, seq, blk), BF16), room(w_out)]
        + [room(a) for a in late]
        + [
            pltpu.VMEM((heads, seq, LANES), F32),
            pltpu.VMEM((heads, seq, LANES), F32),
            pltpu.VMEM((heads, LANES, 2 * seq), F32),
            pltpu.VMEM((heads, seq, blk), BF16),
            pltpu.VMEM((heads, blk, LANES), BF16),
            pltpu.VMEM((seq, model), BF16),
            pltpu.VMEM((3, seq, head_cols), BF16),
            pltpu.VMEM((SMALL, model), F32),
            pltpu.VMEM((seq, model), BF16),
            pltpu.VMEM((2, 2 * head_cols + extra, model), BF16),
            pltpu.SemaphoreType.DMA((7 * count + 1 + len(late),)),
            pltpu.SemaphoreType.DMA((6,)),
        ],
        prefetch=1,
        mib=52,
        name="attend_back",
        cost=cost,
    )(side, starts, groups, own, gain, buckets, *[Came(a) for a in dn], *joined, *first, exps, w_out, *late)


def shards(
    tokens,
    row_lengths,
    instruction_mask,
    task_groups,
    rel_buckets,
    gain_attn,
    w_query,
    w_key,
    w_value,
    rel_table,
    w_out,
    gain_ffn,
    w_in,
    w_back,
    out_grad,
):
    blk, model = tokens.shape[1:]
    count = lax.axis_size("tensor")
    head_cols = w_query.shape[1]
    bucket_count, heads = rel_table.shape
    width = head_cols // heads
    seq = blk * count
    half = count // 2
    bits = tensor_bits(count)
    here = lax.axis_index("tensor")
    starts = (here ^ jnp.array(block_order(count), jnp.int32)) * blk
    weights = (w_query.T, w_key.T, w_value.T)
    own_row = lax.axis_index("dp")[None]
    turned = jnp.pad(rel_buckets[::-1], (0, 1), constant_values=-1)
    buckets = jnp.broadcast_to(turned[None], (8, 2 * seq))
    first_side = side_of(dp_steps(lax.axis_size("dp"))[0])

    positions = here * blk + jnp.arange(blk, dtype=jnp.int32)
    keep = (positions < row_lengths[0]) & (instruction_mask[0] == 0)
    masked_grad = jnp.where(keep[:, None], out_grad[0], 0).astype(BF16)

    turn = Turn()
    low_bits = bits[:-1]

    def across(pieces):
        while len(pieces) > 1:
            bit = low_bits[len(low_bits) - len(pieces).bit_length() + 1]
            near = len(pieces) // 2
            others = [swap_tensor(piece, bit) for piece in pieces[near:]]
            pieces = list(zip(pieces[:near], others, strict=True))
            if near > 1:
                pieces = [turn.done(add(a, turn(b))) for a, b in pieces]
        return pieces[0]

    own_tok = tokens[0]
    joined = jnp.concatenate((masked_grad, w_out))
    bias = bias_tiles(rel_table, buckets)
    ready = (joined, starts, own_row, bias)
    assert count == 4
    far_tok = swap_tensor(own_tok, 2)
    near_tok = swap_tensor(own_tok, 1)
    far_tok, ready = lax.optimization_barrier((far_tok, ready))
    joined, starts, own_row, bias = ready
    tok = [own_tok, far_tok, near_tok, swap_tensor(far_tok, 1)]
    joined = [joined, swap_tensor(joined, 2)]
    ctx, packed, exps, linv, normed, tok_all, q, v, k_turned = turn.done(
        attend(row_lengths, starts, bias, gain_attn, *weights, tok)
    )
    contexts, _ = gather_tensor(packed, count)
    joined = [turn(piece) for piece in joined]
    joined = joined + [swap_tensor(piece, bits[-1]) for piece in joined]
    hidden, unit, spread, active, dn_low, dn_high, feed_send, feed_keep = turn.done(
        feed(first_side, task_groups, own_row, gain_ffn, w_in, w_back, tok_all, contexts, joined)
    )
    dn_came = swap_tensor(dn_high, bits[-1])
    sum_feed = DpSum(turn, feed_send, feed_keep, finish_feed)
    assert half == 2 and len(low_bits) == 1
    flip = block_order(count).index(low_bits[0])
    got = {}

    def swap_dn(cost):
        got["dn"], sent = turn.done(add_swap(dn_low, turn(dn_came), half, flip, cost))
        got["dn_came"] = swap_tensor(sent, low_bits[0])

    def sum_dn(cost):
        got["dn"] = turn.done(add_pieces(got["dn"], turn(got["dn_came"]), half, cost))
        got["dn_far"] = [swap_tensor(piece, bits[-1]) for piece in got["dn"]]

    def back(cost):
        dn = [*got["dn"], *[turn(piece) for piece in got["dn_far"]]]
        results = attend_back(
            cost,
            bucket_count,
            first_side,
            starts,
            task_groups,
            own_row,
            gain_ffn,
            w_out,
            buckets,
            dn,
            unit,
            spread,
            joined,
            ctx,
            linv,
            exps,
            q,
            v,
            k_turned,
            normed,
            weights,
            tok_all,
        )
        got["dh"], small, send, keep, got["in_low"], in_high = turn.done(results)
        got["two"] = DpSum(turn, send, keep, finish_heads, small)
        got["in_came"] = swap_tensor(in_high, bits[-1])

    def swap_in(cost):
        own, other = turn.done(add_pieces(got["in_low"], turn(got["in_came"]), half, cost))
        got["in_own"], got["in_came"] = own, swap_tensor(other, low_bits[0])

    def end_tokens(cost):
        args = (gain_attn, own_tok, got["in_own"], turn(got["in_came"]), got["dh"], cost)
        got["tokens"] = turn.done(finish_tokens(*args))[None]

    def out_part(cost):
        parts = turn.done(feed_out(turn(active), w_back, count, cost))
        got["out_low"] = parts[:half]
        got["out_came"] = [swap_tensor(part, bits[-1]) for part in parts[half:]]

    def swap_out(cost):
        pairs = zip(got["out_low"], got["out_came"], strict=True)
        got["out_own"], got["out_other"] = [turn.done(add(own, turn(came), cost)) for own, came in pairs]

    def go_mixed(cost):
        got["out_came"] = swap_tensor(turn(got["out_other"]), low_bits[0])

    def end_mixed(cost):
        got["mixed"] = turn.done(finish_mixed(hidden, got["out_own"], turn(got["out_came"]), cost))[None]

    def start_gains():
        while got["two"].at < len(got["two"].pairs):
            got["two"].step()
        got["gains"] = got["two"].small[SMALL // 2 :]
        got["gains_came"] = swap_tensor(got["gains"], bits[-1])

    def gains_a(cost):
        got["gains"] = turn.done(add(got["gains"], turn(got["gains_came"]), cost))
        got["gains_came"] = swap_tensor(got["gains"], low_bits[0])

    def gains_b(cost):
        got["gains"] = turn.done(add(got["gains"], turn(got["gains_came"]), cost))

    stages = dict(
        swap_dn=swap_dn,
        sum_dn=sum_dn,
        back=back,
        swap_in=swap_in,
        end_tokens=end_tokens,
        out_part=out_part,
        swap_out=swap_out,
        go_mixed=go_mixed,
        end_mixed=end_mixed,
        gains_a=gains_a,
        gains_b=gains_b,
        end_heads=lambda cost: got["two"].rest(),
        end_feed=lambda cost: sum_feed.rest(),
    )
    for name in ORDER:
        cost = cost_of(name)
        if name in stages:
            stages[name](cost)
        elif name.startswith("feed"):
            sum_feed.step(cost)
        else:
            got["two"].step(cost)
            if name == "two3":
                start_gains()
    grad_query, grad_key, grad_value, grad_out = got["two"].result
    grad_back, grad_in = sum_feed.result
    return (
        got["mixed"],
        got["tokens"],
        got["gains"][0],
        grad_query.T,
        grad_key.T,
        grad_value.T,
        got["two"].small[:heads, :bucket_count].T,
        grad_out,
        got["gains"][4],
        grad_in,
        grad_back,
    )


def solution(mesh):
    return jax.shard_map(
        shards,
        mesh=mesh,
        in_specs=(
            P("dp", "tensor", None),
            P("dp"),
            P("dp", "tensor"),
            P(),
            P(),
            P(),
            P(None, "tensor"),
            P(None, "tensor"),
            P(None, "tensor"),
            P(None, "tensor"),
            P("tensor", None),
            P(),
            P(None, "tensor"),
            P("tensor", None),
            P("dp", "tensor", None),
        ),
        out_specs=(
            P("dp", "tensor", None),
            P("dp", "tensor", None),
            P(),
            P(None, "tensor"),
            P(None, "tensor"),
            P(None, "tensor"),
            P(None, "tensor"),
            P("tensor", None),
            P(),
            P(None, "tensor"),
            P("tensor", None),
        ),
        check_vma=False,
    )
```

```python
import functools

import jax
import jax.numpy as jnp
from jax import lax
from jax.experimental import pallas as pl
from jax.experimental.pallas import tpu as pltpu
from jax.sharding import PartitionSpec as P

NORM_EPS = 1e-06
MASK_FILL = -1000000000.0
F32 = jnp.float32
BF16 = jnp.bfloat16
LANES = 128
FREE = jax.ShapeDtypeStruct
FAR = pltpu.HBM
HEAVY = pl.CostEstimate(flops=10**11, bytes_accessed=1024, transcendentals=0)
LIGHT = pl.CostEstimate(flops=1024, bytes_accessed=1024, transcendentals=0)
ORDER = (
    "swap_dn", "out_part", "feed1", "swap_out", "sum_dn", "feed2",
    "back", "feed3", "swap_in", "two1", "feed4", "two2",
    "go_mixed", "feed5", "two3", "end_tokens", "gains_a", "end_mixed",
    "two4", "gains_b", "two5", "end_feed", "end_heads",
)
LONG = (
    "feed", "end_tokens", "feed3", "feed4", "two2",
)


def cost_of(name):
    return HEAVY if name in LONG else LIGHT
GELU_SCALE = 0.7978845608028654
GELU_CUBE = 0.044715


def dot_nn(left, right):
    return jnp.dot(left, right, preferred_element_type=F32)


def dot_nt(left, right):
    return lax.dot_general(left, right, (((1,), (1,)), ((), ())), preferred_element_type=F32)


def dot_tn(left, right):
    return lax.dot_general(left, right, (((0,), (0,)), ((), ())), preferred_element_type=F32)


def vmem_whole(shape):
    return pl.BlockSpec(shape, lambda i: (0,) * len(shape))


class Came:
    def __init__(self, array):
        self.array = array


def local_call(kernel, *, out_shape, grid, in_specs, out_specs, scratch_shapes=(), prefetch=0, mib, name, cost=LIGHT):
    def place(value, spec):
        if isinstance(value, Came):
            return value.array
        if value.ndim < 2 or spec.memory_space is pltpu.SMEM:
            return value
        return pltpu.with_memory_space_constraint(value, pltpu.HBM)

    def run(*args):
        given = [place(value, spec) for value, spec in zip(args[prefetch:], in_specs, strict=True)]
        return call(*args[:prefetch], *given)

    call = pl.pallas_call(
        kernel,
        grid_spec=pltpu.PrefetchScalarGridSpec(
            num_scalar_prefetch=prefetch,
            grid=grid,
            in_specs=in_specs,
            out_specs=out_specs,
            scratch_shapes=scratch_shapes,
        ),
        out_shape=out_shape,
        compiler_params=pltpu.CompilerParams(vmem_limit_bytes=mib << 20),
        cost_estimate=cost,
        name=name,
    )
    return run


class Turn:
    def __init__(self):
        self.last = None

    def __call__(self, value):
        if self.last is None:
            return value
        return lax.optimization_barrier((value, self.last))[0]

    def done(self, value):
        self.last = value[0] if isinstance(value, (list, tuple)) else value
        return value


def block_order(count):
    order = [0]
    bit = count // 2
    while bit:
        order = order + [slot | bit for slot in order]
        bit //= 2
    return order


def tensor_bits(count):
    bits = []
    bit = count // 2
    while bit:
        bits.append(bit)
        bit //= 2
    return bits


def swap_tensor(value, bit):
    size = lax.axis_size("tensor")
    return lax.ppermute(value, "tensor", [(i, i ^ bit) for i in range(size)])


def gather_tensor(value, count, ready=()):
    slots = [value]
    for bit in tensor_bits(count):
        came = [swap_tensor(piece, bit) for piece in slots]
        if ready:
            came, ready = lax.optimization_barrier((came, ready))
        slots = slots + came
    return slots, ready


def scatter_tensor(value, count, bits=None):
    for bit in reversed(tensor_bits(count) if bits is None else bits):
        half = value.shape[0] // 2
        came = swap_tensor(value[half:], bit)
        value = (value[:half].astype(F32) + came.astype(F32)).astype(BF16)
    return value


def dp_steps(count):
    bits = []
    bit = 1
    while bit < count:
        bits.append(bit)
        bit *= 2
    return list(zip(bits, bits[1::-1] + bits[2:], strict=True))


def swap_dp(value, pair):
    rows, cols = lax.axis_size("dp"), lax.axis_size("tensor")
    route = []
    for row in range(rows):
        for col in range(cols):
            route.append((row * cols + col, (row ^ pair[col % 2]) * cols + col))
    return lax.ppermute(value, ("dp", "tensor"), route)


def side_of(pair):
    row, col = lax.axis_index("dp"), lax.axis_index("tensor")
    bit = jnp.where(col % 2 == 1, pair[1], pair[0])
    return ((row & bit) != 0).astype(jnp.int32)[None]


def add_kernel(left_ref, right_ref, out_ref):
    total = left_ref[...].astype(F32) + right_ref[...].astype(F32)
    out_ref[...] = total.astype(out_ref.dtype)


def add(left, right, cost=LIGHT):
    return local_call(
        add_kernel,
        grid=(1,),
        in_specs=[vmem_whole(left.shape)] * 2,
        out_specs=vmem_whole(left.shape),
        out_shape=FAR(left.shape, left.dtype),
        mib=8,
        name="add",
        cost=cost,
    )(left, Came(right))


def add_pieces_kernel(count, *refs):
    step = pl.program_id(0)
    for k in range(count):

        @pl.when(step == k)
        def _():
            total = refs[0][...].astype(F32) + refs[1][...].astype(F32)
            refs[2 + k][...] = total.astype(BF16)


def add_pieces(left, right, count, cost=LIGHT):
    rows, cols = left.shape
    part = pl.BlockSpec((rows // count, cols), lambda i: (i, 0))
    return local_call(
        functools.partial(add_pieces_kernel, count),
        grid=(count,),
        in_specs=[part, part],
        out_specs=[vmem_whole((rows // count, cols))] * count,
        out_shape=[FAR((rows // count, cols), BF16)] * count,
        mib=10,
        name="add_pieces",
        cost=cost,
    )(left, Came(right))


def add_swap_kernel(left_ref, right_ref, plain_ref, swapped_ref):
    total = (left_ref[...].astype(F32) + right_ref[...].astype(F32)).astype(BF16)
    plain_ref[...] = total
    swapped_ref[...] = total


def add_swap(left, right, count, flip, cost=LIGHT):
    rows, cols = left.shape
    part = pl.BlockSpec((rows // count, cols), lambda i: (i, 0))
    return local_call(
        add_swap_kernel,
        grid=(count,),
        in_specs=[part, part],
        out_specs=[part, pl.BlockSpec((rows // count, cols), lambda i: (i ^ flip, 0))],
        out_shape=[FAR((rows, cols), BF16), FREE((rows, cols), BF16)],
        mib=10,
        name="add_swap",
        cost=cost,
    )(left, Came(right))


def fold_kernel(side_ref, kept_ref, came_ref, send_ref, keep_ref):
    total = (kept_ref[...].astype(F32) + came_ref[...].astype(F32)).astype(BF16)

    @pl.when(pl.program_id(0) == 0)
    def _():
        send_ref[...] = total

    @pl.when(pl.program_id(0) == 1)
    def _():
        keep_ref[...] = total


def fold(side, kept, came, cost=LIGHT):
    rows, cols = kept.shape
    half = rows // 2
    if half % 16:
        total = (kept.astype(F32) + came.astype(F32)).astype(BF16)
        return [lax.dynamic_slice_in_dim(total, k * half, half) for k in (1 - side[0], side[0])]
    place = pl.BlockSpec((half, cols), lambda i, side: (jnp.where(i == 0, 1 - side[0], side[0]), 0))
    whole = pl.BlockSpec((half, cols), lambda i, side: (0, 0))
    return local_call(
        fold_kernel,
        grid=(2,),
        in_specs=[place, place],
        out_specs=[whole, whole],
        out_shape=[FREE((half, cols), BF16), FAR((half, cols), BF16)],
        prefetch=1,
        mib=8,
        name="fold",
        cost=cost,
    )(side, kept, Came(came))


def join_kernel(steps, side_ref, own_ref, came_ref, out_ref):
    upper = pl.program_id(0) // steps
    mine = upper == side_ref[0]

    @pl.when(mine)
    def _():
        out_ref[...] = own_ref[...].astype(out_ref.dtype)

    @pl.when(jnp.logical_not(mine))
    def _():
        out_ref[...] = came_ref[...].astype(out_ref.dtype)


def join(side, own, came, cost=LIGHT):
    rows, cols = own.shape
    if rows % 16:
        mine = side[0] != 0
        pair = (jnp.where(mine, came, own), jnp.where(mine, own, came))
        return jnp.concatenate(pair)
    steps = 1
    part = rows // steps
    half = pl.BlockSpec((part, cols), lambda i, side: (i % steps, 0))
    return local_call(
        functools.partial(join_kernel, steps),
        grid=(2 * steps,),
        in_specs=[half, half],
        out_specs=pl.BlockSpec((part, cols), lambda i, side: (i, 0)),
        out_shape=FAR((2 * rows, cols), BF16),
        prefetch=1,
        mib=10,
        name="join",
        cost=cost,
    )(side, own, Came(came))


SMALL = 16


def split_small(value):
    coarse = value.astype(BF16)
    return jnp.concatenate((coarse, (value - coarse.astype(F32)).astype(BF16)), axis=0)


def read_small(rows):
    return rows[:SMALL].astype(F32) + rows[SMALL:].astype(F32)


def fold_small_kernel(side_ref, kept_ref, came_ref, small_came_ref, small_ref, send_ref, keep_ref, small_out_ref):
    total = (kept_ref[...].astype(F32) + came_ref[...].astype(F32)).astype(BF16)
    half = keep_ref.shape[0]

    @pl.when(pl.program_id(0) == 0)
    def _():
        small = split_small(read_small(small_ref) + read_small(small_came_ref))
        send_ref[:half] = total
        send_ref[half:] = small
        small_out_ref[...] = small

    @pl.when(pl.program_id(0) == 1)
    def _():
        keep_ref[...] = total


def fold_small(side, kept, came, small, cost=LIGHT):
    rows, cols = kept.shape
    half = rows // 2
    extra = 2 * SMALL
    if half % extra:
        send, keep = fold(side, kept, came[:rows])
        small = split_small(read_small(small) + read_small(came[rows:]))
        return jnp.concatenate((send, small)), keep, small
    place = pl.BlockSpec((half, cols), lambda i, side: (jnp.where(i == 0, 1 - side[0], side[0]), 0))

    def whole(count):
        return pl.BlockSpec((count, cols), lambda i, side: (0, 0))

    return local_call(
        fold_small_kernel,
        grid=(2,),
        in_specs=[place, place, pl.BlockSpec((extra, cols), lambda i, side: (rows // extra, 0)), whole(extra)],
        out_specs=[whole(half + extra), whole(half), whole(extra)],
        out_shape=[FREE((half + extra, cols), BF16), FAR((half, cols), BF16), FAR((extra, cols), BF16)],
        prefetch=1,
        mib=10,
        name="fold_small",
        cost=cost,
    )(side, kept, Came(came), Came(came), small)


def add_small_kernel(kept_ref, came_ref, small_ref, out_ref, small_out_ref):
    rows = kept_ref.shape[0]
    out_ref[...] = (kept_ref[...].astype(F32) + came_ref[:rows].astype(F32)).astype(BF16)
    small_out_ref[...] = read_small(small_ref) + read_small(came_ref[rows:])


def add_small(kept, came, small, cost=LIGHT):
    rows, cols = kept.shape
    if rows % (2 * SMALL):
        return add(kept, came[:rows]), read_small(small) + read_small(came[rows:])
    return local_call(
        add_small_kernel,
        grid=(1,),
        in_specs=[vmem_whole(kept.shape), vmem_whole(came.shape), vmem_whole(small.shape)],
        out_specs=[vmem_whole(kept.shape), vmem_whole((SMALL, cols))],
        out_shape=[FAR(kept.shape, BF16), FAR((SMALL, cols), F32)],
        mib=8,
        name="add_small",
        cost=cost,
    )(kept, Came(came), small)


class DpSum:
    def __init__(self, turn, send, keep, finish, small=None):
        self.turn, self.finish, self.small = turn, finish, small
        self.pairs = dp_steps(lax.axis_size("dp"))
        self.at = 0
        self.keep = keep
        self.came = swap_dp(send, self.pairs[0])

    def step(self, cost=LIGHT):
        turn, last = self.turn, len(self.pairs) - 1
        came = turn(self.came)
        if self.at < last:
            after = self.pairs[self.at + 1]
            if self.small is None:
                send, self.keep = turn.done(fold(side_of(after), self.keep, came, cost))
            else:
                results = turn.done(fold_small(side_of(after), self.keep, came, self.small, cost))
                send, self.keep, self.small = results
            self.came = swap_dp(send, after)
        elif self.at == last:
            if self.small is None:
                self.keep = turn.done(add(self.keep, came, cost))
            else:
                self.keep, self.small = turn.done(add_small(self.keep, came, self.small, cost))
            self.came = swap_dp(self.keep, self.pairs[last])
        else:
            place = 2 * last + 1 - self.at
            side = side_of(self.pairs[place])
            if place == 0:
                self.result = turn.done(self.finish(side, self.keep, came))
            else:
                self.keep = turn.done(join(side, self.keep, came, cost))
                self.came = swap_dp(self.keep, self.pairs[place - 1])
        self.at += 1

    def rest(self):
        while self.at < 2 * len(self.pairs):
            self.step()
        return self.result


def finish_feed_kernel(side_ref, own_ref, came_ref, back_ref, in_ref):
    step = pl.program_id(0)
    many = back_ref.shape[0]

    def put(source):
        back_ref[...] = source[:many].astype(F32)
        in_ref[...] = source[many:].astype(F32)

    @pl.when(step == side_ref[0])
    def _():
        put(own_ref)

    @pl.when(step != side_ref[0])
    def _():
        put(came_ref)


def finish_feed(side, own, came):
    rows, cols = own.shape
    whole = pl.BlockSpec((rows, cols), lambda i, side: (0, 0))
    return local_call(
        finish_feed_kernel,
        grid=(2,),
        in_specs=[whole, whole],
        out_specs=[pl.BlockSpec((rows // 2, cols), lambda i, side: (i, 0))] * 2,
        out_shape=[FREE((rows, cols), F32)] * 2,
        prefetch=1,
        mib=20,
        name="finish_feed",
    )(side, own, Came(came))


def finish_heads_kernel(side_ref, own_ref, came_ref, q_ref, k_ref, v_ref, out_ref):
    step = pl.program_id(0)
    cols = q_ref.shape[0]
    for half, refs in enumerate(((q_ref, k_ref), (v_ref, out_ref))):
        for source, is_own in ((own_ref, True), (came_ref, False)):

            @pl.when((step == half) & ((side_ref[0] == half) == is_own))
            def _():
                refs[0][...] = source[:cols].astype(F32)
                refs[1][...] = source[cols:].astype(F32)


def finish_heads(side, own, came):
    rows, cols = own.shape
    each = rows // 2
    whole = pl.BlockSpec((rows, cols), lambda i, side: (0, 0))
    return local_call(
        finish_heads_kernel,
        grid=(2,),
        in_specs=[whole, whole],
        out_specs=[pl.BlockSpec((each, cols), lambda i, side: (0, 0))] * 4,
        out_shape=[FREE((each, cols), F32)] * 4,
        prefetch=1,
        mib=12,
        name="finish_heads",
    )(side, own, Came(came))


def group_scale(groups_ref, own_ref):
    own = groups_ref[own_ref[0]]
    alike = jnp.int32(0)
    for row in range(groups_ref.shape[0]):
        alike += (groups_ref[row] == own).astype(jnp.int32)
    return lax.rsqrt(jnp.full((1, LANES), alike.astype(F32)))[:, 0:1]


def row_of(ref):
    return ref[...].reshape(1, ref.shape[0])


def norm_rows(values):
    return lax.rsqrt(jnp.mean(values * values, axis=-1, keepdims=True) + NORM_EPS)


def norm_back(dnormed, unit, spread, gain):
    scaled = gain * dnormed
    inner = jnp.mean(scaled * unit, axis=-1, keepdims=True)
    return spread * (scaled - unit * inner), dnormed * unit


def bias_lanes(seq, first_row, first_col):
    start = seq - LANES - first_row + first_col
    return pl.multiple_of(start, LANES)


def bias_kernel(table_ref, buckets_ref, bias_ref):
    which = buckets_ref[...]
    heads, _, wide = bias_ref.shape
    for h in range(heads):
        rel = jnp.zeros((8, wide), F32)
        for b in range(table_ref.shape[0]):
            rel = jnp.where(which == b, table_ref[b, h], rel)
        full = jnp.broadcast_to(rel[0:1], (LANES, wide))
        bias_ref[h] = pltpu.roll(full, wide - (LANES - 1), 1, stride=1, stride_axis=0)


def bias_tiles(table, buckets):
    shape = (table.shape[1], LANES, buckets.shape[1])
    return local_call(
        bias_kernel,
        grid=(1,),
        in_specs=[pl.BlockSpec(memory_space=pltpu.SMEM), vmem_whole(buckets.shape)],
        out_specs=vmem_whole(shape),
        out_shape=FAR(shape, F32),
        mib=16,
        name="bias_tiles",
        cost=HEAVY,
    )(table, buckets)


def attend_kernel(heads, count, length_ref, starts_ref, gain_ref, wq_ref, wk_ref, wv_ref, *refs):
    tok_refs, bias_far, refs = refs[:count], refs[count], refs[count + 1 :]
    (ctx_ref, packed_ref, exps_ref, linv_ref, normed_ref, tok_all_ref) = refs[:6]
    (q_ref, v_ref, k_turned_ref, k_ref, v_turned_ref, bias_ref, all_normed, scores_ref, sem) = refs[6:]
    step = pl.program_id(0)
    blk = ctx_ref.shape[0]
    seq = blk * count
    head_cols = wq_ref.shape[0]
    width = head_cols // heads

    @pl.when(step == 0)
    def _():
        bias_copy = pltpu.make_async_copy(bias_far, bias_ref, sem)
        bias_copy.start()
        lane = lax.broadcasted_iota(jnp.int32, (blk, LANES - width), 1)
        row = lax.broadcasted_iota(jnp.int32, (blk, LANES - width), 0)
        line = lax.broadcasted_iota(jnp.int32, (LANES - width, blk), 0)
        place = lax.broadcasted_iota(jnp.int32, (LANES - width, blk), 1)
        ones_q = jnp.where(lane == 0, 1.0, 0.0)
        ones_v = jnp.where(lane < 2, 1.0, 0.0)
        ones_turned = jnp.where(line < 2, 1.0, 0.0)
        for b in range(count):
            values = tok_refs[b][...].astype(F32)
            normed = (values * norm_rows(values) * row_of(gain_ref)).astype(BF16)
            rows = slice(b * blk, (b + 1) * blk)
            all_normed[rows] = normed
            used = length_ref[0] - starts_ref[b]
            fill = jnp.where((lane == 0) & (row >= used), MASK_FILL, 0.0)
            fill_turned = jnp.where((line == 0) & (place >= used), MASK_FILL, 0.0)
            query = dot_nt(normed, wq_ref[...])
            keys = dot_nt(normed, wk_ref[...])
            values = dot_nt(normed, wv_ref[...])
            keys_turned = dot_nt(wk_ref[...], normed)
            values_turned = dot_nt(wv_ref[...], normed)
            for h in range(heads):
                cols = slice(h * width, (h + 1) * width)
                q_ref[h, rows] = jnp.concatenate((query[:, cols], ones_q), axis=1).astype(BF16)
                k_ref[h, rows] = jnp.concatenate((keys[:, cols], fill), axis=1).astype(BF16)
                v_ref[h, rows] = jnp.concatenate((values[:, cols], ones_v), axis=1).astype(BF16)
                k_turned_ref[h, :, rows] = jnp.concatenate((keys_turned[cols], fill_turned), axis=0).astype(BF16)
                v_turned_ref[h, :, rows] = jnp.concatenate((values_turned[cols], ones_turned), axis=0).astype(BF16)
        bias_copy.wait()

    row0 = pl.multiple_of(step * blk, blk)
    first_query = starts_ref[step]
    normed_ref[...] = all_normed[pl.ds(row0, blk)]
    for b in range(count):

        @pl.when(step == b)
        def _():
            tok_all_ref[...] = tok_refs[b][...]

    outs = []
    linv = jnp.zeros((blk, LANES), F32)
    stat_lane = lax.broadcasted_iota(jnp.int32, (blk, LANES), 1)
    for h in range(heads):
        query = q_ref[h, pl.ds(row0, blk)]
        top = jnp.full((8, blk), -3.0e38, F32)
        for b in range(count):
            for a in range(blk // LANES):
                rows = slice(b * blk + a * LANES, b * blk + (a + 1) * LANES)
                start = bias_lanes(seq, starts_ref[b] + a * LANES, first_query)
                scores = dot_nt(k_ref[h, rows], query) + bias_ref[h, :, pl.ds(start, blk)]
                scores_ref[rows] = scores
                top = jnp.maximum(top, jnp.max(scores.reshape(LANES // 8, 8, blk), axis=0))
        top = jnp.max(top, axis=0, keepdims=True)
        for c in range(seq // LANES):
            rows = slice(c * LANES, (c + 1) * LANES)
            exps_ref[h, rows] = jnp.exp(scores_ref[rows] - top).astype(BF16)
        mixed = dot_nn(v_turned_ref[h], exps_ref[h]).T
        inverse = 1.0 / mixed[:, width : width + 1]
        outs.append(mixed[:, :width] * inverse)
        linv = jnp.where(stat_lane == h, inverse, linv)
    ctx = jnp.concatenate(outs, axis=1).astype(BF16)
    ctx_ref[...] = ctx
    linv_ref[...] = linv
    packed_ref[pl.ds(row0, blk)] = ctx[:, :LANES]
    rest = head_cols - LANES
    for k in range(count):

        @pl.when(step == k)
        def _():
            place = seq + (k % (count // 2)) * blk
            lanes = (k // (count // 2)) * rest
            packed_ref[place : place + blk, lanes : lanes + rest] = ctx[:, LANES:]


def attend(length, starts, bias, gain, w_query, w_key, w_value, tok):
    count = len(tok)
    blk, model = tok[0].shape
    seq = blk * count
    heads = bias.shape[0]
    head_cols = w_query.shape[0]
    smem = pl.BlockSpec(memory_space=pltpu.SMEM)
    assert 2 * (head_cols - LANES) == LANES
    return local_call(
        functools.partial(attend_kernel, heads, count),
        grid=(count,),
        in_specs=[smem, smem, vmem_whole((model,))]
        + [vmem_whole((head_cols, model))] * 3
        + [vmem_whole((blk, model))] * count
        + [pl.BlockSpec(memory_space=pl.ANY)],
        out_specs=[
            pl.BlockSpec((blk, head_cols), lambda i: (i, 0)),
            vmem_whole((seq * 3 // 2, LANES)),
            pl.BlockSpec((heads, seq, blk), lambda i: (0, 0, i)),
            pl.BlockSpec((blk, LANES), lambda i: (i, 0)),
            pl.BlockSpec((blk, model), lambda i: (i, 0)),
            pl.BlockSpec((blk, model), lambda i: (i, 0)),
            vmem_whole((heads, seq, LANES)),
            vmem_whole((heads, seq, LANES)),
            vmem_whole((heads, LANES, seq)),
        ],
        out_shape=[
            FAR((seq, head_cols), BF16),
            FAR((seq * 3 // 2, LANES), BF16),
            FAR((heads, seq, seq), BF16),
            FAR((seq, LANES), F32),
            FAR((seq, model), BF16),
            FAR((seq, model), BF16),
            FAR((heads, seq, LANES), BF16),
            FAR((heads, seq, LANES), BF16),
            FAR((heads, LANES, seq), BF16),
        ],
        scratch_shapes=[
            pltpu.VMEM((heads, seq, LANES), BF16),
            pltpu.VMEM((heads, LANES, seq), BF16),
            pltpu.VMEM((heads, LANES, 2 * seq), F32),
            pltpu.VMEM((seq, model), BF16),
            pltpu.VMEM((seq, blk), F32),
            pltpu.SemaphoreType.DMA,
        ],
        mib=28,
        name="attend",
        cost=HEAVY,
    )(length, starts, gain, w_query, w_key, w_value, *[Came(piece) for piece in tok], bias)


def feed_kernel(count, side_ref, groups_ref, own_ref, gain_ref, *refs):
    tok_far, ctx_far, refs = refs[0], refs[1 : 1 + count], refs[1 + count :]
    w_in_far, w_back_far, joined_far, refs = refs[0], refs[1], refs[2 : 2 + count], refs[2 + count :]
    hidden_ref, unit_ref, spread_ref, active_ref, dn_low_ref, dn_high_ref, send_far, keep_far = refs[:8]
    tok_all, ctx_all, w_in_ref, w_back_ref, w_out_ref, grad_all, normed_now, dup_all, active_turned = refs[8:17]
    normed_turned, hidden_now, halves, sems, out_sems = refs[17:]
    step = pl.program_id(0)
    blk = hidden_ref.shape[0]
    half = count // 2
    span = blk * half
    units, model = w_back_ref.shape
    rest = LANES // 2
    many, fewer = units // 2, model // 2
    used = 0

    def copy(far, near):
        nonlocal used
        used += 1
        return pltpu.make_async_copy(far, near, sems.at[used - 1])

    row_copies, out_copies, grad_copies = [], [], []
    for b in range(count):
        rows = pl.ds(b * blk, blk)
        found = [copy(tok_far.at[rows], tok_all.at[rows])]
        for k in range(count):
            c = b ^ k
            lanes = 2 * k * LANES
            found.append(copy(ctx_far[k].at[pl.ds(c * blk, blk)], ctx_all.at[rows, pl.ds(lanes, LANES)]))
            place = pl.ds(count * blk + (c % half) * blk, blk)
            found.append(copy(ctx_far[k].at[place], ctx_all.at[rows, pl.ds(lanes + LANES, LANES)]))
        row_copies.append(found)
        grad_copies.append(copy(joined_far[b].at[pl.ds(0, blk)], grad_all.at[rows]))
    for k in range(count):
        for part in range(2):
            top = 2 * k * LANES
            out_copies.append(copy(joined_far[k].at[pl.ds(blk, LANES)], w_out_ref.at[part, pl.ds(top, LANES)]))
            place = w_out_ref.at[part, pl.ds(top + LANES + (part ^ (k // half)) * rest, rest)]
            out_copies.append(copy(joined_far[k].at[pl.ds(blk + LANES, rest)], place))
    in_copy = copy(w_in_far, w_in_ref)
    back_copy = copy(w_back_far, w_back_ref)

    @pl.when(step == 0)
    def _():
        early = [one for b in range(half) for one in row_copies[b]]
        late = [one for b in range(half, count) for one in row_copies[b]]
        for one in [*out_copies, *early, in_copy, *grad_copies[:half], back_copy, *late, *grad_copies[half:]]:
            one.start()
        for part in range(2):
            for k in range(count):
                other = 2 * k * LANES + LANES + (1 - (part ^ (k // half))) * rest
                w_out_ref[part, other : other + rest] = jnp.zeros((rest, model), BF16)
        for one in out_copies:
            one.wait()

    for part in range(2):

        @pl.when(step == part)
        def _():
            for b in range(part * half, (part + 1) * half):
                for one in row_copies[b]:
                    one.wait()

    rows = pl.ds(pl.multiple_of(step * span, span), span)
    for b in range(half):
        there = pl.ds(pl.multiple_of(step * span + b * blk, blk), blk)
        hidden_now[b * blk : (b + 1) * blk] = tok_all[there].astype(F32) + dot_nn(ctx_all[there], w_out_ref[step])
    strip = 32 if blk % 32 == 0 else blk
    for r in range(0, span, strip):
        some = slice(r, r + strip)
        hidden = hidden_now[some]
        spread = norm_rows(hidden)
        unit = hidden * spread
        unit_ref[some] = unit.astype(BF16)
        spread_ref[some] = jnp.broadcast_to(spread, (strip, LANES))
        normed_now[some] = (unit * row_of(gain_ref)).astype(BF16)
    normed = normed_now[...]
    normed_turned[:, rows] = normed.T

    @pl.when(step == 0)
    def _():
        hidden_ref[...] = hidden_now[0:blk]
        in_copy.wait()
        back_copy.wait()

    for part in range(2):

        @pl.when(step == part)
        def _():
            for b in range(part * half, (part + 1) * half):
                grad_copies[b].wait()

    grad = grad_all[rows]
    scale = group_scale(groups_ref, own_ref)
    part = 256 if units % 256 == 0 else units
    for b in range(0, span, 256):
        near = slice(b, b + 256)
        there = pl.ds(pl.multiple_of(step * span + b, 256), 256)
        for c in range(0, units, part):
            cols = slice(c, c + part)
            up = dot_nn(normed[near], w_in_ref[:, cols])
            dactive = dot_nt(grad[near], w_back_ref[cols])
            square = up * up
            bend = jnp.tanh(up * (GELU_SCALE + GELU_SCALE * GELU_CUBE * square))
            bell = 0.5 + 0.5 * bend
            active = (up * bell).astype(BF16)
            steep = GELU_SCALE + 3.0 * GELU_SCALE * GELU_CUBE * square
            slope = (bell + (0.5 * up) * (1.0 - bend * bend) * steep) * scale
            active_ref[near, cols] = active
            active_turned[cols, there] = active.T
            dup_all[there, cols] = (dactive * slope).astype(BF16)

    def put(dn_ref):
        for b in range(0, span, 256):
            near = slice(b, b + 256)
            there = pl.ds(pl.multiple_of(step * span + b, 256), 256)
            dn_ref[near] = dot_nt(dup_all[there], w_in_ref[...]).astype(BF16)

    @pl.when(step == 0)
    def _():
        put(dn_low_ref)

    @pl.when(step == 1)
    def _():
        put(dn_high_ref)
        going = []
        for k, (far, side) in enumerate(((send_far, 1 - side_ref[0]), (keep_far, side_ref[0]))):
            back = dot_nn(active_turned[pl.ds(side * many, many)], grad_all[...]) * scale
            halves[k, :many] = back.astype(BF16)
            halves[k, many:] = dot_nn(normed_turned[pl.ds(side * fewer, fewer)], dup_all[...]).astype(BF16)
            going.append(pltpu.make_async_copy(halves.at[k], far, out_sems.at[k]))
            going[-1].start()
        for one in going:
            one.wait()


def feed(side, groups, own, gain, w_in, w_back, tok, ctx, joined):
    count = len(ctx)
    rows, model = tok.shape
    blk = rows // count
    units = w_in.shape[1]
    span = rows // 2
    by_row = pl.BlockSpec((span, model), lambda i, side: (i, 0))
    anywhere = pl.BlockSpec(memory_space=pl.ANY)
    smem = pl.BlockSpec(memory_space=pltpu.SMEM)

    def whole(shape):
        return pl.BlockSpec(shape, lambda i, side: (0, 0))

    grads = ((units + model) // 2, model)
    copies = count * (4 + 2 * count) + 2 + 2 * count
    return local_call(
        functools.partial(feed_kernel, count),
        grid=(2,),
        in_specs=[smem, smem, pl.BlockSpec((model,), lambda i, side: (0,))] + [anywhere] * (3 + 2 * count),
        out_specs=[
            whole((blk, model)),
            by_row,
            pl.BlockSpec((span, LANES), lambda i, side: (i, 0)),
            pl.BlockSpec((span, units), lambda i, side: (i, 0)),
            *[whole((span, model))] * 2,
            anywhere,
            anywhere,
        ],
        out_shape=[FAR((blk, model), F32), FAR((rows, model), BF16), FAR((rows, LANES), F32), FAR((rows, units), BF16)]
        + [FAR((span, model), BF16)] * 2
        + [FAR(grads, BF16)] * 2,
        scratch_shapes=[
            pltpu.VMEM((rows, model), BF16),
            pltpu.VMEM((rows, 2 * count * LANES), BF16),
            pltpu.VMEM((model, units), BF16),
            pltpu.VMEM((units, model), BF16),
            pltpu.VMEM((2, 2 * count * LANES, model), BF16),
            pltpu.VMEM((rows, model), BF16),
            pltpu.VMEM((span, model), BF16),
            pltpu.VMEM((rows, units), BF16),
            pltpu.VMEM((units, rows), BF16),
            pltpu.VMEM((model, rows), BF16),
            pltpu.VMEM((span, model), F32),
            pltpu.VMEM((2, *grads), BF16),
            pltpu.SemaphoreType.DMA((copies,)),
            pltpu.SemaphoreType.DMA((2,)),
        ],
        prefetch=1,
        mib=52,
        name="feed",
        cost=cost_of("feed"),
    )(side, groups, own, gain, tok, ctx[0], *[Came(a) for a in ctx[1:]], w_in, w_back, *joined)


def feed_out_kernel(active_ref, w_back_ref, *out_refs):
    for k, ref in enumerate(out_refs):

        @pl.when(pl.program_id(0) == k)
        def _():
            ref[...] = dot_nn(active_ref[...], w_back_ref[...]).astype(BF16)


def feed_out(active, w_back, count, cost):
    rows, units = active.shape
    model = w_back.shape[1]
    blk = rows // count
    return local_call(
        feed_out_kernel,
        grid=(count,),
        in_specs=[pl.BlockSpec((blk, units), lambda i: (i, 0)), vmem_whole(w_back.shape)],
        out_specs=[vmem_whole((blk, model))] * count,
        out_shape=[FAR((blk, model), BF16)] * count,
        mib=16,
        name="feed_out",
        cost=cost,
    )(active, w_back)


def finish_mixed_kernel(hidden_ref, own_ref, came_ref, out_ref):
    total = own_ref[...].astype(F32) + came_ref[...].astype(F32)
    out_ref[...] = (hidden_ref[...] + total).astype(BF16)


def finish_mixed(hidden, own, came, cost=LIGHT):
    blk, model = own.shape
    place = pl.BlockSpec((blk, model), lambda i: (0, 0))
    return local_call(
        finish_mixed_kernel,
        grid=(1,),
        in_specs=[place] * 3,
        out_specs=place,
        out_shape=jax.ShapeDtypeStruct((blk, model), BF16),
        mib=10,
        name="finish_mixed",
        cost=cost,
    )(hidden, own, Came(came))


def finish_tokens_kernel(gain_ref, tok_ref, own_ref, came_ref, dh_ref, out_ref):
    dnormed = own_ref[...].astype(F32) + came_ref[...].astype(F32)
    values = tok_ref[...].astype(F32)
    spread = norm_rows(values)
    out_ref[...] = dh_ref[...].astype(F32) + norm_back(dnormed, values * spread, spread, row_of(gain_ref))[0]


def finish_tokens(gain, tok, own, came, dh_own, cost=LIGHT):
    blk, model = own.shape
    steps = 2 if blk % 32 == 0 else 1
    place = pl.BlockSpec((blk // steps, model), lambda i: (i, 0))
    return local_call(
        finish_tokens_kernel,
        grid=(steps,),
        in_specs=[vmem_whole((model,))] + [place] * 4,
        out_specs=place,
        out_shape=jax.ShapeDtypeStruct((blk, model), F32),
        mib=10,
        name="finish_tokens",
        cost=cost,
    )(gain, tok, own, Came(came), dh_own)


def attend_back_kernel(heads, count, side_ref, starts_ref, groups_ref, own_ref, gain_ref, buckets_ref, *refs):
    dn_far, joined_far, refs = refs[:count], refs[count : 2 * count], refs[2 * count :]
    unit_far, spread_far, ctx_far, linv_far, exps_far, w_out_far, refs = *refs[:6], refs[6:]
    late_far, refs = refs[:8], refs[8:]
    dh_own_far, small_far, send_far, keep_far, in_low_far, in_high_far, refs = *refs[:6], refs[6:]
    dn_all, grad_all, unit_all, spread_all, ctx_all, linv_all, exps_all, w_out_ref, refs = *refs[:8], refs[8:]
    late_near, refs = refs[:8], refs[8:]
    v_ref, q_ref, k_turned_ref, normed_ref, tok_ref, wq_ref, wk_ref, wv_ref = late_near
    dk_ref, dv_ref, acc_ref, ds_ref, given_ref, dh_all, dj_ref, sums_ref, in_all, halves, sems, out_sems = refs
    block = pl.program_id(0)
    seq, model = dh_all.shape
    blk = seq // count
    head_cols = ctx_all.shape[1]
    width = head_cols // heads
    wide = acc_ref.shape[2]
    half_cols = 2 * head_cols
    strip = 32 if blk % 32 == 0 else blk

    def first_copies(b):
        rows = pl.ds(b * blk, blk)
        pairs = [
            (dn_far[b], dn_all.at[rows]),
            (unit_far.at[rows], unit_all.at[rows]),
            (spread_far.at[rows], spread_all.at[rows]),
            (joined_far[b].at[pl.ds(0, blk)], grad_all.at[rows]),
            (ctx_far.at[rows], ctx_all.at[rows]),
            (linv_far.at[rows], linv_all.at[rows]),
        ]
        return [pltpu.make_async_copy(far, near, sems.at[7 * b + k]) for k, (far, near) in enumerate(pairs)]

    def exps_copy(b):
        cols = pl.ds(b * blk, blk)
        return pltpu.make_async_copy(exps_far.at[:, :, cols], exps_all.at[b % 2], sems.at[7 * b + 6])

    out_copy = pltpu.make_async_copy(w_out_far, w_out_ref, sems.at[7 * count])
    late = [pltpu.make_async_copy(late_far[k], late_near[k], sems.at[7 * count + 1 + k]) for k in range(8)]

    @pl.when(block == 0)
    def _():
        for copy in [*first_copies(0), out_copy, late[0], exps_copy(0), late[1], late[2], *first_copies(1)]:
            copy.start()
        dk_ref[...] = jnp.zeros_like(dk_ref)
        dv_ref[...] = jnp.zeros_like(dv_ref)
        acc_ref[...] = jnp.zeros_like(acc_ref)

    for b in range(count):

        @pl.when(block == b)
        def _():
            if b + 1 < count:
                exps_copy(b + 1).start()
            if b == 0:
                for k in range(2, count):
                    for copy in first_copies(k):
                        copy.start()
                for copy in late[3:]:
                    copy.start()
            for copy in first_copies(b):
                copy.wait()
            if b == 0:
                out_copy.wait()
                for copy in late[:3]:
                    copy.wait()
            exps_copy(b).wait()

    row0 = pl.multiple_of(block * blk, blk)
    now = pl.ds(row0, blk)
    scale = group_scale(groups_ref, own_ref)
    for r in range(0, blk, strip):
        there = pl.ds(pl.multiple_of(row0 + r, strip), strip)
        unit = unit_all[there].astype(F32)
        scaled = row_of(gain_ref) * dn_all[there].astype(F32)
        inner = jnp.mean(scaled * unit, axis=-1, keepdims=True)
        dhidden = spread_all[there, 0:1] * (scaled - unit * inner)
        dh_all[there] = (dhidden + grad_all[there].astype(F32) * scale).astype(BF16)

    dctx = dot_nt(dh_all[now], w_out_ref[...])
    product = dctx * ctx_all[now].astype(F32)
    lane = lax.broadcasted_iota(jnp.int32, (blk, LANES - width), 1)
    for h in range(heads):
        cols = slice(h * width, (h + 1) * width)
        inverse = linv_all[now, h : h + 1]
        inner = -jnp.sum(product[:, cols], axis=1, keepdims=True) * inverse
        coarse = inner.astype(BF16).astype(F32)
        extra = jnp.where(lane == 0, coarse, jnp.where(lane == 1, inner - coarse, 0.0))
        given_ref[h] = jnp.concatenate((dctx[:, cols] * inverse, extra), axis=1).astype(BF16)

    slot = lax.rem(block, 2)
    first_query = starts_ref[block]
    dquery = []
    for h in range(heads):
        given = given_ref[h]
        for b in range(count):
            for a in range(blk // LANES):
                rows = slice(b * blk + a * LANES, b * blk + (a + 1) * LANES)
                dscores = exps_all[slot, h, rows].astype(F32) * dot_nt(v_ref[h, rows], given)
                ds_ref[h, rows] = dscores.astype(BF16)
                start = bias_lanes(seq, starts_ref[b] + a * LANES, first_query)
                acc_ref[h, :, pl.ds(start, blk)] += dscores
        dk_ref[h] += dot_nn(ds_ref[h], q_ref[h, now])
        dv_ref[h] += dot_nn(exps_all[slot, h], given)
        dquery.append(dot_nn(k_turned_ref[h], ds_ref[h]).T[:, :width])
    dj_ref[0, now] = jnp.concatenate(dquery, axis=1).astype(BF16)

    @pl.when(block == 0)
    def _():
        total = jnp.zeros((1, model), F32)
        for r in range(0, blk, strip):
            product = unit_all[r : r + strip].astype(F32) * dn_all[r : r + strip].astype(F32)
            total += jnp.sum(product, axis=0, keepdims=True)
        sums_ref[...] = jnp.zeros_like(sums_ref)
        sums_ref[12:16] = jnp.broadcast_to(total, (4, model))
        pltpu.make_async_copy(dh_all.at[pl.ds(0, blk)], dh_own_far, out_sems.at[0]).start()

    @pl.when(block == count - 1)
    def _():
        dj_ref[1] = jnp.concatenate([dk_ref[h][:, :width] for h in range(heads)], axis=1).astype(BF16)
        dj_ref[2] = jnp.concatenate([dv_ref[h][:, :width] for h in range(heads)], axis=1).astype(BF16)
        going = [pltpu.make_async_copy(dh_all.at[pl.ds(0, blk)], dh_own_far, out_sems.at[0])]

        def send_out(near, far):
            going.append(pltpu.make_async_copy(near, far, out_sems.at[len(going)]))
            going[-1].start()

        for copy in late[3:]:
            copy.wait()
        gain_total = jnp.zeros((1, model), F32)
        for b in range(count):
            rows = slice(b * blk, (b + 1) * blk)
            dnormed = dot_nn(dj_ref[0, rows], wq_ref[...])
            dnormed = dnormed + dot_nn(dj_ref[1, rows], wk_ref[...])
            dnormed = dnormed + dot_nn(dj_ref[2, rows], wv_ref[...])
            in_all[rows] = dnormed.astype(BF16)
            for r in range(0, blk, strip):
                values = tok_ref[b * blk + r : b * blk + r + strip].astype(F32)
                product = dnormed[r : r + strip] * (values * norm_rows(values))
                gain_total += jnp.sum(product, axis=0, keepdims=True)
        send_out(in_all.at[pl.ds(0, seq // 2)], in_low_far)
        send_out(in_all.at[pl.ds(seq // 2, seq // 2)], in_high_far)
        sums_ref[8:12] = jnp.broadcast_to(gain_total, (4, model))

        drel = []
        for h in range(heads):
            part = acc_ref[h]
            rows = LANES
            while rows > 1:
                rows //= 2
                part = part[:rows] + pltpu.roll(part[rows:], wide - rows, 1)
            drel.append(pltpu.roll(part, LANES - 1, 1))
        drel = jnp.concatenate(drel + [jnp.zeros((8 - heads, wide), F32)], axis=0)
        bucket = lax.broadcasted_iota(jnp.int32, (LANES, wide), 0)
        onehot = jnp.where(bucket == jnp.broadcast_to(buckets_ref[0:1], (LANES, wide)), 1.0, 0.0).astype(BF16)
        table = jnp.zeros((8, LANES), F32)
        for _ in range(3):
            coarse = drel.astype(BF16)
            table = table + dot_nt(jnp.concatenate((coarse, jnp.zeros_like(coarse)), axis=0), onehot)[:8]
            drel = drel - coarse.astype(F32)
        sums_ref[0:8, 0:LANES] = table
        halves[0, half_cols:] = split_small(sums_ref[...])
        send_out(halves.at[0, pl.ds(half_cols, 2 * SMALL)], small_far)
        side = side_ref[0]
        for k in range(2):

            @pl.when((side == 0) == (k == 1))
            def _():
                halves[k, :head_cols] = dot_tn(dj_ref[0], normed_ref[...]).astype(BF16)
                halves[k, head_cols:half_cols] = dot_tn(dj_ref[1], normed_ref[...]).astype(BF16)

            @pl.when((side == 0) == (k == 0))
            def _():
                halves[k, :head_cols] = dot_tn(dj_ref[2], normed_ref[...]).astype(BF16)
                halves[k, head_cols:half_cols] = dot_tn(ctx_all[...], dh_all[...]).astype(BF16)

            if k == 0:
                send_out(halves.at[0], send_far)
            else:
                send_out(halves.at[1, pl.ds(0, half_cols)], keep_far)
        for copy in going:
            copy.wait()


def attend_back(cost, bucket_count, side, starts, groups, own, gain, w_out, buckets, dn, unit, spread, joined, ctx, linv, exps, q, v, k_turned, normed, weights, tok):
    head_cols, model = w_out.shape
    count = starts.shape[0]
    heads, seq = exps.shape[:2]
    assert bucket_count <= LANES and heads <= 8
    blk = seq // count

    def whole(shape):
        return pl.BlockSpec(shape, lambda i, side: (0,) * len(shape))

    def room(value):
        return pltpu.VMEM(value.shape, value.dtype)

    first = [unit, spread, ctx, linv]
    late = [v, q, k_turned, normed, tok, *weights]
    smem = pl.BlockSpec(memory_space=pltpu.SMEM)
    anywhere = pl.BlockSpec(memory_space=pl.ANY)
    extra = 2 * SMALL
    outs = [(blk, model), (extra, model), (2 * head_cols + extra, model), (2 * head_cols, model), (seq // 2, model), (seq // 2, model)]
    return local_call(
        functools.partial(attend_back_kernel, heads, count),
        grid=(count,),
        in_specs=[smem, smem, smem, whole((model,)), whole((8, 2 * seq))] + [anywhere] * (2 * count + 6 + len(late)),
        out_specs=[anywhere] * len(outs),
        out_shape=[FAR(shape, BF16) for shape in outs],
        scratch_shapes=[pltpu.VMEM((seq, model), BF16), pltpu.VMEM((seq, model), BF16)]
        + [room(a) for a in first]
        + [pltpu.VMEM((2, heads, seq, blk), BF16), room(w_out)]
        + [room(a) for a in late]
        + [
            pltpu.VMEM((heads, seq, LANES), F32),
            pltpu.VMEM((heads, seq, LANES), F32),
            pltpu.VMEM((heads, LANES, 2 * seq), F32),
            pltpu.VMEM((heads, seq, blk), BF16),
            pltpu.VMEM((heads, blk, LANES), BF16),
            pltpu.VMEM((seq, model), BF16),
            pltpu.VMEM((3, seq, head_cols), BF16),
            pltpu.VMEM((SMALL, model), F32),
            pltpu.VMEM((seq, model), BF16),
            pltpu.VMEM((2, 2 * head_cols + extra, model), BF16),
            pltpu.SemaphoreType.DMA((7 * count + 1 + len(late),)),
            pltpu.SemaphoreType.DMA((6,)),
        ],
        prefetch=1,
        mib=52,
        name="attend_back",
        cost=cost,
    )(side, starts, groups, own, gain, buckets, *[Came(a) for a in dn], *joined, *first, exps, w_out, *late)


def shards(
    tokens,
    row_lengths,
    instruction_mask,
    task_groups,
    rel_buckets,
    gain_attn,
    w_query,
    w_key,
    w_value,
    rel_table,
    w_out,
    gain_ffn,
    w_in,
    w_back,
    out_grad,
):
    blk, model = tokens.shape[1:]
    count = lax.axis_size("tensor")
    head_cols = w_query.shape[1]
    bucket_count, heads = rel_table.shape
    width = head_cols // heads
    seq = blk * count
    half = count // 2
    bits = tensor_bits(count)
    here = lax.axis_index("tensor")
    starts = (here ^ jnp.array(block_order(count), jnp.int32)) * blk
    weights = (w_query.T, w_key.T, w_value.T)
    own_row = lax.axis_index("dp")[None]
    turned = jnp.pad(rel_buckets[::-1], (0, 1), constant_values=-1)
    buckets = jnp.broadcast_to(turned[None], (8, 2 * seq))
    first_side = side_of(dp_steps(lax.axis_size("dp"))[0])

    positions = here * blk + jnp.arange(blk, dtype=jnp.int32)
    keep = (positions < row_lengths[0]) & (instruction_mask[0] == 0)
    masked_grad = jnp.where(keep[:, None], out_grad[0], 0).astype(BF16)

    turn = Turn()
    low_bits = bits[:-1]

    def across(pieces):
        while len(pieces) > 1:
            bit = low_bits[len(low_bits) - len(pieces).bit_length() + 1]
            near = len(pieces) // 2
            others = [swap_tensor(piece, bit) for piece in pieces[near:]]
            pieces = list(zip(pieces[:near], others, strict=True))
            if near > 1:
                pieces = [turn.done(add(a, turn(b))) for a, b in pieces]
        return pieces[0]

    own_tok = tokens[0]
    joined = jnp.concatenate((masked_grad, w_out))
    bias = bias_tiles(rel_table, buckets)
    ready = (joined, starts, own_row, bias)
    assert count == 4
    far_tok = swap_tensor(own_tok, 2)
    near_tok = swap_tensor(own_tok, 1)
    far_tok, ready = lax.optimization_barrier((far_tok, ready))
    joined, starts, own_row, bias = ready
    tok = [own_tok, far_tok, near_tok, swap_tensor(far_tok, 1)]
    joined = [joined, swap_tensor(joined, 2)]
    ctx, packed, exps, linv, normed, tok_all, q, v, k_turned = turn.done(
        attend(row_lengths, starts, bias, gain_attn, *weights, tok)
    )
    contexts, _ = gather_tensor(packed, count)
    joined = [turn(piece) for piece in joined]
    joined = joined + [swap_tensor(piece, bits[-1]) for piece in joined]
    hidden, unit, spread, active, dn_low, dn_high, feed_send, feed_keep = turn.done(
        feed(first_side, task_groups, own_row, gain_ffn, w_in, w_back, tok_all, contexts, joined)
    )
    dn_came = swap_tensor(dn_high, bits[-1])
    sum_feed = DpSum(turn, feed_send, feed_keep, finish_feed)
    assert half == 2 and len(low_bits) == 1
    flip = block_order(count).index(low_bits[0])
    got = {}

    def swap_dn(cost):
        got["dn"], sent = turn.done(add_swap(dn_low, turn(dn_came), half, flip, cost))
        got["dn_came"] = swap_tensor(sent, low_bits[0])

    def sum_dn(cost):
        got["dn"] = turn.done(add_pieces(got["dn"], turn(got["dn_came"]), half, cost))
        got["dn_far"] = [swap_tensor(piece, bits[-1]) for piece in got["dn"]]

    def back(cost):
        dn = [*got["dn"], *[turn(piece) for piece in got["dn_far"]]]
        results = attend_back(
            cost,
            bucket_count,
            first_side,
            starts,
            task_groups,
            own_row,
            gain_ffn,
            w_out,
            buckets,
            dn,
            unit,
            spread,
            joined,
            ctx,
            linv,
            exps,
            q,
            v,
            k_turned,
            normed,
            weights,
            tok_all,
        )
        got["dh"], small, send, keep, got["in_low"], in_high = turn.done(results)
        got["two"] = DpSum(turn, send, keep, finish_heads, small)
        got["in_came"] = swap_tensor(in_high, bits[-1])

    def swap_in(cost):
        own, other = turn.done(add_pieces(got["in_low"], turn(got["in_came"]), half, cost))
        got["in_own"], got["in_came"] = own, swap_tensor(other, low_bits[0])

    def end_tokens(cost):
        args = (gain_attn, own_tok, got["in_own"], turn(got["in_came"]), got["dh"], cost)
        got["tokens"] = turn.done(finish_tokens(*args))[None]

    def out_part(cost):
        parts = turn.done(feed_out(turn(active), w_back, count, cost))
        got["out_low"] = parts[:half]
        got["out_came"] = [swap_tensor(part, bits[-1]) for part in parts[half:]]

    def swap_out(cost):
        pairs = zip(got["out_low"], got["out_came"], strict=True)
        got["out_own"], got["out_other"] = [turn.done(add(own, turn(came), cost)) for own, came in pairs]

    def go_mixed(cost):
        got["out_came"] = swap_tensor(turn(got["out_other"]), low_bits[0])

    def end_mixed(cost):
        got["mixed"] = turn.done(finish_mixed(hidden, got["out_own"], turn(got["out_came"]), cost))[None]

    def start_gains():
        while got["two"].at < len(got["two"].pairs):
            got["two"].step()
        got["gains"] = got["two"].small[SMALL // 2 :]
        got["gains_came"] = swap_tensor(got["gains"], bits[-1])

    def gains_a(cost):
        got["gains"] = turn.done(add(got["gains"], turn(got["gains_came"]), cost))
        got["gains_came"] = swap_tensor(got["gains"], low_bits[0])

    def gains_b(cost):
        got["gains"] = turn.done(add(got["gains"], turn(got["gains_came"]), cost))

    stages = dict(
        swap_dn=swap_dn,
        sum_dn=sum_dn,
        back=back,
        swap_in=swap_in,
        end_tokens=end_tokens,
        out_part=out_part,
        swap_out=swap_out,
        go_mixed=go_mixed,
        end_mixed=end_mixed,
        gains_a=gains_a,
        gains_b=gains_b,
        end_heads=lambda cost: got["two"].rest(),
        end_feed=lambda cost: sum_feed.rest(),
    )
    for name in ORDER:
        cost = cost_of(name)
        if name in stages:
            stages[name](cost)
        elif name.startswith("feed"):
            sum_feed.step(cost)
        else:
            got["two"].step(cost)
            if name == "two3":
                start_gains()
    grad_query, grad_key, grad_value, grad_out = got["two"].result
    grad_back, grad_in = sum_feed.result
    return (
        got["mixed"],
        got["tokens"],
        got["gains"][0],
        grad_query.T,
        grad_key.T,
        grad_value.T,
        got["two"].small[:heads, :bucket_count].T,
        grad_out,
        got["gains"][4],
        grad_in,
        grad_back,
    )


def solution(mesh):
    return jax.shard_map(
        shards,
        mesh=mesh,
        in_specs=(
            P("dp", "tensor", None),
            P("dp"),
            P("dp", "tensor"),
            P(),
            P(),
            P(),
            P(None, "tensor"),
            P(None, "tensor"),
            P(None, "tensor"),
            P(None, "tensor"),
            P("tensor", None),
            P(),
            P(None, "tensor"),
            P("tensor", None),
            P("dp", "tensor", None),
        ),
        out_specs=(
            P("dp", "tensor", None),
            P("dp", "tensor", None),
            P(),
            P(None, "tensor"),
            P(None, "tensor"),
            P(None, "tensor"),
            P(None, "tensor"),
            P("tensor", None),
            P(),
            P(None, "tensor"),
            P("tensor", None),
        ),
        check_vma=False,
    )
```
